32 devices in a mesh: rep: 4 (over y, x), ep: 8 (over z, core).
Axes of the slice: x: 2, y: 2, z: 4, core: 2. Of those that a mesh axis runs over, the one named last changes fastest.
Arguments:
- tokens: bfloat16 [4096, 3584], P(('rep', 'ep')), may hold values from -6 to 6
- out_grad: bfloat16 [4096, 3584], P(('rep', 'ep')), may hold values from -3 to 3
- expert_ids: int32 [4096, 8], P(('rep', 'ep')), may hold values from 0 to 127, all different within a row; in each aligned block of 128 rows (0 to 127, 128 to 255, ...) at most 16 rows name the same one
- route_weight: bfloat16 [4096, 8], P(('rep', 'ep')), may hold values from 0.049804688 to 0.59765625
- live_count: int32 [4], replicated, may hold values from 96 to 128
- cap_blocks: int32 [4, 1], replicated, may hold values from 1 to 3
- w_gate: bfloat16 [3584, 1024], P('rep', 'ep'), may hold values from -0.09375 to 0.09375
- w_up: bfloat16 [3584, 1024], P('rep', 'ep'), may hold values from -0.09375 to 0.09375
- w_down_t: bfloat16 [3584, 1024], P('rep', 'ep'), may hold values from -0.1875 to 0.1875
Outputs:
- grad_tokens: bfloat16 [4096, 3584], P(('rep', 'ep'))
- grad_weight: float32 [4096, 8], P(('rep', 'ep'))
- grad_gate: bfloat16 [3584, 1024], P('rep', 'ep')
- grad_up: bfloat16 [3584, 1024], P('rep', 'ep')
- grad_down_t: bfloat16 [3584, 1024], P('rep', 'ep')
The draws below stay inside these ranges and needn't reach their ends.
Inputs may be any that keep to these rules, and one draw needn't show every extreme that they name: `expert_ids`: among the 128 rows of one device, no expert is named by more than 16 rows; each row names 8 different experts.
All inputs are finite; a program needn't handle non-finite values.
Results may differ from the reference program's by a relative error of at most 0.019.
Values may be sent and summed in bfloat16 or wider, within the bound.
No kernel may reach another device: no remote copies, remote signals or barrier semaphores. Data moves between devices by JAX's collectives and lax.ppermute only.
A program may use at most 128 MiB of HBM per device.

```python
import math
import jax
import jax.numpy as jnp
import numpy as np
from jax import lax

D = 3584
F_WIN = 1024
F_DEV = 128
EXPERTS = 128
TOP = 8
TOK_DEV = 128
SLOT = 16
BLOCK = 128
MAX_BLOCKS = 3
SPLIT = 8
FLIGHT = 1
TOKENS = 4096
UNITS = 1024
N_REP = 4
N_EP = 8


def draw_live_count(key, part):
    lowest = TOK_DEV * 3 // 4
    drawn_counts = jax.random.randint(jax.random.fold_in(key, 11), (N_REP,), lowest, TOK_DEV + 1)
    full_group = jax.random.randint(jax.random.fold_in(key, 12), (), 0, N_REP)
    return jnp.where(jnp.arange(N_REP) == full_group, TOK_DEV, drawn_counts).astype(jnp.int32)


def draw_cap_blocks(key, part):
    drawn_blocks = jax.random.randint(jax.random.fold_in(key, 21), (N_REP, FLIGHT), 1, MAX_BLOCKS + 1)
    full_entry = jax.random.randint(jax.random.fold_in(key, 22), (), 0, N_REP * FLIGHT)
    marker = jnp.arange(N_REP * FLIGHT).reshape(N_REP, FLIGHT) == full_entry
    return jnp.where(marker, MAX_BLOCKS, drawn_blocks).astype(jnp.int32)


def with_spikes(values, key, source, target, shards_of, factor):
    def block_of(dim):
        return (jnp.arange(values.shape[dim]) // (values.shape[dim] // shards_of)).reshape((-1,) + (1,) * (values.ndim - 1 - dim))

    near = jax.random.permutation(key, shards_of)[block_of(target)]
    other_side = (block_of(target) + shards_of // 2) % shards_of
    return jnp.where((block_of(source) == near) | (block_of(source) == other_side), factor * values, values)


def block_levels(rng, dims, pieces, low, largest):
    loudness = 1.0
    for dim, blocks in pieces:
        steps = jax.random.uniform(jax.random.fold_in(jax.random.fold_in(rng, 6), dim), (blocks,), jnp.float32, low / len(pieces), largest / len(pieces))
        loudness = loudness * jnp.repeat(jnp.exp(steps), dims[dim] // blocks).reshape((-1,) + (1,) * (len(dims) - 1 - dim))
    return loudness


def routed_block(key, own, number, rows, count, top, reach, lean):
    sequence = jax.random.permutation(key, count)
    packed, common = shares(count, rows * top, reach, lean, True), shares(count, rows * top, reach, lean, False)
    places = jnp.arange(count)

    def named(sizes, turn):
        used = int((sizes > 0).sum())
        fixed = max(1, used // 4)
        shifted = fixed + (places - fixed + turn * (used - fixed)) % max(1, count - fixed)
        return jnp.zeros((count,), jnp.int32).at[sequence[jnp.where(places < fixed, places, shifted)]].set(jnp.asarray(sizes, jnp.int32))

    sizes = jnp.where(number % 4 == 0, named(packed, number // 4), named(common, number - number // 4 - 1))
    mixed = jax.random.permutation(jax.random.fold_in(own, 3), count)
    giver, taker = mixed[0:count // 2 * 2:2], mixed[1:count // 2 * 2:2]
    room = jnp.minimum(sizes[giver] - 1, reach - sizes[taker]) // 2
    room = jnp.where((giver == sequence[0]) | (taker == sequence[0]) | (sizes[taker] == 0), 0, jnp.maximum(room, 0))
    shifted = jax.random.randint(jax.random.fold_in(own, 4), (count // 2,), 0, 1 << 20) % (room + 1)
    sizes = sizes.at[giver].add(-shifted).at[taker].add(shifted)
    items = jnp.searchsorted(jnp.cumsum(sizes), jnp.arange(rows * top), side="right").astype(jnp.int32)
    grid = items.reshape(top, rows).T
    grid = grid[jax.random.permutation(jax.random.fold_in(own, 1), rows)]
    turn = jax.random.randint(jax.random.fold_in(own, 2), (rows, 1), 0, top)
    return jnp.take_along_axis(grid, (jnp.arange(top)[None, :] + turn) % top, axis=1)


def shares(amount, total, reach, skew, full):
    loads = [(1 << 20) // math.isqrt(grade ** skew) + 1 for grade in range(1, amount + 1)]
    largest = reach if full else min(reach, max(-(-total // amount), total * loads[0] // sum(loads)))
    least = 1 if total - largest >= amount - 1 else 0
    counts, spare = [largest] + [least] * (amount - 1), total - largest - least * (amount - 1)
    while spare > 0:
        movable = [i for i in range(1, amount) if counts[i] < largest] or [i for i in range(1, amount) if counts[i] < reach]
        pool, remaining = sum([loads[i] for i in movable]), spare
        for i in movable:
            addition = min(reach - counts[i], max(1, remaining * loads[i] // pool), spare)
            counts[i] = counts[i] + addition
            spare = spare - addition
    return np.array(counts)


def scatter_about(rng, extent, spread, bound, split=(), kind=jnp.bfloat16):
    result = jax.random.normal(rng, extent, jnp.float32) * spread
    if len(split) > 0:
        result = block_levels(rng, extent, split, -0.22, 0.18) * result
    return jnp.clip(result, min=-bound, max=bound).astype(kind)


def bell_draw_with(own_key, extent, width, limit, pieces, heavy, kind=jnp.bfloat16):
    entries = width * jax.random.normal(own_key, extent, jnp.float32)
    if pieces:
        entries = entries * block_levels(own_key, extent, pieces, -0.22, 0.18)
    return jnp.clip(with_spikes(entries, jax.random.fold_in(own_key, 3), *heavy), -limit, limit).astype(kind)


def setup_inputs(seed: int = 0) -> dict:
    streams_of = jax.random.split(jax.random.key(seed), 10)
    tokens = bell_draw_with(streams_of[0], (TOKENS, D), 1.0, 6.0, ((0, 32),), (0, 1, 32, 2.75))
    out_grad = scatter_about(streams_of[1], (TOKENS, D), 0.5, 3.0, ((0, 32),))
    expert_ids_keys = jax.random.split(jax.random.fold_in(streams_of[2], 1), TOKENS // TOK_DEV)
    expert_ids_turns = jax.random.permutation(jax.random.fold_in(streams_of[2], 3), TOKENS // TOK_DEV)
    expert_ids = jax.vmap(lambda own, number: routed_block(jax.random.fold_in(streams_of[2], 2), own, number, TOK_DEV, EXPERTS, TOP, SLOT, 1))(expert_ids_keys, expert_ids_turns).reshape((TOKENS, TOP))
    route_weight = jnp.clip(0.049804688 + 0.54785156 * jax.random.uniform(streams_of[3], (TOKENS, TOP), jnp.float32) ** block_levels(streams_of[3], (TOKENS, TOP), ((0, 32),), -0.2, 0.2), 0.049804688, 0.59765625).astype(jnp.bfloat16)
    live_count = draw_live_count(jax.random.fold_in(streams_of[9], 71), 0)
    cap_blocks = draw_cap_blocks(jax.random.fold_in(streams_of[9], 71), 0)
    w_gate = scatter_about(streams_of[6], (D, UNITS), D ** -0.5, 0.09375, ((0, 4), (1, 8)))
    w_up = scatter_about(streams_of[7], (D, UNITS), D ** -0.5, 0.09375, ((0, 4), (1, 8)))
    w_down_t = scatter_about(streams_of[8], (D, UNITS), F_WIN ** -0.5, 0.1875, ((0, 4), (1, 8)))
    return {"tokens": tokens, "out_grad": out_grad, "expert_ids": expert_ids, "route_weight": route_weight, "live_count": live_count, "cap_blocks": cap_blocks, "w_gate": w_gate, "w_up": w_up, "w_down_t": w_down_t}


def keep_rounded(values):
    rounded = lax.optimization_barrier(values.astype(jnp.bfloat16))
    return rounded.astype(jnp.float32)


def group_grads(group_x, group_dy, group_ids, group_weight, live_here, blocks_here, w_gate, w_up, w_down_t):
    token_total = group_x.shape[0]
    flight = N_EP // SPLIT
    spacing = EXPERTS // flight
    cap_rows = MAX_BLOCKS * BLOCK
    local_index = jnp.arange(token_total, dtype=jnp.int32) % TOK_DEV
    is_live = local_index < live_here
    grad_x = jnp.zeros((token_total, D), jnp.float32)
    grad_w = jnp.zeros((token_total, TOP), jnp.float32)
    gate_cols = []
    up_cols = []
    down_cols = []
    for expert in range(flight):
        matches = group_ids == expert * spacing
        routed = jnp.any(matches, axis=1) & is_live
        arrival = jnp.cumsum(routed.astype(jnp.int32), dtype=jnp.int32) - 1
        kept_mask = routed & (arrival < blocks_here[expert] * BLOCK)
        picked = jnp.nonzero(kept_mask, size=cap_rows, fill_value=0)[0].astype(jnp.int32)
        kept_total = jnp.sum(kept_mask.astype(jnp.int32))
        in_range = (jnp.arange(cap_rows, dtype=jnp.int32) < kept_total).astype(jnp.float32)
        token_rows = group_x[picked]
        grad_rows = group_dy[picked]
        row_match = matches[picked]
        rate = jnp.sum(jnp.where(row_match, group_weight[picked].astype(jnp.float32), 0.0), axis=1) * in_range
        first_col = expert * F_WIN
        gate_part = w_gate[:, first_col:first_col + F_WIN]
        up_part = w_up[:, first_col:first_col + F_WIN]
        down_part = w_down_t[:, first_col:first_col + F_WIN]
        pre_gate = jnp.dot(token_rows, gate_part, preferred_element_type=jnp.float32)
        pre_up = jnp.dot(token_rows, up_part, preferred_element_type=jnp.float32)
        back_hidden = jnp.dot(grad_rows, down_part, preferred_element_type=jnp.float32)
        sigmoid_gate = jax.nn.sigmoid(pre_gate)
        activated = pre_gate * sigmoid_gate
        hidden = activated * pre_up
        slice_score = jnp.sum((hidden * back_hidden).reshape(cap_rows, SPLIT, F_DEV), axis=2)
        row_score = jnp.sum(keep_rounded(slice_score), axis=1) * in_range
        scaled = back_hidden * rate[:, None]
        weighted_hidden = (hidden * rate[:, None]).astype(jnp.bfloat16)
        gate_grad = (scaled * pre_up * sigmoid_gate * (1.0 + pre_gate * (1.0 - sigmoid_gate))).astype(jnp.bfloat16)
        up_grad = (scaled * activated).astype(jnp.bfloat16)
        slice_x = jnp.einsum("csf,dsf->csd", gate_grad.astype(jnp.float32).reshape(cap_rows, SPLIT, F_DEV), gate_part.astype(jnp.float32).reshape(D, SPLIT, F_DEV))
        slice_x = slice_x + jnp.einsum("csf,dsf->csd", up_grad.astype(jnp.float32).reshape(cap_rows, SPLIT, F_DEV), up_part.astype(jnp.float32).reshape(D, SPLIT, F_DEV))
        row_x = jnp.sum(keep_rounded(slice_x), axis=1) * in_range[:, None]
        grad_x = grad_x.at[picked].add(row_x)
        grad_w = grad_w.at[picked].add(jnp.where(row_match, row_score[:, None], 0.0))
        gate_cols.append(jnp.dot(token_rows.T, gate_grad, preferred_element_type=jnp.float32))
        up_cols.append(jnp.dot(token_rows.T, up_grad, preferred_element_type=jnp.float32))
        down_cols.append(jnp.dot(grad_rows.T, weighted_hidden, preferred_element_type=jnp.float32))
    return grad_x, grad_w, jnp.concatenate(gate_cols, axis=1), jnp.concatenate(up_cols, axis=1), jnp.concatenate(down_cols, axis=1)


def reference(tokens, out_grad, expert_ids, route_weight, live_count, cap_blocks, w_gate, w_up, w_down_t):
    per_group = TOK_DEV * N_EP

    def step(carry, group):
        group_x, group_dy, group_ids, group_weight, live_here, blocks_here = group
        grad_x, grad_w, term_gate, term_up, term_down = group_grads(group_x, group_dy, group_ids, group_weight, live_here, blocks_here, w_gate, w_up, w_down_t)
        new_carry = (carry[0] + keep_rounded(term_gate), carry[1] + keep_rounded(term_up), carry[2] + keep_rounded(term_down))
        return new_carry, (grad_x.astype(jnp.bfloat16), grad_w)

    empty = jnp.zeros((D, UNITS), jnp.float32)
    inputs = (tokens.reshape(N_REP, per_group, D), out_grad.reshape(N_REP, per_group, D), expert_ids.reshape(N_REP, per_group, TOP), route_weight.reshape(N_REP, per_group, TOP), live_count, cap_blocks)
    totals, outputs = lax.scan(step, (empty, empty, empty), inputs)
    grad_x, grad_w = outputs
    return (grad_x.reshape(TOKENS, D), grad_w.reshape(TOKENS, TOP), totals[0].astype(jnp.bfloat16), totals[1].astype(jnp.bfloat16), totals[2].astype(jnp.bfloat16))
```

```python
import jax
import jax.numpy as jnp
from jax import lax
from jax.sharding import PartitionSpec as P

EXPERTS = 128
SLOT = 16
BLOCK = 128
SPLIT = 8


def local(
    tokens, out_grad, expert_ids, route_weight, live_count, cap_blocks, w_gate, w_up, w_down_t
):
    rep_count = lax.axis_size("rep")
    ep_count = lax.axis_size("ep")
    flight = ep_count // SPLIT
    spacing = EXPERTS // flight
    tok_count, model_dim = tokens.shape
    width, units = w_gate.shape
    rep_index = lax.axis_index("rep")
    ep_index = lax.axis_index("ep")
    my_expert = ep_index // SPLIT
    same_split = [[w * SPLIT + s for w in range(flight)] for s in range(SPLIT)]
    same_expert = [[w * SPLIT + s for s in range(SPLIT)] for w in range(flight)]

    live_here = live_count[rep_index]
    targets = jnp.arange(flight, dtype=jnp.int32) * spacing
    matches = expert_ids[:, :, None] == targets[None, None, :]
    token_index = jnp.arange(tok_count, dtype=jnp.int32)
    routed = jnp.any(matches, axis=1) & (token_index[:, None] < live_here)
    weight_of = jnp.sum(
        jnp.where(matches, route_weight[:, :, None].astype(jnp.float32), 0.0), axis=1
    )
    slot_rank = jnp.cumsum(routed.astype(jnp.int32), axis=0, dtype=jnp.int32) - 1
    slot_ids = jnp.arange(SLOT, dtype=jnp.int32)
    placed = routed[:, :, None] & (slot_rank[:, :, None] == slot_ids[None, None, :])
    placed = placed.reshape(tok_count, flight * SLOT).astype(jnp.bfloat16)

    def pick(rows):
        chosen = lax.dot_general(
            placed, rows, (((0,), (0,)), ((), ())), preferred_element_type=jnp.float32
        ).astype(jnp.bfloat16)
        return chosen.reshape(flight, SLOT, rep_count, width).transpose(2, 0, 1, 3)

    send = jnp.stack([pick(tokens), pick(out_grad)], axis=1)
    send_weight = jnp.sum(
        placed.reshape(tok_count, flight, SLOT).astype(jnp.float32) * weight_of[:, :, None], axis=0
    ).astype(jnp.bfloat16)
    got = lax.all_to_all(send, "rep", split_axis=0, concat_axis=0, tiled=True)
    if flight > 1:
        got = lax.all_to_all(
            got, "ep", split_axis=2, concat_axis=2, tiled=True, axis_index_groups=same_split
        )
    rows = lax.all_gather(got, "ep", axis=0, axis_index_groups=same_expert)
    rows = rows.transpose(2, 1, 3, 0, 4, 5).reshape(2, rep_count * ep_count * SLOT, width)
    flat_x, flat_dy = rows[0], rows[1]
    all_weight = lax.all_gather(send_weight, "ep", axis=0)
    got_weight = lax.dynamic_index_in_dim(all_weight, my_expert, axis=1, keepdims=False)

    capacity = BLOCK * cap_blocks[rep_index, my_expert]
    present = got_weight > 0
    counts = jnp.sum(present.astype(jnp.int32), axis=1)
    starts = jnp.cumsum(counts, dtype=jnp.int32) - counts
    arrival_rank = starts[:, None] + slot_ids[None, :]
    kept_mask = present & (arrival_rank < capacity)
    rate = jnp.where(kept_mask, got_weight.astype(jnp.float32), 0.0).reshape(-1)[:, None]
    kept = kept_mask.reshape(-1).astype(jnp.float32)

    pre = jnp.concatenate(
        [
            jnp.dot(flat_x, w_gate, preferred_element_type=jnp.float32),
            jnp.dot(flat_x, w_up, preferred_element_type=jnp.float32),
            jnp.dot(flat_dy, w_down_t, preferred_element_type=jnp.float32),
        ],
        axis=1,
    )
    pre = lax.all_to_all(
        pre.reshape(rep_count, ep_count * SLOT, 3 * units), "rep", split_axis=0, concat_axis=0, tiled=True
    )
    pre = jnp.sum(pre, axis=0)
    pre_gate, pre_up, back_hidden = pre[:, :units], pre[:, units : 2 * units], pre[:, 2 * units :]
    sigmoid_gate = jax.nn.sigmoid(pre_gate)
    activated = pre_gate * sigmoid_gate
    hidden = activated * pre_up
    score = (jnp.sum(hidden * back_hidden, axis=1) * kept).astype(jnp.bfloat16)
    scaled = back_hidden * rate
    grads = jnp.concatenate(
        [
            scaled * pre_up * sigmoid_gate * (1.0 + pre_gate * (1.0 - sigmoid_gate)),
            scaled * activated,
            hidden * rate,
        ],
        axis=1,
    ).astype(jnp.bfloat16)
    grads = lax.all_gather(grads, "rep", axis=0, tiled=True)
    gate_grad, up_grad, weighted = grads[:, :units], grads[:, units : 2 * units], grads[:, 2 * units :]

    contract_units = (((1,), (1,)), ((), ()))
    partial_x = lax.dot_general(
        gate_grad, w_gate, contract_units, preferred_element_type=jnp.float32
    ) + lax.dot_general(up_grad, w_up, contract_units, preferred_element_type=jnp.float32)
    partial_x = partial_x.astype(jnp.bfloat16).reshape(rep_count, flight, SPLIT, SLOT, width)
    back = lax.all_to_all(
        partial_x, "ep", split_axis=2, concat_axis=2, tiled=True, axis_index_groups=same_expert
    )
    back = jnp.sum(back, axis=2, dtype=jnp.float32).astype(jnp.bfloat16)
    if flight > 1:
        back = lax.all_to_all(
            back, "ep", split_axis=1, concat_axis=1, tiled=True, axis_index_groups=same_split
        )
    back = lax.all_to_all(back, "rep", split_axis=0, concat_axis=0, tiled=True)
    back = back.transpose(1, 2, 0, 3).reshape(flight * SLOT, model_dim)
    grad_tokens = jnp.dot(placed, back, preferred_element_type=jnp.float32).astype(jnp.bfloat16)

    all_score = lax.all_to_all(
        score.reshape(ep_count, SLOT), "ep", split_axis=0, concat_axis=0, tiled=True
    )
    slot_score = jnp.sum(
        all_score.reshape(flight, SPLIT, SLOT), axis=1, dtype=jnp.float32
    )
    token_score = jnp.sum(
        placed.reshape(tok_count, flight, SLOT).astype(jnp.float32) * slot_score[None], axis=2
    )
    grad_weight = jnp.sum(jnp.where(matches, token_score[:, None, :], 0.0), axis=2)

    contract_rows = (((0,), (0,)), ((), ()))

    def weight_grad(inputs, hidden_grad):
        return lax.dot_general(
            inputs, hidden_grad, contract_rows, preferred_element_type=jnp.float32
        ).astype(jnp.bfloat16)

    return (
        grad_tokens,
        grad_weight,
        weight_grad(flat_x, gate_grad),
        weight_grad(flat_x, up_grad),
        weight_grad(flat_dy, weighted),
    )


def solution(mesh):
    return jax.shard_map(
        local,
        mesh=mesh,
        in_specs=(
            P(("rep", "ep"), None),
            P(("rep", "ep"), None),
            P(("rep", "ep"), None),
            P(("rep", "ep"), None),
            P(),
            P(),
            P("rep", "ep"),
            P("rep", "ep"),
            P("rep", "ep"),
        ),
        out_specs=(
            P(("rep", "ep"), None),
            P(("rep", "ep"), None),
            P("rep", "ep"),
            P("rep", "ep"),
            P("rep", "ep"),
        ),
        check_vma=False,
    )
```

```python
import functools

import jax
import jax.numpy as jnp
from jax import lax
from jax.experimental import pallas as pl
from jax.experimental.pallas import tpu as pltpu
from jax.sharding import PartitionSpec as P

EXPERTS = 128
SLOT = 16
BLOCK = 128
SPLIT = 8
CORES = 2
CHIPS = SPLIT // CORES
LANES = 128
F32 = jnp.float32
BF16 = jnp.bfloat16
SMEM = pl.BlockSpec(memory_space=pltpu.SMEM)
VMEM = pl.BlockSpec(memory_space=pltpu.VMEM)


def shape(dims, kind=BF16):
    return jax.ShapeDtypeStruct(dims, kind)


def call(kernel, outs, args, scalars=0, scratch=(), flops=0):
    size = sum(a.size * a.dtype.itemsize for a in args) + sum(
        o.size * o.dtype.itemsize for o in outs
    )
    return pl.pallas_call(
        kernel,
        out_shape=tuple(outs),
        in_specs=[SMEM] * scalars + [VMEM] * (len(args) - scalars),
        out_specs=tuple([VMEM] * len(outs)),
        scratch_shapes=scratch,
        compiler_params=pltpu.CompilerParams(vmem_limit_bytes=40 * 1024 * 1024),
        cost_estimate=pl.CostEstimate(flops=flops, bytes_accessed=size, transcendentals=0),
    )(*args)


def dot(a, b, dims=((1,), (0,))):
    return lax.dot_general(a, b, (dims, ((), ())), preferred_element_type=F32)


def iota(dims, axis):
    return lax.broadcasted_iota(jnp.int32, dims, axis)


def pack_kernel(rep, flight, live_ref, tok_ref, grad_ref, ids_ref, rw_ref, *refs):
    pays, hdr_ref, placed_ref, rows = refs[:rep], refs[rep], refs[rep + 1], refs[rep + 2]
    r = lax.axis_index("rep")
    mine = lax.axis_index("ep") // SPLIT
    count = tok_ref.shape[0]
    width = tok_ref.shape[1] // rep
    spacing = EXPERTS // flight
    token = iota((count, 1), 0)
    lower = (iota((count, count), 1) <= iota((count, count), 0)).astype(BF16)
    lane = iota((count, LANES), 1)
    weights = rw_ref[...].astype(F32)
    header = jnp.zeros((SLOT, LANES), F32)
    for w in range(flight):
        expert = jnp.bitwise_xor(mine, w)
        match = ids_ref[...] == expert * spacing
        routed = jnp.any(match, axis=1, keepdims=True) & (token < live_ref[r])
        weight = jnp.sum(jnp.where(match, weights, 0.0), axis=1, keepdims=True)
        routed_f = jnp.broadcast_to(jnp.where(routed, 1.0, 0.0), (count, LANES))
        rank = dot(lower, routed_f.astype(BF16)) - 1.0
        placed = jnp.where((rank == (lane % SLOT).astype(F32)), routed_f, 0.0).astype(BF16)
        placed_ref[w] = placed
        first = placed[:, :SLOT]
        header += dot(first, jnp.where(lane == expert, weight, 0.0).astype(BF16), ((0,), (0,)))
        for part, ref in enumerate((tok_ref, grad_ref)):
            chosen = dot(first, ref[...], ((0,), (0,))).astype(BF16)
            for b in range(rep):
                rows[b, w, part] = chosen[:, b * width : (b + 1) * width]
    hdr_ref[0] = header
    for k in range(rep):
        pays[k][...] = rows[jnp.bitwise_xor(r, k)]


def join_kernel(rep, flight, *refs):
    pays, xs, dys = refs[:rep], refs[rep : rep + flight], refs[rep + flight :]
    for w in range(flight):
        for k in range(rep):
            xs[w][k] = pays[k][w, 0]
            dys[w][k] = pays[k][w, 1]


def forward_kernel(rep, count, *refs):
    blocks, own_w, other_w = refs[:count], refs[count], refs[count + 1]
    sums, rows_ref = refs[count + 2 : count + 2 + rep], refs[count + 2 + rep]
    width = own_w.shape[0]
    units = own_w.shape[1]
    for k in range(rep):
        rows = jnp.concatenate([b[k] for b in blocks], axis=0)
        rows_ref[k] = rows
        sums[k][:, :units] = dot(rows, own_w[...]).astype(sums[k].dtype)
        sums[k][:, units:] = dot(rows, other_w[...]).astype(sums[k].dtype)


def hidden_kernel(rep, count, units, cap_ref, hdr_ref, *refs):
    sums_x, sums_d = refs[:rep], refs[rep : 2 * rep]
    weights = refs[2 * rep : 4 * rep]
    back_refs, grad_refs = refs[4 * rep : 4 * rep + count], refs[4 * rep + count :]
    r = lax.axis_index("rep")
    e = lax.axis_index("ep")
    mine = e // SPLIT
    width = weights[0].shape[0]
    ep = hdr_ref.shape[0]
    rates = jnp.where(iota(hdr_ref.shape, 2) == mine, hdr_ref[...], 0.0)
    rates = jnp.sum(rates, axis=2, keepdims=True)
    present = rates > 0.0
    counts = jnp.sum(jnp.where(present, 1.0, 0.0), axis=1, keepdims=True)
    order = jnp.bitwise_xor(iota((ep, 1, 1), 0), e)
    capacity = (BLOCK * cap_ref[r, mine]).astype(F32)
    slot = iota((SLOT, 1), 0).astype(F32)
    rate_rows, kept_rows = [], []
    for j in range(count):
        source = CORES * j
        before = jnp.where(order < jnp.bitwise_xor(e, source), counts, 0.0)
        start = jnp.sum(before, axis=0)
        kept = jnp.where(present[source] & (start + slot < capacity), 1.0, 0.0)
        kept_rows.append(kept)
        rate_rows.append(rates[source] * kept)
    rate = jnp.concatenate(rate_rows, axis=0)
    kept = jnp.concatenate(kept_rows, axis=0)

    total_x = sums_x[0][...]
    total_d = sums_d[0][...]
    for k in range(1, rep):
        total_x = total_x + sums_x[k][...].astype(F32)
        total_d = total_d + sums_d[k][...].astype(F32)
    lane = iota((count * SLOT, LANES), 1)
    scores = jnp.zeros((count * SLOT, LANES), F32)
    pairs = []
    for i in range(CORES):
        pre_gate = total_x[:, 2 * i * units : (2 * i + 1) * units]
        pre_up = total_x[:, (2 * i + 1) * units : (2 * i + 2) * units]
        back_hidden = total_d[:, i * units : (i + 1) * units]
        sig = 1.0 / (1.0 + jnp.exp(-pre_gate))
        activated = pre_gate * sig
        hidden = activated * pre_up
        score = jnp.sum(hidden * back_hidden, axis=1, keepdims=True) * kept
        scores = jnp.where(lane == i, score, scores)
        scaled = back_hidden * rate
        gate_grad = (scaled * pre_up * sig * (1.0 + pre_gate * (1.0 - sig))).astype(BF16)
        up_grad = (scaled * activated).astype(BF16)
        grad_refs[i][:, :units] = gate_grad
        grad_refs[i][:, units : 2 * units] = up_grad
        grad_refs[i][:, 2 * units :] = (hidden * rate).astype(BF16)
        pairs.append(jnp.concatenate([gate_grad, up_grad], axis=1))
    for k in range(rep):
        back = dot(pairs[0], weights[2 * k][...], ((1,), (1,)))
        back = back + dot(pairs[1], weights[2 * k + 1][...], ((1,), (1,)))
        back = back.astype(BF16)
        for j in range(count):
            back_refs[j][:, k * width : (k + 1) * width] = back[j * SLOT : (j + 1) * SLOT]
    scores = scores.astype(BF16)
    for j in range(count):
        back_refs[j][:, rep * width :] = scores[j * SLOT : (j + 1) * SLOT]


def weight_kernel(rep, units, x_own, x_other, d_own, d_other, *refs):
    grads, outs = refs[: 2 * rep], refs[2 * rep :]
    width = x_own.shape[2]
    gate_up = jnp.zeros((width, 2 * units), F32)
    down = jnp.zeros((width, units), F32)
    for i, (x_ref, d_ref) in enumerate(((x_own, d_own), (x_other, d_other))):
        got = jnp.concatenate([grads[2 * k + i][...] for k in range(rep)], axis=0)
        rows = x_ref[...].reshape(got.shape[0], width)
        gate_up = gate_up + dot(rows, got[:, : 2 * units], ((0,), (0,)))
        rows = d_ref[...].reshape(got.shape[0], width)
        down = down + dot(rows, got[:, 2 * units :], ((0,), (0,)))
    outs[0][...] = gate_up[:, :units].astype(BF16)
    outs[1][...] = gate_up[:, units:].astype(BF16)
    outs[2][...] = down.astype(BF16)


def token_kernel(rep, flight, placed_ref, ids_ref, *refs):
    backs, out_ref, weight_ref, blocks = refs[:-3], refs[-3], refs[-2], refs[-1]
    r = lax.axis_index("rep")
    mine = lax.axis_index("ep") // SPLIT
    spacing = EXPERTS // flight
    width = out_ref.shape[1] // rep
    depth = CHIPS * SLOT
    joined = [
        jnp.concatenate([b[...] for b in backs[w * CHIPS : (w + 1) * CHIPS]], axis=0)
        for w in range(flight)
    ]
    for k in range(rep):
        total = jnp.zeros((out_ref.shape[0], width), F32)
        for w in range(flight):
            total = total + dot(placed_ref[w][:, :depth], joined[w][:, k * width : (k + 1) * width])
        blocks[jnp.bitwise_xor(r, k)] = total.astype(BF16)
    for b in range(rep):
        out_ref[:, b * width : (b + 1) * width] = blocks[b]
    result = jnp.zeros(weight_ref.shape, F32)
    for w in range(flight):
        score = dot(placed_ref[w][:, :depth], joined[w][:, rep * width :])
        score = jnp.sum(score, axis=1, keepdims=True)
        match = ids_ref[...] == jnp.bitwise_xor(mine, w) * spacing
        result = result + jnp.where(match, score, 0.0)
    weight_ref[...] = result


def local(
    tokens, out_grad, expert_ids, route_weight, live_count, cap_blocks, w_gate, w_up, w_down_t
):
    rep = lax.axis_size("rep")
    ep = lax.axis_size("ep")
    flight = ep // SPLIT
    count = ep // CORES
    tok_count, model_dim = tokens.shape
    width, units = w_gate.shape
    rows = count * SLOT

    def send(array, rep_bits, ep_bits):
        mask = rep_bits * ep + ep_bits
        pairs = [(a, a ^ mask) for a in range(rep * ep)]
        return lax.ppermute(array, ("rep", "ep"), pairs)

    packed = call(
        functools.partial(pack_kernel, rep, flight),
        [shape((flight, 2, SLOT, width))] * rep
        + [shape((1, SLOT, LANES), F32), shape((flight, tok_count, LANES))],
        [live_count, tokens, out_grad, expert_ids, route_weight],
        scalars=1,
        scratch=[pltpu.VMEM((rep, flight, 2, SLOT, width), BF16)],
    )
    pays, header, placed = packed[:rep], packed[rep], packed[rep + 1]
    pays = [pays[0]] + [send(pays[k], k, 0) for k in range(1, rep)]
    gate_up = jnp.concatenate([w_gate, w_up], axis=1)
    gate_up_other, down_other = send(gate_up, 0, 1), send(w_down_t, 0, 1)
    bit = 1
    while bit < ep:
        header = jnp.concatenate([header, send(header, 0, bit)], axis=0)
        bit *= 2

    joined = call(
        functools.partial(join_kernel, rep, flight),
        [shape((rep, SLOT, width))] * (2 * flight),
        pays,
    )
    gate_up_late, joined = lax.optimization_barrier((gate_up, joined))
    xs, dys = joined[:flight], joined[flight:]
    x_blocks = [xs[0]] + [send(xs[j // CHIPS], 0, CORES * j) for j in range(1, count)]
    dy_blocks = [dys[0]] + [send(dys[j // CHIPS], 0, CORES * j) for j in range(1, count)]
    stored = [gate_up, gate_up_other]
    for k in range(1, rep):
        moved = send(gate_up_late, k, 0)
        stored += [moved, send(moved, 0, 1)]

    def forward(blocks, own, other):
        columns = 2 * own.shape[1]
        results = call(
            functools.partial(forward_kernel, rep, count),
            [shape((rows, columns), F32)]
            + [shape((rows, columns))] * (rep - 1)
            + [shape((rep, rows, width))],
            blocks + [own, other],
            flops=2 * rep * rows * width * columns,
        )
        sums, all_rows = results[:rep], results[rep]
        return [sums[0]] + [send(sums[k], k, 0) for k in range(1, rep)], all_rows

    sums_x, x_rows = forward(x_blocks, gate_up, gate_up_other)
    sums_d, dy_rows = forward(dy_blocks, w_down_t, down_other)
    x_rows_other, dy_rows_other = send(x_rows, 0, 1), send(dy_rows, 0, 1)

    results = call(
        functools.partial(hidden_kernel, rep, count, units),
        [shape((SLOT, model_dim + LANES))] * count + [shape((rows, 3 * units))] * CORES,
        [cap_blocks, header] + sums_x + sums_d + stored,
        scalars=1,
        flops=2 * rows * model_dim * 4 * units,
    )
    backs, grads = results[:count], results[count:]
    backs = [backs[0]] + [send(backs[j], 0, CORES * j) for j in range(1, count)]
    grads = [
        grads[i] if k + i == 0 else send(grads[i], k, i) for k in range(rep) for i in range(CORES)
    ]

    grad_gate, grad_up, grad_down = call(
        functools.partial(weight_kernel, rep, units),
        [shape((width, units))] * 3,
        [x_rows, x_rows_other, dy_rows, dy_rows_other] + grads,
        flops=2 * 2 * rep * rows * width * 3 * units,
    )
    grad_tokens, grad_weight = call(
        functools.partial(token_kernel, rep, flight),
        [shape((tok_count, model_dim)), shape(expert_ids.shape, F32)],
        [placed, expert_ids] + backs,
        scratch=[pltpu.VMEM((rep, tok_count, width), BF16)],
        flops=2 * tok_count * CHIPS * SLOT * model_dim,
    )
    return grad_tokens, grad_weight, grad_gate, grad_up, grad_down


def solution(mesh):
    return jax.shard_map(
        local,
        mesh=mesh,
        in_specs=(
            P(("rep", "ep"), None),
            P(("rep", "ep"), None),
            P(("rep", "ep"), None),
            P(("rep", "ep"), None),
            P(),
            P(),
            P("rep", "ep"),
            P("rep", "ep"),
            P("rep", "ep"),
        ),
        out_specs=(
            P(("rep", "ep"), None),
            P(("rep", "ep"), None),
            P("rep", "ep"),
            P("rep", "ep"),
            P("rep", "ep"),
        ),
        check_vma=False,
    )
```

```python
import functools

import jax
import jax.numpy as jnp
from jax import lax
from jax.experimental import pallas as pl
from jax.experimental.pallas import tpu as pltpu
from jax.sharding import PartitionSpec as P

EXPERTS = 128
SLOT = 16
BLOCK = 128
SPLIT = 8
CORES = 2
CHIPS = SPLIT // CORES
LANES = 128
F32 = jnp.float32
BF16 = jnp.bfloat16
PARTS = 4
ANY = pl.BlockSpec(memory_space=pl.ANY)
VMEM = pl.BlockSpec(memory_space=pltpu.VMEM)


def shape(dims, kind=BF16):
    return jax.ShapeDtypeStruct(dims, kind)


def call(kernel, outs, args, outside=0, scratch=(), flops=0):
    size = sum(a.size * a.dtype.itemsize for a in args) + sum(
        o.size * o.dtype.itemsize for o in outs
    )
    return pl.pallas_call(
        kernel,
        out_shape=tuple(outs),
        in_specs=[ANY] * outside + [VMEM] * (len(args) - outside),
        out_specs=tuple([VMEM] * len(outs)),
        scratch_shapes=scratch,
        compiler_params=pltpu.CompilerParams(vmem_limit_bytes=24 * 1024 * 1024),
        cost_estimate=pl.CostEstimate(flops=flops, bytes_accessed=size, transcendentals=0),
    )(*args)


def dot(a, b, dims=((1,), (0,))):
    return lax.dot_general(a, b, (dims, ((), ())), preferred_element_type=F32)


def iota(dims, axis):
    return lax.broadcasted_iota(jnp.int32, dims, axis)


def ring_chip(place):
    return jnp.bitwise_xor(place, place // 2)


def pack_kernel(rep, flight, live_ref, tok_ref, grad_ref, ids_ref, rw_ref, *refs):
    pays, placed_ref = refs[:flight], refs[flight]
    live, data, rows, sems = refs[flight + 1 :]
    r = lax.axis_index("rep")
    mine = lax.axis_index("ep") // SPLIT
    count, model = tok_ref.shape
    width = model // rep
    spacing = EXPERTS // flight
    live_copy = pltpu.make_async_copy(live_ref, live, sems.at[2 * PARTS])
    live_copy.start()
    copies = []
    for part, ref in enumerate((tok_ref, grad_ref)):
        for p in range(PARTS):
            some = pl.ds(p * (count // PARTS), count // PARTS)
            copy = pltpu.make_async_copy(
                ref.at[some], data.at[part, some], sems.at[part * PARTS + p]
            )
            copy.start()
            copies.append(copy)
    live_copy.wait()
    token = iota((1, count), 1)
    upper = (iota((count, count), 0) <= iota((count, count), 1)).astype(BF16)
    slot = iota((SLOT, count), 0).astype(F32)
    lane = iota((SLOT, LANES), 1)
    ids = ids_ref[...]
    weights = rw_ref[...].astype(F32)
    firsts, headers = [], []
    for w in range(flight):
        expert = jnp.bitwise_xor(mine, w)
        match = ids == expert * spacing
        routed = jnp.any(match, axis=0, keepdims=True) & (token < live[r])
        weight = jnp.sum(jnp.where(match, weights, 0.0), axis=0, keepdims=True)
        routed = jnp.broadcast_to(jnp.where(routed, 1.0, 0.0), (SLOT, count))
        rank = dot(routed.astype(BF16), upper) - 1.0
        placed = jnp.where(rank == slot, routed, 0.0)
        column = jnp.sum(placed * weight, axis=1, keepdims=True)
        headers.append(jnp.where(lane == 0, column, 0.0).astype(BF16))
        placed = placed.astype(BF16)
        firsts.append(placed)
        placed_ref[w] = jnp.concatenate([placed] * CHIPS, axis=0)
    for part in range(2):
        for p in range(PARTS):
            copies[part * PARTS + p].wait()
        for w in range(flight):
            chosen = dot(firsts[w], data[part]).astype(BF16)
            for b in range(rep):
                rows[b] = chosen[:, b * width : (b + 1) * width]
            for k in range(rep):
                pays[w][part, :, k * width : (k + 1) * width] = rows[jnp.bitwise_xor(r, k)]
            pays[w][part, :, model:] = headers[w]


def forward_kernel(rep, count, *refs):
    blocks, pieces, outs = refs[:count], refs[count : -(rep + 3)], refs[-(rep + 3) :]
    pre_x, pre_d, header_ref, parts = outs[0], outs[1], outs[2], outs[3:]
    half, columns = pieces[0].shape
    width = 2 * half
    units = columns // 3
    rows = [jnp.concatenate([b[part] for b in blocks], axis=0) for part in range(2)]
    for j in range(count):
        header_ref[j] = blocks[j][0, :, rep * width :]
    for k in range(rep):
        for part in range(2):
            parts[k][part] = rows[part][:, k * width : (k + 1) * width]
    for i in range(CORES):
        sum_x, sum_d = 0.0, 0.0
        for p in range(len(pieces) // CORES):
            piece = pieces[CORES * p + i]
            some = slice(p * half, (p + 1) * half)
            sum_x = sum_x + dot(rows[0][:, some], piece[:, : 2 * units])
            sum_d = sum_d + dot(rows[1][:, some], piece[:, 2 * units :])
        pre_x[:, 2 * i * units : 2 * (i + 1) * units] = sum_x
        pre_d[:, i * units : (i + 1) * units] = sum_d


def hidden_kernel(rep, count, cap_ref, own_ref, other_ref, pre_x, pre_d, *refs):
    parts, pieces = refs[0], refs[1 : 1 + 4 * rep]
    back_refs, grad_refs = refs[1 + 4 * rep : 1 + 4 * rep + count], refs[1 + 4 * rep + count : -2]
    cap, sem = refs[-2:]
    cap_copy = pltpu.make_async_copy(cap_ref, cap, sem)
    cap_copy.start()
    half, columns = pieces[0].shape
    width = 2 * half
    units = columns // 3
    r = lax.axis_index("rep")
    e = lax.axis_index("ep")
    mine = e // SPLIT
    place = ring_chip((e % SPLIT) // CORES)
    cap_copy.wait()
    capacity = (BLOCK * cap[r, mine]).astype(F32)
    lane = iota((SLOT, LANES), 1)
    sources, rates, counts = [], [], []
    for core, ref in enumerate((own_ref, other_ref)):
        for j in range(count):
            chip = ring_chip((place + CHIPS - j % CHIPS) % CHIPS)
            expert = jnp.bitwise_xor(mine, j // CHIPS)
            source = expert * SPLIT + chip * CORES + jnp.bitwise_xor(e % CORES, core)
            rate = jnp.where(lane == 0, ref[j].astype(F32), 0.0)
            rate = jnp.sum(rate, axis=1, keepdims=True)
            sources.append(source)
            rates.append(rate)
            counts.append(jnp.sum(jnp.where(rate > 0.0, 1.0, 0.0), axis=0, keepdims=True))
    slot = iota((SLOT, 1), 0).astype(F32)
    rate_rows, kept_rows = [], []
    for j in range(count):
        start = jnp.zeros((1, 1), F32)
        for other in range(len(sources)):
            start = start + jnp.where(sources[other] < sources[j], counts[other], 0.0)
        kept = jnp.where((rates[j] > 0.0) & (start + slot < capacity), 1.0, 0.0)
        kept_rows.append(kept)
        rate_rows.append(rates[j] * kept)
    rate = jnp.concatenate(rate_rows, axis=0)
    kept = jnp.concatenate(kept_rows, axis=0)

    lane = iota((count * SLOT, LANES), 1)
    scores = jnp.zeros((count * SLOT, LANES), F32)
    pairs = []
    for i in range(CORES):
        sum_x = pre_x[:, 2 * i * units : 2 * (i + 1) * units]
        sum_d = pre_d[:, i * units : (i + 1) * units]
        for h in range(2):
            piece = pieces[CORES * (2 * rep - 2 + h) + i]
            some = slice(h * half, (h + 1) * half)
            sum_x = sum_x + dot(parts[0, :, some], piece[:, : 2 * units])
            sum_d = sum_d + dot(parts[1, :, some], piece[:, 2 * units :])
        pre_gate, pre_up, back_hidden = sum_x[:, :units], sum_x[:, units:], sum_d
        sig = 1.0 / (1.0 + jnp.exp(-pre_gate))
        activated = pre_gate * sig
        hidden = activated * pre_up
        score = jnp.sum(hidden * back_hidden, axis=1, keepdims=True) * kept
        scores = jnp.where(lane == i, score, scores)
        scaled = back_hidden * rate
        gate_grad = (scaled * pre_up * sig * (1.0 + pre_gate * (1.0 - sig))).astype(BF16)
        up_grad = (scaled * activated).astype(BF16)
        grad_refs[i][:, :units] = gate_grad
        grad_refs[i][:, units : 2 * units] = up_grad
        grad_refs[i][:, 2 * units :] = (hidden * rate).astype(BF16)
        pairs.append(jnp.concatenate([gate_grad, up_grad], axis=1))
    for p in range(2 * rep):
        back = dot(pairs[0], pieces[CORES * p][:, : 2 * units], ((1,), (1,)))
        back = back + dot(pairs[1], pieces[CORES * p + 1][:, : 2 * units], ((1,), (1,)))
        back = back.astype(BF16)
        for j in range(count):
            back_refs[j][:, p * half : (p + 1) * half] = back[j * SLOT : (j + 1) * SLOT]
    scores = scores.astype(BF16)
    for j in range(count):
        back_refs[j][:, rep * width :] = scores[j * SLOT : (j + 1) * SLOT]


def weight_kernel(rep, units, *refs):
    own, other, grads, outs = refs[:rep], refs[rep : 2 * rep], refs[2 * rep : 3 * rep], refs[-3:]
    width = own[0].shape[2]
    got = jnp.concatenate([g[...] for g in grads], axis=0)
    rows = [
        jnp.concatenate([ref[part] for k in range(rep) for ref in (own[k], other[k])], axis=0)
        for part in range(2)
    ]
    gate_up = dot(rows[0], got[:, : 2 * units], ((0,), (0,)))
    outs[0][...] = gate_up[:, :units].astype(BF16)
    outs[1][...] = gate_up[:, units:].astype(BF16)
    outs[2][...] = dot(rows[1], got[:, 2 * units :], ((0,), (0,))).astype(BF16)


def token_kernel(rep, flight, placed_ref, ids_ref, *refs):
    backs, out_ref, weight_ref, blocks = refs[:-3], refs[-3], refs[-2], refs[-1]
    r = lax.axis_index("rep")
    mine = lax.axis_index("ep") // SPLIT
    spacing = EXPERTS // flight
    width = out_ref.shape[1] // rep
    joined = [
        jnp.concatenate([b[...] for b in backs[w * CHIPS : (w + 1) * CHIPS]], axis=0)
        for w in range(flight)
    ]
    for k in range(rep):
        total = 0.0
        for w in range(flight):
            some = joined[w][:, k * width : (k + 1) * width]
            total = total + dot(placed_ref[w], some, ((0,), (0,)))
        blocks[jnp.bitwise_xor(r, k)] = total.astype(BF16)
    for b in range(rep):
        out_ref[:, b * width : (b + 1) * width] = blocks[b]
    result = jnp.zeros(weight_ref.shape, F32)
    for w in range(flight):
        score = dot(joined[w][:, rep * width :], placed_ref[w], ((0,), (0,)))
        score = jnp.sum(score, axis=0, keepdims=True)
        match = ids_ref[...] == jnp.bitwise_xor(mine, w) * spacing
        result = result + jnp.where(match, score, 0.0)
    weight_ref[...] = result


def local(
    tokens, out_grad, expert_ids, route_weight, live_count, cap_blocks, w_gate, w_up, w_down_t
):
    rep = lax.axis_size("rep")
    ep = lax.axis_size("ep")
    flight = ep // SPLIT
    count = ep // CORES
    tok_count, model_dim = tokens.shape
    width, units = w_gate.shape
    half = width // 2
    rows = count * SLOT
    payload = model_dim + LANES

    def send(array, rep_bits, ep_bits):
        mask = rep_bits * ep + ep_bits
        pairs = [(a, a ^ mask) for a in range(rep * ep)]
        return lax.ppermute(array, ("rep", "ep"), pairs)

    def send_ring(array, step):
        pairs = []
        for expert in range(flight):
            for p in range(CHIPS):
                q = (p + step) % CHIPS
                for core in range(CORES):
                    first = expert * SPLIT + core
                    pairs.append((first + CORES * (p ^ p // 2), first + CORES * (q ^ q // 2)))
        return lax.ppermute(array, "ep", pairs)

    first, second = (
        jnp.concatenate([w[h * half : (h + 1) * half] for w in (w_gate, w_up, w_down_t)], axis=1)
        for h in range(2)
    )
    halves = {(0, 0): first, (0, 1): second}
    for k in range(1, rep):
        low, high = k & -k, 1 << (k.bit_length() - 1)
        halves[k, 0] = send(halves[k ^ low, 0], low, 0)
        halves[k, 1] = send(halves[k ^ high, 1], high, 0)
    pieces = []
    for k in range(rep):
        for h in range(2):
            pieces += [halves[k, h], send(halves[k, h], 0, 1)]

    packed = call(
        functools.partial(pack_kernel, rep, flight),
        [shape((2, SLOT, payload))] * flight + [shape((flight, CHIPS * SLOT, tok_count))],
        [live_count, tokens, out_grad, expert_ids.T, route_weight.T],
        outside=3,
        scratch=[
            pltpu.SMEM(live_count.shape, jnp.int32),
            pltpu.VMEM((2, tok_count, model_dim), BF16),
            pltpu.VMEM((rep, SLOT, width), BF16),
            pltpu.SemaphoreType.DMA((2 * PARTS + 1,)),
        ],
    )
    pays, placed = packed[:flight], packed[flight]
    blocks = []
    for w in range(flight):
        block = pays[w] if w == 0 else send(pays[w], 0, w * SPLIT)
        blocks.append(block)
        for _ in range(1, CHIPS):
            block = send_ring(block, 1)
            blocks.append(block)

    results = call(
        functools.partial(forward_kernel, rep, count),
        [
            shape((rows, 2 * CORES * units), F32),
            shape((rows, CORES * units), F32),
            shape((count, SLOT, LANES)),
        ]
        + [shape((2, rows, width))] * rep,
        blocks + pieces[: -2 * CORES],
        flops=2 * rows * model_dim * 3 * CORES * units,
    )
    pre_x, pre_d, header, parts = results[0], results[1], results[2], list(results[3:])
    header_other = send(header, 0, 1)
    results = call(
        functools.partial(hidden_kernel, rep, count),
        [shape((SLOT, payload))] * count + [shape((rows, 3 * units))] * CORES,
        [cap_blocks, header, header_other, pre_x, pre_d, parts[-1]] + pieces,
        outside=1,
        scratch=[pltpu.SMEM(cap_blocks.shape, jnp.int32), pltpu.SemaphoreType.DMA(())],
        flops=2 * rows * model_dim * 4 * units,
    )
    backs, grads = results[:count], results[count:]
    grads = jnp.concatenate([grads[0], send(grads[1], 0, 1)], axis=0)
    returned = [backs[0]]
    for j in range(1, count):
        back = send_ring(backs[j], CHIPS - j % CHIPS) if j % CHIPS else backs[j]
        returned.append(send(back, 0, j // CHIPS * SPLIT) if j >= CHIPS else back)

    own_rows = [parts[0]] + [send(parts[k], k, 0) for k in range(1, rep)]
    other_rows = [send(own_rows[k], 0, 1) for k in range(rep)]
    group_grads = [grads] + [send(grads, k, 0) for k in range(1, rep)]
    grad_gate, grad_up, grad_down = call(
        functools.partial(weight_kernel, rep, units),
        [shape((width, units))] * 3,
        own_rows + other_rows + group_grads,
        flops=2 * 2 * rep * rows * width * 3 * units,
    )
    grad_tokens, grad_weight = call(
        functools.partial(token_kernel, rep, flight),
        [shape((tok_count, model_dim)), shape(expert_ids.shape[::-1], F32)],
        [placed, expert_ids.T] + returned,
        scratch=[pltpu.VMEM((rep, tok_count, width), BF16)],
        flops=2 * tok_count * CHIPS * SLOT * model_dim,
    )
    return grad_tokens, grad_weight.T, grad_gate, grad_up, grad_down


def solution(mesh):
    return jax.shard_map(
        local,
        mesh=mesh,
        in_specs=(
            P(("rep", "ep"), None),
            P(("rep", "ep"), None),
            P(("rep", "ep"), None),
            P(("rep", "ep"), None),
            P(),
            P(),
            P("rep", "ep"),
            P("rep", "ep"),
            P("rep", "ep"),
        ),
        out_specs=(
            P(("rep", "ep"), None),
            P(("rep", "ep"), None),
            P("rep", "ep"),
            P("rep", "ep"),
            P("rep", "ep"),
        ),
        check_vma=False,
    )
```

```python
import functools

import jax
import jax.numpy as jnp
from jax import lax
from jax.experimental import pallas as pl
from jax.experimental.pallas import tpu as pltpu
from jax.sharding import PartitionSpec as P

EXPERTS = 128
SLOT = 16
BLOCK = 128
SPLIT = 8
CORES = 2
CHIPS = SPLIT // CORES
LANES = 128
F32 = jnp.float32
BF16 = jnp.bfloat16
PARTS = 4
ANY = pl.BlockSpec(memory_space=pl.ANY)
VMEM = pl.BlockSpec(memory_space=pltpu.VMEM)


def shape(dims, kind=BF16):
    return jax.ShapeDtypeStruct(dims, kind)


def call(kernel, outs, args, inside=(), scratch=(), flops=0):
    size = sum(a.size * a.dtype.itemsize for a in args) + sum(
        o.size * o.dtype.itemsize for o in outs
    )
    return pl.pallas_call(
        kernel,
        out_shape=tuple(outs),
        in_specs=[VMEM if n in inside else ANY for n in range(len(args))],
        out_specs=tuple([VMEM] * len(outs)),
        scratch_shapes=scratch,
        compiler_params=pltpu.CompilerParams(vmem_limit_bytes=24 * 1024 * 1024),
        cost_estimate=pl.CostEstimate(flops=flops, bytes_accessed=size, transcendentals=0),
    )(*args)


def buffers(arrays):
    held = [pltpu.VMEM(a.shape, a.dtype) for a in arrays]
    return held + [pltpu.SemaphoreType.DMA((len(arrays),))]


def fetch(refs, held, sems):
    copies = [
        pltpu.make_async_copy(ref, buffer, sems.at[n])
        for n, (ref, buffer) in enumerate(zip(refs, held))
    ]
    for copy in copies:
        copy.start()
    return copies


def dot(a, b, dims=((1,), (0,))):
    return lax.dot_general(a, b, (dims, ((), ())), preferred_element_type=F32)


def iota(dims, axis):
    return lax.broadcasted_iota(jnp.int32, dims, axis)


def pack_kernel(rep, flight, live_ref, tok_ref, grad_ref, ids_ref, rw_ref, *refs):
    pays, placed_ref = refs[:flight], refs[flight]
    live, data, rows, sems = refs[flight + 1 :]
    r = lax.axis_index("rep")
    mine = lax.axis_index("ep") // SPLIT
    count, model = tok_ref.shape
    width = model // rep
    spacing = EXPERTS // flight
    live_copy = pltpu.make_async_copy(live_ref, live, sems.at[2 * PARTS])
    live_copy.start()
    copies = []
    for part, ref in enumerate((tok_ref, grad_ref)):
        for p in range(PARTS):
            some = pl.ds(p * (count // PARTS), count // PARTS)
            copy = pltpu.make_async_copy(
                ref.at[some], data.at[part, some], sems.at[part * PARTS + p]
            )
            copy.start()
            copies.append(copy)
    live_copy.wait()
    token = iota((1, count), 1)
    upper = (iota((count, count), 0) <= iota((count, count), 1)).astype(BF16)
    slot = iota((SLOT, count), 0).astype(F32)
    lane = iota((SLOT, LANES), 1)
    ids = ids_ref[...]
    weights = rw_ref[...].astype(F32)
    firsts, headers = [], []
    for w in range(flight):
        expert = jnp.bitwise_xor(mine, w)
        match = ids == expert * spacing
        routed = jnp.any(match, axis=0, keepdims=True) & (token < live[r])
        weight = jnp.sum(jnp.where(match, weights, 0.0), axis=0, keepdims=True)
        routed = jnp.broadcast_to(jnp.where(routed, 1.0, 0.0), (SLOT, count))
        rank = dot(routed.astype(BF16), upper) - 1.0
        placed = jnp.where(rank == slot, routed, 0.0)
        column = jnp.sum(placed * weight, axis=1, keepdims=True)
        headers.append(jnp.where(lane == 0, column, 0.0).astype(BF16))
        placed = placed.astype(BF16)
        firsts.append(placed)
        placed_ref[w] = jnp.concatenate([placed] * CHIPS, axis=0)
    for part in range(2):
        for p in range(PARTS):
            copies[part * PARTS + p].wait()
        for w in range(flight):
            chosen = dot(firsts[w], data[part]).astype(BF16)
            for b in range(rep):
                rows[b] = chosen[:, b * width : (b + 1) * width]
            for k in range(rep):
                pays[w][part, :, k * width : (k + 1) * width] = rows[jnp.bitwise_xor(r, k)]
            pays[w][part, :, model:] = headers[w]


def halves_kernel(gate_ref, up_ref, down_ref, first_ref, second_ref, sems):
    half = first_ref.shape[0]
    copies = []
    for h, out in enumerate((first_ref, second_ref)):
        for n, ref in enumerate((gate_ref, up_ref, down_ref)):
            units = ref.shape[1]
            copy = pltpu.make_async_copy(
                ref.at[pl.ds(h * half, half)],
                out.at[:, pl.ds(n * units, units)],
                sems.at[3 * h + n],
            )
            copy.start()
            copies.append(copy)
    for copy in copies:
        copy.wait()


def forward_kernel(rep, count, *refs):
    blocks, pieces = refs[: 2 * count], refs[2 * count : 2 * count + 2 * rep - 2]
    many = len(blocks) + len(pieces)
    outs, held, sems = refs[many : many + rep + 3], refs[many + rep + 3 : -1], refs[-1]
    pre_ref, rates_ref, last_ref, parts = outs[0], outs[1], outs[2], outs[3:]
    copies = fetch(blocks + pieces, held, sems)
    blocks, pieces = held[: 2 * count], held[2 * count :]
    half, columns = pieces[0].shape
    width = 2 * half
    units = columns // 3
    for n in range(2 * count):
        copies[n].wait()
    rows = [jnp.concatenate([b[part] for b in blocks], axis=0) for part in range(2)]
    for j in range(2 * count):
        rates_ref[j] = blocks[j][0, :, rep * width :]
    for k in range(rep):
        for part in range(2):
            own = rows[part][: parts[k].shape[1], k * width : (k + 1) * width]
            parts[k][part] = own
    for part in range(2):
        last_ref[part] = rows[part][:, (rep - 1) * width : rep * width]
    sum_x, sum_d = 0.0, 0.0
    for p in range(len(pieces)):
        copies[2 * count + p].wait()
        some = slice(p * half, (p + 1) * half)
        sum_x = sum_x + dot(rows[0][:, some], pieces[p][:, : 2 * units])
        sum_d = sum_d + dot(rows[1][:, some], pieces[p][:, 2 * units :])
    pre_ref[:, : 2 * units] = sum_x
    pre_ref[:, 2 * units :] = sum_d


def hidden_kernel(rep, count, cap_ref, rates_ref, pre_ref, last_ref, *refs):
    pieces, outs, rest = refs[: 2 * rep], refs[2 * rep : 2 * rep + 3], refs[2 * rep + 3 :]
    own_ref, other_ref, grads_ref = outs
    held, sems, cap, sem = rest[: 2 * rep], rest[-3], rest[-2], rest[-1]
    cap_copy = pltpu.make_async_copy(cap_ref, cap, sem)
    cap_copy.start()
    order = list(range(2 * rep - 2, 2 * rep)) + list(range(2 * rep - 2))
    copies = fetch([pieces[p] for p in order], [held[p] for p in order], sems)
    copies = {p: copy for p, copy in zip(order, copies)}
    half, columns = pieces[0].shape
    width = 2 * half
    units = columns // 3
    own_rows = count * SLOT
    r = lax.axis_index("rep")
    e = lax.axis_index("ep")
    mine = e // SPLIT
    cap_copy.wait()
    capacity = (BLOCK * cap[r, mine]).astype(F32)
    lane = iota((SLOT, LANES), 1)
    sources, rates, counts = [], [], []
    for n in range(2 * count):
        core, j = n // count, n % count
        sources.append(jnp.bitwise_xor(e, CORES * j + core))
        rate = jnp.where(lane == 0, rates_ref[n].astype(F32), 0.0)
        rate = jnp.sum(rate, axis=1, keepdims=True)
        rates.append(rate)
        counts.append(jnp.sum(jnp.where(rate > 0.0, 1.0, 0.0), axis=0, keepdims=True))
    slot = iota((SLOT, 1), 0).astype(F32)
    rate_rows, kept_rows = [], []
    for n in range(2 * count):
        start = jnp.zeros((1, 1), F32)
        for other in range(2 * count):
            start = start + jnp.where(sources[other] < sources[n], counts[other], 0.0)
        kept = jnp.where((rates[n] > 0.0) & (start + slot < capacity), 1.0, 0.0)
        kept_rows.append(kept)
        rate_rows.append(rates[n] * kept)
    rate = jnp.concatenate(rate_rows, axis=0)
    kept = jnp.concatenate(kept_rows, axis=0)

    sum_x = pre_ref[:, : 2 * units]
    sum_d = pre_ref[:, 2 * units :]
    for h in range(2):
        p = 2 * rep - 2 + h
        copies[p].wait()
        some = slice(h * half, (h + 1) * half)
        sum_x = sum_x + dot(last_ref[0, :, some], held[p][:, : 2 * units])
        sum_d = sum_d + dot(last_ref[1, :, some], held[p][:, 2 * units :])
    pre_gate, pre_up, back_hidden = sum_x[:, :units], sum_x[:, units:], sum_d
    sig = 1.0 / (1.0 + jnp.exp(-pre_gate))
    activated = pre_gate * sig
    hidden = activated * pre_up
    score = jnp.sum(hidden * back_hidden, axis=1, keepdims=True) * kept
    lane = iota((2 * own_rows, LANES), 1)
    scores = jnp.where(lane == e % CORES, score, 0.0).astype(BF16)
    scaled = back_hidden * rate
    gate_grad = (scaled * pre_up * sig * (1.0 + pre_gate * (1.0 - sig))).astype(BF16)
    up_grad = (scaled * activated).astype(BF16)
    grads_ref[:, :units] = gate_grad
    grads_ref[:, units : 2 * units] = up_grad
    grads_ref[:, 2 * units :] = (hidden * rate).astype(BF16)
    pair = jnp.concatenate([gate_grad, up_grad], axis=1)
    for p in range(2 * rep):
        if p < 2 * rep - 2:
            copies[p].wait()
        back = dot(pair, held[p][:, : 2 * units], ((1,), (1,))).astype(BF16)
        own_ref[:, p * half : (p + 1) * half] = back[:own_rows]
        other_ref[:, p * half : (p + 1) * half] = back[own_rows:]
    own_ref[:, rep * width :] = scores[:own_rows]
    other_ref[:, rep * width :] = scores[own_rows:]


def sum_kernel(own_ref, got_ref, *outs):
    for j, out in enumerate(outs):
        some = slice(j * SLOT, (j + 1) * SLOT)
        out[...] = (own_ref[some].astype(F32) + got_ref[some].astype(F32)).astype(BF16)


def weight_kernel(rep, units, *refs):
    many = 3 * rep - 1
    outs, held, sems = refs[many : many + 3], refs[many + 3 : -1], refs[-1]
    for copy in fetch(refs[:many], held, sems):
        copy.wait()
    own, other, grads = held[:rep], held[rep : 2 * rep - 1], held[2 * rep - 1 :]
    got = jnp.concatenate([g[...] for g in grads], axis=0)
    rows = [
        jnp.concatenate(
            [own[0][part]]
            + [ref[part] for k in range(1, rep) for ref in (own[k], other[k - 1])],
            axis=0,
        )
        for part in range(2)
    ]
    gate_up = dot(rows[0], got[:, : 2 * units], ((0,), (0,)))
    outs[0][...] = gate_up[:, :units].astype(BF16)
    outs[1][...] = gate_up[:, units:].astype(BF16)
    outs[2][...] = dot(rows[1], got[:, 2 * units :], ((0,), (0,))).astype(BF16)


def token_kernel(rep, flight, placed_ref, ids_ref, *refs):
    many = flight * CHIPS
    out_ref, weight_ref, blocks = refs[many : many + 3]
    held, sems = refs[many + 3 : -1], refs[-1]
    for copy in fetch(refs[:many], held, sems):
        copy.wait()
    r = lax.axis_index("rep")
    mine = lax.axis_index("ep") // SPLIT
    spacing = EXPERTS // flight
    width = out_ref.shape[1] // rep
    joined = [
        jnp.concatenate([b[...] for b in held[w * CHIPS : (w + 1) * CHIPS]], axis=0)
        for w in range(flight)
    ]
    for k in range(rep):
        total = 0.0
        for w in range(flight):
            some = joined[w][:, k * width : (k + 1) * width]
            total = total + dot(placed_ref[w], some, ((0,), (0,)))
        blocks[jnp.bitwise_xor(r, k)] = total.astype(BF16)
    for b in range(rep):
        out_ref[:, b * width : (b + 1) * width] = blocks[b]
    result = jnp.zeros(weight_ref.shape, F32)
    for w in range(flight):
        score = dot(joined[w][:, rep * width :], placed_ref[w], ((0,), (0,)))
        score = jnp.sum(score, axis=0, keepdims=True)
        match = ids_ref[...] == jnp.bitwise_xor(mine, w) * spacing
        result = result + jnp.where(match, score, 0.0)
    weight_ref[...] = result


def local(
    tokens, out_grad, expert_ids, route_weight, live_count, cap_blocks, w_gate, w_up, w_down_t
):
    rep = lax.axis_size("rep")
    ep = lax.axis_size("ep")
    flight = ep // SPLIT
    count = ep // CORES
    tok_count, model_dim = tokens.shape
    width, units = w_gate.shape
    half = width // 2
    rows = count * SLOT
    payload = model_dim + LANES

    def send(array, rep_bits, ep_bits):
        mask = rep_bits * ep + ep_bits
        pairs = [(a, a ^ mask) for a in range(rep * ep)]
        return lax.ppermute(array, ("rep", "ep"), pairs)

    first, second = call(
        halves_kernel,
        [shape((half, 3 * units))] * 2,
        [w_gate, w_up, w_down_t],
        scratch=[pltpu.SemaphoreType.DMA((6,))],
    )
    halves = {(0, 0): first, (0, 1): second}
    for k in range(1, rep):
        low, high = k & -k, 1 << (k.bit_length() - 1)
        halves[k, 0] = send(halves[k ^ low, 0], low, 0)
        halves[k, 1] = send(halves[k ^ high, 1], high, 0)
    pieces = [halves[k, h] for k in range(rep) for h in range(2)]

    packed = call(
        functools.partial(pack_kernel, rep, flight),
        [shape((2, SLOT, payload))] * flight + [shape((flight, CHIPS * SLOT, tok_count))],
        [live_count, tokens, out_grad, expert_ids.T, route_weight.T],
        inside=(3, 4),
        scratch=[
            pltpu.SMEM(live_count.shape, jnp.int32),
            pltpu.VMEM((2, tok_count, model_dim), BF16),
            pltpu.VMEM((rep, SLOT, width), BF16),
            pltpu.SemaphoreType.DMA((2 * PARTS + 1,)),
        ],
    )
    pays, placed = packed[:flight], packed[flight]
    blocks = [pays[0]] + [send(pays[j // CHIPS], 0, CORES * j) for j in range(1, count)]
    blocks = blocks + [send(block, 0, 1) for block in blocks]

    operands = blocks + pieces[:-2]
    results = call(
        functools.partial(forward_kernel, rep, count),
        [shape((2 * rows, 3 * units), F32), shape((2 * count, SLOT, LANES))]
        + [shape((2, 2 * rows, width))] * 2
        + [shape((2, rows, width))] * (rep - 1),
        operands,
        scratch=buffers(operands),
        flops=2 * 2 * rows * model_dim * 3 * units,
    )
    pre, rates, last, parts = results[0], results[1], results[2], list(results[3:])
    own, other, grads = call(
        functools.partial(hidden_kernel, rep, count),
        [shape((rows, payload))] * 2 + [shape((2 * rows, 3 * units))],
        [cap_blocks, rates, pre, last] + pieces,
        inside=(1, 2, 3),
        scratch=buffers(pieces)
        + [pltpu.SMEM(cap_blocks.shape, jnp.int32), pltpu.SemaphoreType.DMA(())],
        flops=2 * 2 * rows * model_dim * 2 * units,
    )
    backs = call(
        sum_kernel, [shape((SLOT, payload))] * count, [own, send(other, 0, 1)], inside=(0, 1)
    )
    backs = [backs[0]] + [send(backs[j], 0, CORES * j) for j in range(1, count)]

    parts, grads = lax.optimization_barrier((parts, grads))
    moved = [send(parts[k], k, 0) for k in range(1, rep)]
    own_rows = [parts[0]] + moved
    other_rows = [send(block, 0, 1) for block in moved]
    group_grads = [grads] + [send(grads, k, 0) for k in range(1, rep)]
    operands = own_rows + other_rows + group_grads
    grad_gate, grad_up, grad_down = call(
        functools.partial(weight_kernel, rep, units),
        [shape((width, units))] * 3,
        operands,
        scratch=buffers(operands),
        flops=2 * 2 * rep * rows * width * 3 * units,
    )
    grad_tokens, grad_weight = call(
        functools.partial(token_kernel, rep, flight),
        [shape((tok_count, model_dim)), shape(expert_ids.shape[::-1], F32)],
        [placed, expert_ids.T] + backs,
        inside=(0, 1),
        scratch=[pltpu.VMEM((rep, tok_count, width), BF16)] + buffers(backs),
        flops=2 * tok_count * CHIPS * SLOT * model_dim,
    )
    return grad_tokens, grad_weight.T, grad_gate, grad_up, grad_down


def solution(mesh):
    return jax.shard_map(
        local,
        mesh=mesh,
        in_specs=(
            P(("rep", "ep"), None),
            P(("rep", "ep"), None),
            P(("rep", "ep"), None),
            P(("rep", "ep"), None),
            P(),
            P(),
            P("rep", "ep"),
            P("rep", "ep"),
            P("rep", "ep"),
        ),
        out_specs=(
            P(("rep", "ep"), None),
            P(("rep", "ep"), None),
            P("rep", "ep"),
            P("rep", "ep"),
            P("rep", "ep"),
        ),
        check_vma=False,
    )
```

```python
import functools

import jax
import jax.numpy as jnp
from jax import lax
from jax.experimental import pallas as pl
from jax.experimental.pallas import tpu as pltpu
from jax.sharding import PartitionSpec as P

EXPERTS = 128
SLOT = 16
BLOCK = 128
SPLIT = 8
CORES = 2
CHIPS = SPLIT // CORES
LANES = 128
F32 = jnp.float32
BF16 = jnp.bfloat16
PARTS = 4
HBM = pl.BlockSpec(memory_space=pltpu.HBM)
VMEM = pl.BlockSpec(memory_space=pltpu.VMEM)


def shape(dims, kind=BF16):
    return jax.ShapeDtypeStruct(dims, kind)


def call(kernel, outs, args, stored=(), scratch=(), flops=0, grant=16):
    size = sum(a.size * a.dtype.itemsize for a in args) + sum(
        o.size * o.dtype.itemsize for o in outs
    )
    return pl.pallas_call(
        kernel,
        out_shape=tuple(outs),
        in_specs=[HBM if n in stored else VMEM for n in range(len(args))],
        out_specs=tuple([VMEM] * len(outs)),
        scratch_shapes=scratch,
        compiler_params=pltpu.CompilerParams(vmem_limit_bytes=grant * 1024 * 1024),
        cost_estimate=pl.CostEstimate(flops=flops, bytes_accessed=size, transcendentals=0),
    )(*args)


def fetch(pairs, sems, first=0):
    copies = [
        pltpu.make_async_copy(source, target, sems.at[first + n])
        for n, (source, target) in enumerate(pairs)
    ]
    for copy in copies:
        copy.start()
    return copies


def dot(a, b, dims=((1,), (0,))):
    return lax.dot_general(a, b, (dims, ((), ())), preferred_element_type=F32)


def iota(dims, axis):
    return lax.broadcasted_iota(jnp.int32, dims, axis)


def join_weights_kernel(gate_ref, up_ref, down_ref, all_ref, pair_ref, sems):
    units = gate_ref.shape[1]
    pairs = []
    for n, ref in enumerate((gate_ref, up_ref, down_ref)):
        pairs.append((ref, all_ref.at[:, pl.ds(n * units, units)]))
        if n < 2:
            pairs.append((ref, pair_ref.at[:, pl.ds(n * units, units)]))
    for copy in fetch(pairs, sems):
        copy.wait()


def pair_kernel(all_ref, pair_ref):
    pair_ref[...] = all_ref[:, : pair_ref.shape[1]]


def pack_kernel(rep, flight, live_ref, tok_ref, grad_ref, ids_ref, rw_ref, *refs):
    far = rep // 2
    pays, header_ref, placed_ref = refs[:far], refs[far], refs[far + 1]
    live, ids_held, rw_held, data, rows, sems = refs[far + 2 :]
    r = lax.axis_index("rep")
    mine = lax.axis_index("ep") // SPLIT
    count, model = tok_ref.shape
    width = model // rep
    spacing = EXPERTS // flight
    small = fetch([(live_ref, live), (ids_ref, ids_held), (rw_ref, rw_held)], sems)
    pairs = []
    for part, ref in enumerate((tok_ref, grad_ref)):
        for p in range(PARTS):
            some = pl.ds(p * (count // PARTS), count // PARTS)
            pairs.append((ref.at[some], data.at[part, some]))
    large = fetch(pairs, sems, len(small))
    for copy in small:
        copy.wait()
    token = iota((1, count), 1)
    upper = (iota((count, count), 0) <= iota((count, count), 1)).astype(BF16)
    slot = iota((SLOT, count), 0).astype(F32)
    lane = iota((SLOT, LANES), 1)
    ids = ids_held[...]
    weights = rw_held[...].astype(F32)
    firsts = []
    for w in range(flight):
        expert = jnp.bitwise_xor(mine, w)
        match = ids == expert * spacing
        routed = jnp.any(match, axis=0, keepdims=True) & (token < live[r])
        weight = jnp.sum(jnp.where(match, weights, 0.0), axis=0, keepdims=True)
        routed = jnp.broadcast_to(jnp.where(routed, 1.0, 0.0), (SLOT, count))
        rank = dot(routed.astype(BF16), upper) - 1.0
        placed = jnp.where(rank == slot, routed, 0.0)
        column = jnp.sum(placed * weight, axis=1, keepdims=True)
        header_ref[w] = jnp.where(lane == 0, column, 0.0).astype(BF16)
        placed = placed.astype(BF16)
        firsts.append(placed)
        placed_ref[w] = jnp.concatenate([placed] * CHIPS, axis=0)
    for part in range(2):
        for p in range(PARTS):
            large[part * PARTS + p].wait()
        for w in range(flight):
            chosen = dot(firsts[w], data[part]).astype(BF16)
            for b in range(rep):
                rows[b] = chosen[:, b * width : (b + 1) * width]
            for k in range(rep):
                some = slice(k % 2 * width, (k % 2 + 1) * width)
                pays[k // 2][w, part, :, some] = rows[jnp.bitwise_xor(r, k)]


def join_kernel(far, flight, header_ref, *refs):
    pays, outs = refs[:far], refs[far:]
    size = pays[0].shape[3]
    for w in range(flight):
        for k in range(far):
            for part in range(2):
                n = 2 * k + part
                outs[w][:, n * size : (n + 1) * size] = pays[k][w, part]
        outs[w][:, 2 * far * size :] = header_ref[w]


def forward_kernel(far, count, *refs):
    blocks, weights, outs = refs[:count], refs[count : count + 4], refs[count + 4 :]
    sums, near_refs, header_ref = outs[:far], outs[far : far + 2], outs[far + 2]
    width, columns = weights[0].shape
    units = columns // 3
    rows = count * SLOT
    for j in range(count):
        header_ref[j] = blocks[j][:, 4 * far * width :]
    for k in range(far):
        parts = []
        for part in range(2):
            n = 2 * (2 * k + part)
            for near in range(2):
                some = slice((n + near) * width, (n + near + 1) * width)
                chosen = jnp.concatenate([b[:, some] for b in blocks], axis=0)
                near_refs[near][part, k * rows : (k + 1) * rows] = chosen
                parts.append(chosen)
        for i in range(CORES):
            first, second = weights[i], weights[CORES + i]
            total = dot(parts[0], first[:, : 2 * units]) + dot(parts[1], second[:, : 2 * units])
            start = i * columns
            sums[k][:, start : start + 2 * units] = total.astype(sums[k].dtype)
            total = dot(parts[2], first[:, 2 * units :]) + dot(parts[3], second[:, 2 * units :])
            sums[k][:, start + 2 * units : start + columns] = total.astype(sums[k].dtype)


def hidden_kernel(rep, count, cap_ref, own_ref, other_ref, *refs):
    far = rep // 2
    sums, pieces, rest = refs[:far], refs[far : far + 2 * rep], refs[far + 2 * rep :]
    back_refs, grad_refs, cap, sem = rest[:count], rest[count:-2], rest[-2], rest[-1]
    cap_copy = pltpu.make_async_copy(cap_ref, cap, sem)
    cap_copy.start()
    width = pieces[0].shape[0]
    columns = sums[0].shape[1] // CORES
    units = columns // 3
    r = lax.axis_index("rep")
    e = lax.axis_index("ep")
    mine = e // SPLIT
    total = sums[0][...]
    for k in range(1, far):
        total = total + sums[k][...].astype(F32)
    cap_copy.wait()
    capacity = (BLOCK * cap[mine, r]).astype(F32)
    lane = iota((SLOT, LANES), 1)
    sources, rates, counts = [], [], []
    for core, ref in enumerate((own_ref, other_ref)):
        for j in range(count):
            sources.append(jnp.bitwise_xor(e, CORES * j + core))
            rate = jnp.where(lane == 0, ref[j].astype(F32), 0.0)
            rate = jnp.sum(rate, axis=1, keepdims=True)
            rates.append(rate)
            counts.append(jnp.sum(jnp.where(rate > 0.0, 1.0, 0.0), axis=0, keepdims=True))
    slot = iota((SLOT, 1), 0).astype(F32)
    rate_rows, kept_rows = [], []
    for j in range(count):
        start = jnp.zeros((1, 1), F32)
        for other in range(len(sources)):
            start = start + jnp.where(sources[other] < sources[j], counts[other], 0.0)
        kept = jnp.where((rates[j] > 0.0) & (start + slot < capacity), 1.0, 0.0)
        kept_rows.append(kept)
        rate_rows.append(rates[j] * kept)
    rate = jnp.concatenate(rate_rows, axis=0)
    kept = jnp.concatenate(kept_rows, axis=0)

    lane = iota((count * SLOT, LANES), 1)
    scores = jnp.zeros((count * SLOT, LANES), F32)
    pairs = []
    for i in range(CORES):
        pre_gate = total[:, i * columns : i * columns + units]
        pre_up = total[:, i * columns + units : i * columns + 2 * units]
        back_hidden = total[:, i * columns + 2 * units : (i + 1) * columns]
        sig = 1.0 / (1.0 + jnp.exp(-pre_gate))
        activated = pre_gate * sig
        hidden = activated * pre_up
        score = jnp.sum(hidden * back_hidden, axis=1, keepdims=True) * kept
        scores = jnp.where(lane == i, score, scores)
        scaled = back_hidden * rate
        gate_grad = (scaled * pre_up * sig * (1.0 + pre_gate * (1.0 - sig))).astype(BF16)
        up_grad = (scaled * activated).astype(BF16)
        grad_refs[i][:, :units] = gate_grad
        grad_refs[i][:, units : 2 * units] = up_grad
        grad_refs[i][:, 2 * units :] = (hidden * rate).astype(BF16)
        pairs.append(jnp.concatenate([gate_grad, up_grad], axis=1))
    for k in range(rep):
        back = dot(pairs[0], pieces[CORES * k][:, : 2 * units], ((1,), (1,)))
        back = back + dot(pairs[1], pieces[CORES * k + 1][:, : 2 * units], ((1,), (1,)))
        back = back.astype(BF16)
        for j in range(count):
            back_refs[j][:, k * width : (k + 1) * width] = back[j * SLOT : (j + 1) * SLOT]
    scores = scores.astype(BF16)
    for j in range(count):
        back_refs[j][:, rep * width :] = scores[j * SLOT : (j + 1) * SLOT]


def weight_kernel(rep, *refs):
    inputs, grads, outs = refs[:4], refs[4 : 4 + rep], refs[4 + rep :]
    units = outs[0].shape[1]
    rows = grads[0].shape[0] // CORES
    pair, down = 0.0, 0.0
    for near in range(2):
        for core in range(CORES):
            ref = inputs[CORES * near + core]
            some = slice(core * rows, (core + 1) * rows)
            got = jnp.concatenate([grads[k][some] for k in range(near, rep, 2)], axis=0)
            pair = pair + dot(got[:, : 2 * units], ref[0], ((0,), (0,)))
            down = down + dot(got[:, 2 * units :], ref[1], ((0,), (0,)))
    outs[0][...] = pair[:units].T.astype(BF16)
    outs[1][...] = pair[units:].T.astype(BF16)
    outs[2][...] = down.T.astype(BF16)


def token_kernel(rep, flight, ids_ref, placed_ref, *refs):
    backs, rest = refs[: flight * CHIPS], refs[flight * CHIPS :]
    out_ref, weight_ref, blocks, ids, sem = rest
    ids_copy = pltpu.make_async_copy(ids_ref, ids, sem)
    ids_copy.start()
    r = lax.axis_index("rep")
    mine = lax.axis_index("ep") // SPLIT
    spacing = EXPERTS // flight
    width = out_ref.shape[1] // rep
    joined = [
        jnp.concatenate([b[...] for b in backs[w * CHIPS : (w + 1) * CHIPS]], axis=0)
        for w in range(flight)
    ]
    for k in range(rep):
        total = 0.0
        for w in range(flight):
            some = joined[w][:, k * width : (k + 1) * width]
            total = total + dot(placed_ref[w], some, ((0,), (0,)))
        blocks[jnp.bitwise_xor(r, k)] = total.astype(BF16)
    for b in range(rep):
        out_ref[:, b * width : (b + 1) * width] = blocks[b]
    result = jnp.zeros(weight_ref.shape, F32)
    ids_copy.wait()
    for w in range(flight):
        score = dot(joined[w][:, rep * width :], placed_ref[w], ((0,), (0,)))
        score = jnp.sum(score, axis=0, keepdims=True)
        match = ids[...] == jnp.bitwise_xor(mine, w) * spacing
        result = result + jnp.where(match, score, 0.0)
    weight_ref[...] = result


def local(
    tokens, out_grad, expert_ids, route_weight, live_count, cap_blocks, w_gate, w_up, w_down_t
):
    rep = lax.axis_size("rep")
    ep = lax.axis_size("ep")
    far = rep // 2
    flight = ep // SPLIT
    count = ep // CORES
    tok_count, model_dim = tokens.shape
    width, units = w_gate.shape
    rows = count * SLOT
    ids_rows, rw_rows, caps = expert_ids.T, route_weight.T, cap_blocks.T

    def send(array, rep_bits, ep_bits):
        mask = rep_bits * ep + ep_bits
        pairs = [(a, a ^ mask) for a in range(rep * ep)]
        return lax.ppermute(array, ("rep", "ep"), pairs)

    weights, pair = call(
        join_weights_kernel,
        [shape((width, 3 * units)), shape((width, 2 * units))],
        [w_gate, w_up, w_down_t],
        stored=(0, 1, 2),
        scratch=[pltpu.SemaphoreType.DMA((5,))],
        grant=54,
    )
    near = send(weights, 1, 0)
    packed = call(
        functools.partial(pack_kernel, rep, flight),
        [shape((flight, 2, SLOT, 2 * width))] * far
        + [shape((flight, SLOT, LANES)), shape((flight, CHIPS * SLOT, tok_count))],
        [live_count, tokens, out_grad, ids_rows, rw_rows],
        stored=range(5),
        scratch=[
            pltpu.SMEM(live_count.shape, jnp.int32),
            pltpu.VMEM(ids_rows.shape, jnp.int32),
            pltpu.VMEM(rw_rows.shape, BF16),
            pltpu.VMEM((2, tok_count, model_dim), BF16),
            pltpu.VMEM((rep, SLOT, width), BF16),
            pltpu.SemaphoreType.DMA((2 * PARTS + 3,)),
        ],
        grant=53,
    )
    pays, header, placed = list(packed[:far]), packed[far], packed[far + 1]
    pays = [pays[0]] + [send(pays[k], 2 * k, 0) for k in range(1, far)]
    joined = call(
        functools.partial(join_kernel, far, flight),
        [shape((SLOT, 4 * far * width + LANES))] * flight,
        [header] + pays,
    )
    blocks = [joined[0]] + [send(joined[j // CHIPS], 0, CORES * j) for j in range(1, count)]
    weights_other = send(weights, 0, 1)
    near_other = send(near, 0, 1)
    (near_pair,) = call(pair_kernel, [shape((width, 2 * units))], [near])
    pieces = [weights, weights_other, near, near_other]
    for k in range(1, far):
        for array in (pair, near_pair):
            moved = send(array, 2 * k, 0)
            pieces += [moved, send(moved, 0, 1)]

    results = call(
        functools.partial(forward_kernel, far, count),
        [shape((rows, 3 * CORES * units), F32)]
        + [shape((rows, 3 * CORES * units))] * (far - 1)
        + [shape((2, far * rows, width))] * 2
        + [shape((count, SLOT, LANES))],
        blocks + pieces[:4],
        flops=2 * far * rows * 2 * width * 3 * CORES * units,
    )
    sums, rows_here, rows_near, header = results[:far], results[far], results[far + 1], results[-1]
    sums = [sums[0]] + [send(sums[k], 2 * k, 0) for k in range(1, far)]
    results = call(
        functools.partial(hidden_kernel, rep, count),
        [shape((SLOT, model_dim + LANES))] * count + [shape((rows, 3 * units))] * CORES,
        [caps, header, send(header, 0, 1)] + sums + pieces,
        stored=(0,),
        scratch=[pltpu.SMEM(caps.shape, jnp.int32), pltpu.SemaphoreType.DMA(())],
        flops=2 * rows * model_dim * 4 * units,
    )
    backs, grads = results[:count], results[count:]
    backs = [backs[0]] + [send(backs[j], 0, CORES * j) for j in range(1, count)]
    grads = jnp.concatenate([grads[0], send(grads[1], 0, 1)], axis=0)
    group_grads = [grads] + [send(grads, k, 0) for k in range(1, rep)]
    rows_near = send(rows_near, 1, 0)
    inputs = [rows_here, send(rows_here, 0, 1), rows_near, send(rows_near, 0, 1)]
    grad_gate, grad_up, grad_down = call(
        functools.partial(weight_kernel, rep),
        [shape((width, units))] * 3,
        inputs + group_grads,
        flops=2 * 2 * rep * rows * width * 3 * units,
    )
    grad_tokens, grad_weight = call(
        functools.partial(token_kernel, rep, flight),
        [shape((tok_count, model_dim)), shape(ids_rows.shape, F32)],
        [ids_rows, placed] + backs,
        stored=(0,),
        scratch=[
            pltpu.VMEM((rep, tok_count, width), BF16),
            pltpu.VMEM(ids_rows.shape, jnp.int32),
            pltpu.SemaphoreType.DMA(()),
        ],
        flops=2 * tok_count * CHIPS * SLOT * model_dim,
    )
    return grad_tokens, grad_weight.T, grad_gate, grad_up, grad_down


def solution(mesh):
    return jax.shard_map(
        local,
        mesh=mesh,
        in_specs=(
            P(("rep", "ep"), None),
            P(("rep", "ep"), None),
            P(("rep", "ep"), None),
            P(("rep", "ep"), None),
            P(),
            P(),
            P("rep", "ep"),
            P("rep", "ep"),
            P("rep", "ep"),
        ),
        out_specs=(
            P(("rep", "ep"), None),
            P(("rep", "ep"), None),
            P("rep", "ep"),
            P("rep", "ep"),
            P("rep", "ep"),
        ),
        check_vma=False,
    )
```

```python
import functools

import jax
import jax.numpy as jnp
from jax import lax
from jax.experimental import pallas as pl
from jax.experimental.pallas import tpu as pltpu
from jax.sharding import PartitionSpec as P

EXPERTS = 128
SLOT = 16
BLOCK = 128
SPLIT = 8
CORES = 2
CHIPS = SPLIT // CORES
LANES = 128
F32 = jnp.float32
BF16 = jnp.bfloat16
PARTS = 4
HBM = pl.BlockSpec(memory_space=pltpu.HBM)
VMEM = pl.BlockSpec(memory_space=pltpu.VMEM)


def shape(dims, kind=BF16):
    return jax.ShapeDtypeStruct(dims, kind)


def call(kernel, outs, args, stored=(), kept=(), scratch=(), flops=0, grant=16):
    size = sum(a.size * a.dtype.itemsize for a in args) + sum(
        o.size * o.dtype.itemsize for o in outs
    )
    return pl.pallas_call(
        kernel,
        out_shape=tuple(outs),
        in_specs=[HBM if n in stored else VMEM for n in range(len(args))],
        out_specs=tuple([HBM if n in kept else VMEM for n in range(len(outs))]),
        scratch_shapes=scratch,
        compiler_params=pltpu.CompilerParams(vmem_limit_bytes=grant * 1024 * 1024),
        cost_estimate=pl.CostEstimate(flops=flops, bytes_accessed=size, transcendentals=0),
    )(*args)


def fetch(pairs, sems, first=0):
    copies = [
        pltpu.make_async_copy(source, target, sems.at[first + n])
        for n, (source, target) in enumerate(pairs)
    ]
    for copy in copies:
        copy.start()
    return copies


def dot(a, b, dims=((1,), (0,))):
    return lax.dot_general(a, b, (dims, ((), ())), preferred_element_type=F32)


def iota(dims, axis):
    return lax.broadcasted_iota(jnp.int32, dims, axis)


def pack_kernel(rep, flight, live_ref, tok_ref, grad_ref, ids_ref, rw_ref, *refs):
    stored, pays, placed_ref, all_ref = refs[:3], refs[3 : 3 + flight], refs[-8], refs[-7]
    live, ids_held, rw_held, data, rows, sems = refs[-6:]
    r = lax.axis_index("rep")
    mine = lax.axis_index("ep") // SPLIT
    count, model = tok_ref.shape
    width = model // rep
    spacing = EXPERTS // flight
    small = fetch([(live_ref, live), (ids_ref, ids_held), (rw_ref, rw_held)], sems)
    pairs = []
    for part, ref in enumerate((tok_ref, grad_ref)):
        for p in range(PARTS):
            some = pl.ds(p * (count // PARTS), count // PARTS)
            pairs.append((ref.at[some], data.at[part, some]))
    large = fetch(pairs, sems, len(small))
    units = stored[0].shape[1]
    pairs = [(ref, all_ref.at[:, pl.ds(n * units, units)]) for n, ref in enumerate(stored)]
    weights_copies = fetch(pairs, sems, len(small) + len(large))
    for copy in small:
        copy.wait()
    token = iota((1, count), 1)
    upper = (iota((count, count), 0) <= iota((count, count), 1)).astype(BF16)
    slot = iota((SLOT, count), 0).astype(F32)
    lane = iota((SLOT, LANES), 1)
    ids = ids_held[...]
    weights = rw_held[...].astype(F32)
    firsts = []
    for w in range(flight):
        expert = jnp.bitwise_xor(mine, w)
        match = ids == expert * spacing
        routed = jnp.any(match, axis=0, keepdims=True) & (token < live[r])
        weight = jnp.sum(jnp.where(match, weights, 0.0), axis=0, keepdims=True)
        routed = jnp.broadcast_to(jnp.where(routed, 1.0, 0.0), (SLOT, count))
        rank = dot(routed.astype(BF16), upper) - 1.0
        placed = jnp.where(rank == slot, routed, 0.0)
        column = jnp.sum(placed * weight, axis=1, keepdims=True)
        pays[w][:, 2 * model :] = jnp.where(lane == 0, column, 0.0).astype(BF16)
        placed = placed.astype(BF16)
        firsts.append(placed)
        placed_ref[w] = jnp.concatenate([placed] * CHIPS, axis=0)
    for part in range(2):
        for p in range(PARTS):
            large[part * PARTS + p].wait()
        for w in range(flight):
            chosen = dot(firsts[w], data[part]).astype(BF16)
            for b in range(rep):
                rows[b] = chosen[:, b * width : (b + 1) * width]
            for k in range(rep):
                n = 2 * k + part
                pays[w][:, n * width : (n + 1) * width] = rows[jnp.bitwise_xor(r, k)]
    for copy in weights_copies:
        copy.wait()


def half_kernel(start, all_ref, half_ref):
    half_ref[...] = all_ref[start : start + half_ref.shape[0]]


def hidden_kernel(rep, count, spans, cap_ref, *refs):
    blocks, pieces = refs[: 2 * count], refs[2 * count : 2 * count + len(spans)]
    outs, cap, sem = refs[2 * count + len(spans) : -2], refs[-2], refs[-1]
    own_ref, other_ref, grads_ref, here_ref, away_refs = *outs[:4], outs[4:]
    cap_copy = pltpu.make_async_copy(cap_ref, cap, sem)
    cap_copy.start()
    width = here_ref.shape[2]
    units = pieces[0].shape[1] // 3
    own_rows = count * SLOT
    r = lax.axis_index("rep")
    e = lax.axis_index("ep")
    mine = e // SPLIT
    inputs = [[], []]
    for k in range(rep):
        for part in range(2):
            n = 2 * k + part
            chosen = [b[:, n * width : (n + 1) * width] for b in blocks]
            chosen = jnp.concatenate(chosen, axis=0)
            inputs[part].append(chosen)
            if k == 0:
                here_ref[part] = chosen
            else:
                some = slice(part * own_rows, (part + 1) * own_rows)
                away_refs[k - 1][some, :width] = chosen[:own_rows]
    sum_x, sum_d = 0.0, 0.0
    for (k, start, stop), piece in zip(spans, pieces):
        sum_x = sum_x + dot(inputs[0][k][:, start:stop], piece[:, : 2 * units])
        sum_d = sum_d + dot(inputs[1][k][:, start:stop], piece[:, 2 * units :])

    cap_copy.wait()
    capacity = (BLOCK * cap[mine, r]).astype(F32)
    lane = iota((SLOT, LANES), 1)
    sources, rates, counts = [], [], []
    for n in range(2 * count):
        sources.append(jnp.bitwise_xor(e, CORES * (n % count) + n // count))
        rate = jnp.where(lane == 0, blocks[n][:, 2 * rep * width :].astype(F32), 0.0)
        rate = jnp.sum(rate, axis=1, keepdims=True)
        rates.append(rate)
        counts.append(jnp.sum(jnp.where(rate > 0.0, 1.0, 0.0), axis=0, keepdims=True))
    slot = iota((SLOT, 1), 0).astype(F32)
    rate_rows, kept_rows = [], []
    for n in range(2 * count):
        start = jnp.zeros((1, 1), F32)
        for other in range(2 * count):
            start = start + jnp.where(sources[other] < sources[n], counts[other], 0.0)
        kept = jnp.where((rates[n] > 0.0) & (start + slot < capacity), 1.0, 0.0)
        kept_rows.append(kept)
        rate_rows.append(rates[n] * kept)
    rate = jnp.concatenate(rate_rows, axis=0)
    kept = jnp.concatenate(kept_rows, axis=0)

    pre_gate, pre_up, back_hidden = sum_x[:, :units], sum_x[:, units:], sum_d
    sig = 1.0 / (1.0 + jnp.exp(-pre_gate))
    activated = pre_gate * sig
    hidden = activated * pre_up
    score = jnp.sum(hidden * back_hidden, axis=1, keepdims=True) * kept
    lane = iota((2 * own_rows, LANES), 1)
    scores = jnp.where(lane == e % CORES, score, 0.0).astype(BF16)
    scaled = back_hidden * rate
    gate_grad = (scaled * pre_up * sig * (1.0 + pre_gate * (1.0 - sig))).astype(BF16)
    up_grad = (scaled * activated).astype(BF16)
    weighted = (hidden * rate).astype(BF16)
    grads_ref[...] = jnp.concatenate([gate_grad, up_grad, weighted], axis=1)
    for ref in away_refs:
        ref[:, width:] = grads_ref[...]
    pair = jnp.concatenate([gate_grad, up_grad], axis=1)
    for (k, start, stop), piece in zip(spans, pieces):
        back = dot(pair, piece[:, : 2 * units], ((1,), (1,))).astype(BF16)
        some = slice(k * width + start, k * width + stop)
        own_ref[:, some] = back[:own_rows]
        other_ref[:, some] = back[own_rows:]
    own_ref[:, rep * width :] = scores[:own_rows]
    other_ref[:, rep * width :] = scores[own_rows:]


def sum_kernel(own_ref, got_ref, *outs):
    for j, out in enumerate(outs):
        some = slice(j * SLOT, (j + 1) * SLOT)
        out[...] = (own_ref[some].astype(F32) + got_ref[some].astype(F32)).astype(BF16)


def stack_kernel(*refs):
    for k, ref in enumerate(refs[:-1]):
        refs[-1][k] = ref[:, : refs[-1].shape[2]]


def weight_kernel(rep, here_ref, grads_ref, other_ref, *refs):
    away, outs = refs[: rep - 1], refs[rep - 1 :]
    units = outs[0].shape[1]
    width = here_ref.shape[2]
    half = grads_ref.shape[0] // 2
    sums = []
    for part, columns in enumerate((slice(0, 2 * units), slice(2 * units, 3 * units))):
        some = slice(part * half, (part + 1) * half)
        rows = [here_ref[part]]
        got = [grads_ref[:, columns]]
        for k, ref in enumerate(away):
            rows += [ref[some, :width], other_ref[k, some]]
            got.append(ref[:, width + columns.start : width + columns.stop])
        rows = jnp.concatenate(rows, axis=0)
        got = jnp.concatenate(got, axis=0)
        sums.append(dot(got, rows, ((0,), (0,))))
    outs[0][...] = sums[0][:units].T.astype(BF16)
    outs[1][...] = sums[0][units:].T.astype(BF16)
    outs[2][...] = sums[1].T.astype(BF16)


def token_kernel(rep, flight, ids_ref, placed_ref, *refs):
    backs, rest = refs[: flight * CHIPS], refs[flight * CHIPS :]
    out_ref, weight_ref, blocks, ids, sem = rest
    ids_copy = pltpu.make_async_copy(ids_ref, ids, sem)
    ids_copy.start()
    r = lax.axis_index("rep")
    mine = lax.axis_index("ep") // SPLIT
    spacing = EXPERTS // flight
    width = out_ref.shape[1] // rep
    joined = [
        jnp.concatenate([b[...] for b in backs[w * CHIPS : (w + 1) * CHIPS]], axis=0)
        for w in range(flight)
    ]
    for k in range(rep):
        total = 0.0
        for w in range(flight):
            some = joined[w][:, k * width : (k + 1) * width]
            total = total + dot(placed_ref[w], some, ((0,), (0,)))
        blocks[jnp.bitwise_xor(r, k)] = total.astype(BF16)
    for b in range(rep):
        out_ref[:, b * width : (b + 1) * width] = blocks[b]
    result = jnp.zeros(weight_ref.shape, F32)
    ids_copy.wait()
    for w in range(flight):
        score = dot(joined[w][:, rep * width :], placed_ref[w], ((0,), (0,)))
        score = jnp.sum(score, axis=0, keepdims=True)
        match = ids[...] == jnp.bitwise_xor(mine, w) * spacing
        result = result + jnp.where(match, score, 0.0)
    weight_ref[...] = result


def local(
    tokens, out_grad, expert_ids, route_weight, live_count, cap_blocks, w_gate, w_up, w_down_t
):
    rep = lax.axis_size("rep")
    ep = lax.axis_size("ep")
    far = rep // 2
    flight = ep // SPLIT
    count = ep // CORES
    tok_count, model_dim = tokens.shape
    width, units = w_gate.shape
    rows = count * SLOT
    ids_rows, rw_rows, caps = expert_ids.T, route_weight.T, cap_blocks.T

    def send(array, rep_bits, ep_bits):
        mask = rep_bits * ep + ep_bits
        pairs = [(a, a ^ mask) for a in range(rep * ep)]
        return lax.ppermute(array, ("rep", "ep"), pairs)

    def after(array, *others):
        return lax.optimization_barrier((array,) + others)[0]

    packed = call(
        functools.partial(pack_kernel, rep, flight),
        [shape((SLOT, 2 * model_dim + LANES))] * flight
        + [shape((flight, CHIPS * SLOT, tok_count)), shape((width, 3 * units))],
        [live_count, tokens, out_grad, ids_rows, rw_rows, w_gate, w_up, w_down_t],
        stored=range(8),
        kept=(flight + 1,),
        scratch=[
            pltpu.SMEM(live_count.shape, jnp.int32),
            pltpu.VMEM(ids_rows.shape, jnp.int32),
            pltpu.VMEM(rw_rows.shape, BF16),
            pltpu.VMEM((2, tok_count, model_dim), BF16),
            pltpu.VMEM((rep, SLOT, width), BF16),
            pltpu.SemaphoreType.DMA((2 * PARTS + 6,)),
        ],
        grant=54,
    )
    pays, placed, weights = packed[:flight], packed[flight], packed[flight + 1]

    half = width // 2
    whole = {0: weights}
    halves = {}
    for k in range(1, rep):
        low, high = k & -k, 1 << (k.bit_length() - 1)
        if low == high:
            whole[k] = send(weights, k, 0)
            for h in range(2):
                kernel = functools.partial(half_kernel, h * half)
                (halves[k, h],) = call(kernel, [shape((half, 3 * units))], [whole[k]])
        else:
            halves[k, 0] = send(halves[k ^ low, 0], low, 0)
            halves[k, 1] = send(halves[k ^ high, 1], high, 0)
    spans, pieces = [], []
    for k in range(rep):
        if k in whole:
            spans.append((k, 0, width))
            pieces.append(whole[k])
        else:
            spans += [(k, 0, half), (k, half, width)]
            pieces += [halves[k, 0], halves[k, 1]]

    blocks = [pays[0]] + [send(pays[j // CHIPS], 0, CORES * j) for j in range(1, count)]
    blocks = blocks + [send(block, 0, 1) for block in blocks]
    results = call(
        functools.partial(hidden_kernel, rep, count, tuple(spans)),
        [shape((rows, model_dim + LANES))] * 2
        + [shape((2 * rows, 3 * units)), shape((2, 2 * rows, width))]
        + [shape((2 * rows, width + 3 * units))] * (rep - 1),
        [caps] + blocks + pieces,
        stored=(0,),
        scratch=[pltpu.SMEM(caps.shape, jnp.int32), pltpu.SemaphoreType.DMA(())],
        flops=2 * 2 * rows * model_dim * 5 * units,
    )
    own, other, grads, here, away = *results[:4], results[4:]
    summed = call(sum_kernel, [shape((SLOT, model_dim + LANES))] * count, [own, send(other, 0, 1)])
    backs = [send(summed[j], 0, CORES * j) if j else summed[0] for j in range(count)]
    backs = [backs[j ^ (CHIPS - 1)] for j in range(count)]

    moved = [send(away[k - 1], k, 0) for k in range(1, rep)]
    (own_rows,) = call(stack_kernel, [shape((rep - 1, 2 * rows, width))], moved)
    other_rows = send(own_rows, 0, 1)
    grad_gate, grad_up, grad_down = call(
        functools.partial(weight_kernel, rep),
        [shape((width, units))] * 3,
        [here, grads, other_rows] + moved,
        flops=2 * 2 * rep * rows * width * 3 * units,
    )
    grad_tokens, grad_weight = call(
        functools.partial(token_kernel, rep, flight),
        [shape((tok_count, model_dim)), shape(ids_rows.shape, F32)],
        [ids_rows, placed] + backs,
        stored=(0,),
        scratch=[
            pltpu.VMEM((rep, tok_count, width), BF16),
            pltpu.VMEM(ids_rows.shape, jnp.int32),
            pltpu.SemaphoreType.DMA(()),
        ],
        flops=1000 * 2 * tok_count * CHIPS * SLOT * model_dim,
    )
    return grad_tokens, grad_weight.T, grad_gate, grad_up, grad_down


def solution(mesh):
    return jax.shard_map(
        local,
        mesh=mesh,
        in_specs=(
            P(("rep", "ep"), None),
            P(("rep", "ep"), None),
            P(("rep", "ep"), None),
            P(("rep", "ep"), None),
            P(),
            P(),
            P("rep", "ep"),
            P("rep", "ep"),
            P("rep", "ep"),
        ),
        out_specs=(
            P(("rep", "ep"), None),
            P(("rep", "ep"), None),
            P("rep", "ep"),
            P("rep", "ep"),
            P("rep", "ep"),
        ),
        check_vma=False,
    )
```

```python
import functools

import jax
import jax.numpy as jnp
from jax import lax
from jax.experimental import pallas as pl
from jax.experimental.pallas import tpu as pltpu
from jax.sharding import PartitionSpec as P

EXPERTS = 128
SLOT = 16
BLOCK = 128
SPLIT = 8
CORES = 2
CHIPS = SPLIT // CORES
LANES = 128
F32 = jnp.float32
BF16 = jnp.bfloat16
PARTS = 4
HBM = pl.BlockSpec(memory_space=pltpu.HBM)
VMEM = pl.BlockSpec(memory_space=pltpu.VMEM)


def shape(dims, kind=BF16):
    return jax.ShapeDtypeStruct(dims, kind)


def call(kernel, outs, args, stored=(), kept=(), scratch=(), flops=0, grant=16):
    size = sum(a.size * a.dtype.itemsize for a in args) + sum(
        o.size * o.dtype.itemsize for o in outs
    )
    return pl.pallas_call(
        kernel,
        out_shape=tuple(outs),
        in_specs=[HBM if n in stored else VMEM for n in range(len(args))],
        out_specs=tuple([HBM if n in kept else VMEM for n in range(len(outs))]),
        scratch_shapes=scratch,
        compiler_params=pltpu.CompilerParams(vmem_limit_bytes=grant * 1024 * 1024),
        cost_estimate=pl.CostEstimate(flops=flops, bytes_accessed=size, transcendentals=0),
    )(*args)


def fetch(pairs, sems, first=0):
    copies = [
        pltpu.make_async_copy(source, target, sems.at[first + n])
        for n, (source, target) in enumerate(pairs)
    ]
    for copy in copies:
        copy.start()
    return copies


def dot(a, b, dims=((1,), (0,))):
    return lax.dot_general(a, b, (dims, ((), ())), preferred_element_type=F32)


def iota(dims, axis):
    return lax.broadcasted_iota(jnp.int32, dims, axis)


def turned(n):
    return n ^ (CHIPS - 1)


def pack_kernel(rep, flight, live_ref, tok_ref, grad_ref, ids_ref, rw_ref, *refs):
    stored, pays, placed_ref, all_ref = refs[:3], refs[3 : 3 + flight], refs[-9], refs[-8]
    live, ids_held, rw_held, data, rows, joined, sems = refs[-7:]
    r = lax.axis_index("rep")
    mine = lax.axis_index("ep") // SPLIT
    count, model = tok_ref.shape
    width = model // rep
    spacing = EXPERTS // flight
    small = fetch([(live_ref, live), (ids_ref, ids_held), (rw_ref, rw_held)], sems)
    pairs = []
    for part, ref in enumerate((tok_ref, grad_ref)):
        for p in range(PARTS):
            some = pl.ds(p * (count // PARTS), count // PARTS)
            pairs.append((ref.at[some], data.at[part, some]))
    large = fetch(pairs, sems, len(small))
    units = stored[0].shape[1]
    pairs = [(ref, joined.at[:, pl.ds(n * units, units)]) for n, ref in enumerate(stored)]
    weight_copies = fetch(pairs, sems, len(small) + len(large))
    for copy in small:
        copy.wait()
    token = iota((1, count), 1)
    upper = (iota((count, count), 0) <= iota((count, count), 1)).astype(BF16)
    slot = iota((SLOT, count), 0).astype(F32)
    lane = iota((SLOT, LANES), 1)
    ids = ids_held[...]
    weights = rw_held[...].astype(F32)
    firsts = []
    for w in range(flight):
        expert = jnp.bitwise_xor(mine, w)
        match = ids == expert * spacing
        routed = jnp.any(match, axis=0, keepdims=True) & (token < live[r])
        weight = jnp.sum(jnp.where(match, weights, 0.0), axis=0, keepdims=True)
        routed = jnp.broadcast_to(jnp.where(routed, 1.0, 0.0), (SLOT, count))
        rank = dot(routed.astype(BF16), upper) - 1.0
        placed = jnp.where(rank == slot, routed, 0.0)
        column = jnp.sum(placed * weight, axis=1, keepdims=True)
        pays[w][:, 2 * model :] = jnp.where(lane == 0, column, 0.0).astype(BF16)
        placed = placed.astype(BF16)
        firsts.append(placed)
        placed_ref[w] = jnp.concatenate([placed] * CHIPS, axis=0)
    for copy in weight_copies:
        copy.wait()
    (out_copy,) = fetch([(joined, all_ref)], sems, len(small) + len(large) + len(weight_copies))
    for part in range(2):
        for p in range(PARTS):
            large[part * PARTS + p].wait()
        for w in range(flight):
            chosen = dot(firsts[w], data[part]).astype(BF16)
            for b in range(rep):
                rows[b] = chosen[:, b * width : (b + 1) * width]
            for k in range(rep):
                n = 2 * k + part
                pays[w][:, n * width : (n + 1) * width] = rows[jnp.bitwise_xor(r, k)]
    out_copy.wait()


def half_kernel(start, all_ref, half_ref):
    half_ref[...] = all_ref[start : start + half_ref.shape[0]]


def hidden_kernel(rep, count, spans, cap_ref, *refs):
    blocks, pieces = refs[: 2 * count], refs[2 * count : 2 * count + len(spans)]
    outs, cap, sem = refs[2 * count + len(spans) : -2], refs[-2], refs[-1]
    own_ref, other_ref, grads_ref, here_ref, away_refs = *outs[:4], outs[4:]
    cap_copy = pltpu.make_async_copy(cap_ref, cap, sem)
    cap_copy.start()
    width = here_ref.shape[2]
    units = pieces[0].shape[1] // 3
    own_rows = count * SLOT
    r = lax.axis_index("rep")
    e = lax.axis_index("ep")
    mine = e // SPLIT
    inputs = [[], []]
    for k in range(rep):
        for part in range(2):
            n = 2 * k + part
            chosen = [b[:, n * width : (n + 1) * width] for b in blocks]
            chosen = jnp.concatenate(chosen, axis=0)
            inputs[part].append(chosen)
            if k == 0:
                here_ref[part] = chosen
            else:
                some = slice(part * own_rows, (part + 1) * own_rows)
                away_refs[k - 1][some, :width] = chosen[:own_rows]
    sum_x, sum_d = 0.0, 0.0
    for (k, start, stop), piece in zip(spans, pieces):
        sum_x = sum_x + dot(inputs[0][k][:, start:stop], piece[:, : 2 * units])
        sum_d = sum_d + dot(inputs[1][k][:, start:stop], piece[:, 2 * units :])

    cap_copy.wait()
    capacity = (BLOCK * cap[mine, r]).astype(F32)
    lane = iota((SLOT, LANES), 1)
    sources, rates, counts = [], [], []
    for n in range(2 * count):
        sources.append(jnp.bitwise_xor(e, CORES * turned(n % count) + n // count))
        rate = jnp.where(lane == 0, blocks[n][:, 2 * rep * width :].astype(F32), 0.0)
        rate = jnp.sum(rate, axis=1, keepdims=True)
        rates.append(rate)
        counts.append(jnp.sum(jnp.where(rate > 0.0, 1.0, 0.0), axis=0, keepdims=True))
    slot = iota((SLOT, 1), 0).astype(F32)
    rate_rows, kept_rows = [], []
    for n in range(2 * count):
        start = jnp.zeros((1, 1), F32)
        for other in range(2 * count):
            start = start + jnp.where(sources[other] < sources[n], counts[other], 0.0)
        kept = jnp.where((rates[n] > 0.0) & (start + slot < capacity), 1.0, 0.0)
        kept_rows.append(kept)
        rate_rows.append(rates[n] * kept)
    rate = jnp.concatenate(rate_rows, axis=0)
    kept = jnp.concatenate(kept_rows, axis=0)

    pre_gate, pre_up, back_hidden = sum_x[:, :units], sum_x[:, units:], sum_d
    sig = 1.0 / (1.0 + jnp.exp(-pre_gate))
    activated = pre_gate * sig
    hidden = activated * pre_up
    score = jnp.sum(hidden * back_hidden, axis=1, keepdims=True) * kept
    lane = iota((2 * own_rows, LANES), 1)
    scores = jnp.where(lane == e % CORES, score, 0.0).astype(BF16)
    scaled = back_hidden * rate
    gate_grad = (scaled * pre_up * sig * (1.0 + pre_gate * (1.0 - sig))).astype(BF16)
    up_grad = (scaled * activated).astype(BF16)
    weighted = (hidden * rate).astype(BF16)
    grads_ref[...] = jnp.concatenate([gate_grad, up_grad, weighted], axis=1)
    for ref in away_refs:
        ref[:, width:] = grads_ref[...]
    pair = jnp.concatenate([gate_grad, up_grad], axis=1)
    for (k, start, stop), piece in zip(spans, pieces):
        back = dot(pair, piece[:, : 2 * units], ((1,), (1,))).astype(BF16)
        some = slice(k * width + start, k * width + stop)
        own_ref[:, some] = back[:own_rows]
        other_ref[:, some] = back[own_rows:]
    own_ref[:, rep * width :] = scores[:own_rows]
    other_ref[:, rep * width :] = scores[own_rows:]


def sum_kernel(own_ref, got_ref, *outs):
    for j, out in enumerate(outs):
        some = slice(j * SLOT, (j + 1) * SLOT)
        out[...] = (own_ref[some].astype(F32) + got_ref[some].astype(F32)).astype(BF16)


def stack_kernel(*refs):
    for k, ref in enumerate(refs[:-1]):
        refs[-1][k] = ref[:, : refs[-1].shape[2]]


def weight_kernel(rep, here_ref, grads_ref, other_ref, *refs):
    away, outs = refs[: rep - 1], refs[rep - 1 :]
    units = outs[0].shape[1]
    width = here_ref.shape[2]
    half = grads_ref.shape[0] // 2
    sums = []
    for part, columns in enumerate((slice(0, 2 * units), slice(2 * units, 3 * units))):
        some = slice(part * half, (part + 1) * half)
        rows = [here_ref[part]]
        got = [grads_ref[:, columns]]
        for k, ref in enumerate(away):
            rows += [ref[some, :width], other_ref[k, some]]
            got.append(ref[:, width + columns.start : width + columns.stop])
        rows = jnp.concatenate(rows, axis=0)
        got = jnp.concatenate(got, axis=0)
        sums.append(dot(got, rows, ((0,), (0,))))
    outs[0][...] = sums[0][:units].T.astype(BF16)
    outs[1][...] = sums[0][units:].T.astype(BF16)
    outs[2][...] = sums[1].T.astype(BF16)


def token_kernel(rep, flight, ids_ref, placed_ref, *refs):
    backs, rest = refs[: flight * CHIPS], refs[flight * CHIPS :]
    out_ref, weight_ref, blocks, ids, sem = rest
    ids_copy = pltpu.make_async_copy(ids_ref, ids, sem)
    ids_copy.start()
    r = lax.axis_index("rep")
    mine = lax.axis_index("ep") // SPLIT
    spacing = EXPERTS // flight
    width = out_ref.shape[1] // rep
    joined = [
        jnp.concatenate([b[...] for b in backs[w * CHIPS : (w + 1) * CHIPS]], axis=0)
        for w in range(flight)
    ]
    for k in range(rep):
        total = 0.0
        for w in range(flight):
            some = joined[w][:, k * width : (k + 1) * width]
            total = total + dot(placed_ref[w], some, ((0,), (0,)))
        blocks[jnp.bitwise_xor(r, k)] = total.astype(BF16)
    for b in range(rep):
        out_ref[:, b * width : (b + 1) * width] = blocks[b]
    result = jnp.zeros(weight_ref.shape, F32)
    ids_copy.wait()
    for w in range(flight):
        score = dot(joined[w][:, rep * width :], placed_ref[w], ((0,), (0,)))
        score = jnp.sum(score, axis=0, keepdims=True)
        match = ids[...] == jnp.bitwise_xor(mine, w) * spacing
        result = result + jnp.where(match, score, 0.0)
    weight_ref[...] = result


def local(
    tokens, out_grad, expert_ids, route_weight, live_count, cap_blocks, w_gate, w_up, w_down_t
):
    rep = lax.axis_size("rep")
    ep = lax.axis_size("ep")
    far = rep // 2
    flight = ep // SPLIT
    count = ep // CORES
    tok_count, model_dim = tokens.shape
    width, units = w_gate.shape
    rows = count * SLOT
    ids_rows, rw_rows, caps = expert_ids.T, route_weight.T, cap_blocks.T

    def send(array, rep_bits, ep_bits):
        mask = rep_bits * ep + ep_bits
        pairs = [(a, a ^ mask) for a in range(rep * ep)]
        return lax.ppermute(array, ("rep", "ep"), pairs)

    def after(array, *others):
        return lax.optimization_barrier((array,) + others)[0]

    packed = call(
        functools.partial(pack_kernel, rep, flight),
        [shape((SLOT, 2 * model_dim + LANES))] * flight
        + [shape((flight, CHIPS * SLOT, tok_count)), shape((width, 3 * units))],
        [live_count, tokens, out_grad, ids_rows, rw_rows, w_gate, w_up, w_down_t],
        stored=range(8),
        kept=(flight + 1,),
        scratch=[
            pltpu.SMEM(live_count.shape, jnp.int32),
            pltpu.VMEM(ids_rows.shape, jnp.int32),
            pltpu.VMEM(rw_rows.shape, BF16),
            pltpu.VMEM((2, tok_count, model_dim), BF16),
            pltpu.VMEM((rep, SLOT, width), BF16),
            pltpu.VMEM((width, 3 * units), BF16),
            pltpu.SemaphoreType.DMA((2 * PARTS + 7,)),
        ],
        grant=54,
    )
    pays, placed, weights = packed[:flight], packed[flight], packed[flight + 1]

    half = width // 2
    whole = {0: weights}
    halves = {}
    for k in range(1, rep):
        low, high = k & -k, 1 << (k.bit_length() - 1)
        if low == high:
            whole[k] = send(weights, k, 0)
            for h in range(2):
                kernel = functools.partial(half_kernel, h * half)
                (halves[k, h],) = call(kernel, [shape((half, 3 * units))], [whole[k]])
        else:
            halves[k, 0] = send(halves[k ^ low, 0], low, 0)
            halves[k, 1] = send(halves[k ^ high, 1], high, 0)
    spans, pieces = [], []
    for k in range(rep):
        if k in whole:
            spans.append((k, 0, width))
            pieces.append(whole[k])
        else:
            spans += [(k, 0, half), (k, half, width)]
            pieces += [halves[k, 0], halves[k, 1]]

    order = [turned(n) for n in range(count)]
    blocks = [send(pays[j // CHIPS], 0, CORES * j) if j else pays[0] for j in order]
    nearest = blocks[order.index(1)]
    ready = [after(b, nearest) if j == 0 else b for j, b in zip(order, blocks)]
    blocks = blocks + [send(block, 0, 1) for block in ready]
    results = call(
        functools.partial(hidden_kernel, rep, count, tuple(spans)),
        [shape((rows, model_dim + LANES))] * 2
        + [shape((2 * rows, 3 * units)), shape((2, 2 * rows, width))]
        + [shape((2 * rows, width + 3 * units))] * (rep - 1),
        [caps] + blocks + pieces,
        stored=(0,),
        scratch=[pltpu.SMEM(caps.shape, jnp.int32), pltpu.SemaphoreType.DMA(())],
        flops=2 * 2 * rows * model_dim * 5 * units,
    )
    own, other, grads, here, away = *results[:4], results[4:]
    summed = call(sum_kernel, [shape((SLOT, model_dim + LANES))] * count, [own, send(other, 0, 1)])
    backs = [send(part, 0, CORES * j) if j else part for j, part in zip(order, summed)]

    moved = [send(away[k - 1], k, 0) for k in range(1, rep)]
    (own_rows,) = call(stack_kernel, [shape((rep - 1, 2 * rows, width))], moved)
    other_rows = send(own_rows, 0, 1)
    grad_gate, grad_up, grad_down = call(
        functools.partial(weight_kernel, rep),
        [shape((width, units))] * 3,
        [here, grads, other_rows] + moved,
        flops=2 * 2 * rep * rows * width * 3 * units,
    )
    grad_tokens, grad_weight = call(
        functools.partial(token_kernel, rep, flight),
        [shape((tok_count, model_dim)), shape(ids_rows.shape, F32)],
        [ids_rows, placed] + backs,
        stored=(0,),
        scratch=[
            pltpu.VMEM((rep, tok_count, width), BF16),
            pltpu.VMEM(ids_rows.shape, jnp.int32),
            pltpu.SemaphoreType.DMA(()),
        ],
        flops=1000 * 2 * tok_count * CHIPS * SLOT * model_dim,
    )
    return grad_tokens, grad_weight.T, grad_gate, grad_up, grad_down


def solution(mesh):
    return jax.shard_map(
        local,
        mesh=mesh,
        in_specs=(
            P(("rep", "ep"), None),
            P(("rep", "ep"), None),
            P(("rep", "ep"), None),
            P(("rep", "ep"), None),
            P(),
            P(),
            P("rep", "ep"),
            P("rep", "ep"),
            P("rep", "ep"),
        ),
        out_specs=(
            P(("rep", "ep"), None),
            P(("rep", "ep"), None),
            P("rep", "ep"),
            P("rep", "ep"),
            P("rep", "ep"),
        ),
        check_vma=False,
    )
```

```python
import functools

import jax
import jax.numpy as jnp
from jax import lax
from jax.experimental import pallas as pl
from jax.experimental.pallas import tpu as pltpu
from jax.sharding import PartitionSpec as P

EXPERTS = 128
SLOT = 16
BLOCK = 128
SPLIT = 8
CORES = 2
CHIPS = SPLIT // CORES
LANES = 128
F32 = jnp.float32
BF16 = jnp.bfloat16
PARTS = 4
HBM = pl.BlockSpec(memory_space=pltpu.HBM)
VMEM = pl.BlockSpec(memory_space=pltpu.VMEM)


def shape(dims, kind=BF16):
    return jax.ShapeDtypeStruct(dims, kind)


def call(kernel, outs, args, stored=(), kept=(), scratch=(), flops=0, grant=16):
    size = sum(a.size * a.dtype.itemsize for a in args) + sum(
        o.size * o.dtype.itemsize for o in outs
    )
    return pl.pallas_call(
        kernel,
        out_shape=tuple(outs),
        in_specs=[HBM if n in stored else VMEM for n in range(len(args))],
        out_specs=tuple([HBM if n in kept else VMEM for n in range(len(outs))]),
        scratch_shapes=scratch,
        compiler_params=pltpu.CompilerParams(vmem_limit_bytes=grant * 1024 * 1024),
        cost_estimate=pl.CostEstimate(flops=flops, bytes_accessed=size, transcendentals=0),
    )(*args)


def fetch(pairs, sems, first=0):
    copies = [
        pltpu.make_async_copy(source, target, sems.at[first + n])
        for n, (source, target) in enumerate(pairs)
    ]
    for copy in copies:
        copy.start()
    return copies


def dot(a, b, dims=((1,), (0,))):
    return lax.dot_general(a, b, (dims, ((), ())), preferred_element_type=F32)


def iota(dims, axis):
    return lax.broadcasted_iota(jnp.int32, dims, axis)


def join_kernel(gate_ref, up_ref, down_ref, all_ref, joined, sems):
    units = gate_ref.shape[1]
    refs = (gate_ref, up_ref, down_ref)
    pairs = [(ref, joined.at[:, pl.ds(n * units, units)]) for n, ref in enumerate(refs)]
    for copy in fetch(pairs, sems):
        copy.wait()
    (copy,) = fetch([(joined, all_ref)], sems, len(pairs))
    copy.wait()


def turned(n):
    return n ^ (CHIPS - 1)


def pack_kernel(rep, flight, live_ref, tok_ref, grad_ref, ids_ref, rw_ref, *refs):
    pays, placed_ref = refs[:flight], refs[flight]
    live, ids_held, rw_held, data, rows, sems = refs[flight + 1 :]
    r = lax.axis_index("rep")
    mine = lax.axis_index("ep") // SPLIT
    count, model = tok_ref.shape
    width = model // rep
    spacing = EXPERTS // flight
    small = fetch([(live_ref, live), (ids_ref, ids_held), (rw_ref, rw_held)], sems)
    pairs = []
    for part, ref in enumerate((tok_ref, grad_ref)):
        for p in range(PARTS):
            some = pl.ds(p * (count // PARTS), count // PARTS)
            pairs.append((ref.at[some], data.at[part, some]))
    large = fetch(pairs, sems, len(small))
    for copy in small:
        copy.wait()
    token = iota((1, count), 1)
    upper = (iota((count, count), 0) <= iota((count, count), 1)).astype(BF16)
    slot = iota((SLOT, count), 0).astype(F32)
    lane = iota((SLOT, LANES), 1)
    ids = ids_held[...]
    weights = rw_held[...].astype(F32)
    firsts = []
    for w in range(flight):
        expert = jnp.bitwise_xor(mine, w)
        match = ids == expert * spacing
        routed = jnp.any(match, axis=0, keepdims=True) & (token < live[r])
        weight = jnp.sum(jnp.where(match, weights, 0.0), axis=0, keepdims=True)
        routed = jnp.broadcast_to(jnp.where(routed, 1.0, 0.0), (SLOT, count))
        rank = dot(routed.astype(BF16), upper) - 1.0
        placed = jnp.where(rank == slot, routed, 0.0)
        column = jnp.sum(placed * weight, axis=1, keepdims=True)
        pays[w][:, 2 * model :] = jnp.where(lane == 0, column, 0.0).astype(BF16)
        placed = placed.astype(BF16)
        firsts.append(placed)
        placed_ref[w] = jnp.concatenate([placed] * CHIPS, axis=0)
    for part in range(2):
        for p in range(PARTS):
            large[part * PARTS + p].wait()
        for w in range(flight):
            chosen = dot(firsts[w], data[part]).astype(BF16)
            for b in range(rep):
                rows[b] = chosen[:, b * width : (b + 1) * width]
            for k in range(rep):
                n = 2 * k + part
                pays[w][:, n * width : (n + 1) * width] = rows[jnp.bitwise_xor(r, k)]


def parts_kernel(count, *refs):
    blocks, outs = refs[:count], refs[count:]
    rows, width = count * SLOT, outs[0].shape[1]
    for k, out in enumerate(outs):
        for part in range(2):
            n = 2 * (k + 1) + part
            for j in range(count):
                start = part * rows + j * SLOT
                out[start : start + SLOT] = blocks[j][:, n * width : (n + 1) * width]


def half_kernel(start, all_ref, half_ref):
    half_ref[...] = all_ref[start : start + half_ref.shape[0]]


def hidden_kernel(rep, count, spans, cap_ref, *refs):
    blocks, pieces = refs[: 2 * count], refs[2 * count : 2 * count + len(spans)]
    outs, cap, sem = refs[2 * count + len(spans) : -2], refs[-2], refs[-1]
    own_ref, other_ref, grads_ref, here_ref = outs
    cap_copy = pltpu.make_async_copy(cap_ref, cap, sem)
    cap_copy.start()
    width = here_ref.shape[2]
    units = pieces[0].shape[1] // 3
    own_rows = count * SLOT
    r = lax.axis_index("rep")
    e = lax.axis_index("ep")
    mine = e // SPLIT
    inputs = [[], []]
    for k in range(rep):
        for part in range(2):
            n = 2 * k + part
            chosen = [b[:, n * width : (n + 1) * width] for b in blocks]
            chosen = jnp.concatenate(chosen, axis=0)
            inputs[part].append(chosen)
            if k == 0:
                here_ref[part] = chosen
    sum_x, sum_d = 0.0, 0.0
    for (k, start, stop), piece in zip(spans, pieces):
        sum_x = sum_x + dot(inputs[0][k][:, start:stop], piece[:, : 2 * units])
        sum_d = sum_d + dot(inputs[1][k][:, start:stop], piece[:, 2 * units :])

    cap_copy.wait()
    capacity = (BLOCK * cap[mine, r]).astype(F32)
    lane = iota((SLOT, LANES), 1)
    sources, rates, counts = [], [], []
    for n in range(2 * count):
        sources.append(jnp.bitwise_xor(e, CORES * turned(n % count) + n // count))
        rate = jnp.where(lane == 0, blocks[n][:, 2 * rep * width :].astype(F32), 0.0)
        rate = jnp.sum(rate, axis=1, keepdims=True)
        rates.append(rate)
        counts.append(jnp.sum(jnp.where(rate > 0.0, 1.0, 0.0), axis=0, keepdims=True))
    slot = iota((SLOT, 1), 0).astype(F32)
    rate_rows, kept_rows = [], []
    for n in range(2 * count):
        start = jnp.zeros((1, 1), F32)
        for other in range(2 * count):
            start = start + jnp.where(sources[other] < sources[n], counts[other], 0.0)
        kept = jnp.where((rates[n] > 0.0) & (start + slot < capacity), 1.0, 0.0)
        kept_rows.append(kept)
        rate_rows.append(rates[n] * kept)
    rate = jnp.concatenate(rate_rows, axis=0)
    kept = jnp.concatenate(kept_rows, axis=0)

    pre_gate, pre_up, back_hidden = sum_x[:, :units], sum_x[:, units:], sum_d
    sig = 1.0 / (1.0 + jnp.exp(-pre_gate))
    activated = pre_gate * sig
    hidden = activated * pre_up
    score = jnp.sum(hidden * back_hidden, axis=1, keepdims=True) * kept
    lane = iota((2 * own_rows, LANES), 1)
    scores = jnp.where(lane == e % CORES, score, 0.0).astype(BF16)
    scaled = back_hidden * rate
    gate_grad = (scaled * pre_up * sig * (1.0 + pre_gate * (1.0 - sig))).astype(BF16)
    up_grad = (scaled * activated).astype(BF16)
    weighted = (hidden * rate).astype(BF16)
    grads_ref[...] = jnp.concatenate([gate_grad, up_grad, weighted], axis=1)
    pair = jnp.concatenate([gate_grad, up_grad], axis=1)
    for (k, start, stop), piece in zip(spans, pieces):
        back = dot(pair, piece[:, : 2 * units], ((1,), (1,))).astype(BF16)
        some = slice(k * width + start, k * width + stop)
        own_ref[:, some] = back[:own_rows]
        other_ref[:, some] = back[own_rows:]
    own_ref[:, rep * width :] = scores[:own_rows]
    other_ref[:, rep * width :] = scores[own_rows:]


def sum_kernel(own_ref, got_ref, *outs):
    for j, out in enumerate(outs):
        some = slice(j * SLOT, (j + 1) * SLOT)
        out[...] = (own_ref[some].astype(F32) + got_ref[some].astype(F32)).astype(BF16)


def stack_kernel(*refs):
    for k, ref in enumerate(refs[:-1]):
        refs[-1][k] = ref[...]


def weight_kernel(rep, here_ref, own_ref, other_ref, *refs):
    grads, outs = refs[:rep], refs[rep:]
    units = outs[0].shape[1]
    half = grads[0].shape[0] // 2
    sums = []
    for part, columns in enumerate((slice(0, 2 * units), slice(2 * units, 3 * units))):
        some = slice(part * half, (part + 1) * half)
        rows = [here_ref[part]]
        for k in range(rep - 1):
            rows += [own_ref[k, some], other_ref[k, some]]
        rows = jnp.concatenate(rows, axis=0)
        got = jnp.concatenate([ref[:, columns] for ref in grads], axis=0)
        sums.append(dot(got, rows, ((0,), (0,))))
    outs[0][...] = sums[0][:units].T.astype(BF16)
    outs[1][...] = sums[0][units:].T.astype(BF16)
    outs[2][...] = sums[1].T.astype(BF16)


def token_kernel(rep, flight, ids_ref, placed_ref, *refs):
    backs, rest = refs[: flight * CHIPS], refs[flight * CHIPS :]
    out_ref, weight_ref, blocks, ids, sem = rest
    ids_copy = pltpu.make_async_copy(ids_ref, ids, sem)
    ids_copy.start()
    r = lax.axis_index("rep")
    mine = lax.axis_index("ep") // SPLIT
    spacing = EXPERTS // flight
    width = out_ref.shape[1] // rep
    joined = [
        jnp.concatenate([b[...] for b in backs[w * CHIPS : (w + 1) * CHIPS]], axis=0)
        for w in range(flight)
    ]
    for k in range(rep):
        total = 0.0
        for w in range(flight):
            some = joined[w][:, k * width : (k + 1) * width]
            total = total + dot(placed_ref[w], some, ((0,), (0,)))
        blocks[jnp.bitwise_xor(r, k)] = total.astype(BF16)
    for b in range(rep):
        out_ref[:, b * width : (b + 1) * width] = blocks[b]
    result = jnp.zeros(weight_ref.shape, F32)
    ids_copy.wait()
    for w in range(flight):
        score = dot(joined[w][:, rep * width :], placed_ref[w], ((0,), (0,)))
        score = jnp.sum(score, axis=0, keepdims=True)
        match = ids[...] == jnp.bitwise_xor(mine, w) * spacing
        result = result + jnp.where(match, score, 0.0)
    weight_ref[...] = result


def local(
    tokens, out_grad, expert_ids, route_weight, live_count, cap_blocks, w_gate, w_up, w_down_t
):
    rep = lax.axis_size("rep")
    ep = lax.axis_size("ep")
    far = rep // 2
    flight = ep // SPLIT
    count = ep // CORES
    tok_count, model_dim = tokens.shape
    width, units = w_gate.shape
    rows = count * SLOT
    ids_rows, rw_rows, caps = expert_ids.T, route_weight.T, cap_blocks.T

    def send(array, rep_bits, ep_bits):
        mask = rep_bits * ep + ep_bits
        pairs = [(a, a ^ mask) for a in range(rep * ep)]
        return lax.ppermute(array, ("rep", "ep"), pairs)

    def after(array, *others):
        return lax.optimization_barrier((array,) + others)[0]

    (weights,) = call(
        join_kernel,
        [shape((width, 3 * units))],
        [w_gate, w_up, w_down_t],
        stored=(0, 1, 2),
        kept=(0,),
        scratch=[pltpu.VMEM((width, 3 * units), BF16), pltpu.SemaphoreType.DMA((4,))],
        grant=54,
    )
    packed = call(
        functools.partial(pack_kernel, rep, flight),
        [shape((SLOT, 2 * model_dim + LANES))] * flight
        + [shape((flight, CHIPS * SLOT, tok_count))],
        [live_count, tokens, out_grad, ids_rows, rw_rows],
        stored=range(5),
        scratch=[
            pltpu.SMEM(live_count.shape, jnp.int32),
            pltpu.VMEM(ids_rows.shape, jnp.int32),
            pltpu.VMEM(rw_rows.shape, BF16),
            pltpu.VMEM((2, tok_count, model_dim), BF16),
            pltpu.VMEM((rep, SLOT, width), BF16),
            pltpu.SemaphoreType.DMA((2 * PARTS + 3,)),
        ],
        grant=53,
    )
    pays, placed = packed[:flight], packed[flight]

    half = width // 2
    whole = {0: weights}
    halves, sent = {}, []
    for k in range(1, rep):
        low, high = k & -k, 1 << (k.bit_length() - 1)
        if low == high:
            whole[k] = send(weights, k, 0)
            for h in range(2):
                kernel = functools.partial(half_kernel, h * half)
                (halves[k, h],) = call(kernel, [shape((half, 3 * units))], [whole[k]])
                sent.append(halves[k, h])
        else:
            halves[k, 0] = send(halves[k ^ low, 0], low, 0)
            halves[k, 1] = send(halves[k ^ high, 1], high, 0)
    spans, pieces = [], []
    for k in range(rep):
        if k in whole:
            spans.append((k, 0, width))
            pieces.append(whole[k])
        else:
            spans += [(k, 0, half), (k, half, width)]
            pieces += [halves[k, 0], halves[k, 1]]

    order = [turned(n) for n in range(count)]
    blocks = [send(pays[j // CHIPS], 0, CORES * j) if j else pays[0] for j in order]
    parts = call(
        functools.partial(parts_kernel, count),
        [shape((2 * rows, width))] * (rep - 1),
        [after(blocks[0], *sent)] + blocks[1:],
    )
    here, nearest = order.index(0), order.index(1)
    ready = list(blocks)
    ready[here] = after(blocks[here], blocks[nearest])
    blocks = blocks + [send(block, 0, 1) for block in ready]
    results = call(
        functools.partial(hidden_kernel, rep, count, tuple(spans)),
        [shape((rows, model_dim + LANES))] * 2
        + [shape((2 * rows, 3 * units)), shape((2, 2 * rows, width))],
        [caps] + blocks + pieces,
        stored=(0,),
        scratch=[pltpu.SMEM(caps.shape, jnp.int32), pltpu.SemaphoreType.DMA(())],
        flops=2 * 2 * rows * model_dim * 5 * units,
    )
    own, other, grads, here = results
    summed = call(
        sum_kernel,
        [shape((SLOT, model_dim + LANES))] * count,
        [own, send(other, 0, 1)],
        flops=2 * rows * model_dim,
    )
    backs = [send(part, 0, CORES * j) if j else part for j, part in zip(order, summed)]

    moved = [send(part, k, 0) for k, part in enumerate(parts, 1)]
    (own_rows,) = call(stack_kernel, [shape((rep - 1, 2 * rows, width))], [after(moved[0], grads)] + moved[1:])
    other_rows = send(own_rows, 0, 1)
    group_grads = [grads] + [send(grads, k, 0) for k in range(1, rep)]
    grad_gate, grad_up, grad_down = call(
        functools.partial(weight_kernel, rep),
        [shape((width, units))] * 3,
        [here, own_rows, other_rows] + group_grads,
        flops=2 * 2 * rep * rows * width * 3 * units,
    )
    grad_tokens, grad_weight = call(
        functools.partial(token_kernel, rep, flight),
        [shape((tok_count, model_dim)), shape(ids_rows.shape, F32)],
        [ids_rows, placed] + backs,
        stored=(0,),
        scratch=[
            pltpu.VMEM((rep, tok_count, width), BF16),
            pltpu.VMEM(ids_rows.shape, jnp.int32),
            pltpu.SemaphoreType.DMA(()),
        ],
        flops=1000 * 2 * tok_count * CHIPS * SLOT * model_dim,
    )
    return grad_tokens, grad_weight.T, grad_gate, grad_up, grad_down


def solution(mesh):
    return jax.shard_map(
        local,
        mesh=mesh,
        in_specs=(
            P(("rep", "ep"), None),
            P(("rep", "ep"), None),
            P(("rep", "ep"), None),
            P(("rep", "ep"), None),
            P(),
            P(),
            P("rep", "ep"),
            P("rep", "ep"),
            P("rep", "ep"),
        ),
        out_specs=(
            P(("rep", "ep"), None),
            P(("rep", "ep"), None),
            P("rep", "ep"),
            P("rep", "ep"),
            P("rep", "ep"),
        ),
        check_vma=False,
    )
```

```python
import functools

import jax
import jax.numpy as jnp
from jax import lax
from jax.experimental import pallas as pl
from jax.experimental.pallas import tpu as pltpu
from jax.sharding import PartitionSpec as P

EXPERTS = 128
SLOT = 16
BLOCK = 128
SPLIT = 8
CORES = 2
CHIPS = SPLIT // CORES
LANES = 128
F32 = jnp.float32
BF16 = jnp.bfloat16
PARTS = 4
HBM = pl.BlockSpec(memory_space=pltpu.HBM)
VMEM = pl.BlockSpec(memory_space=pltpu.VMEM)


def shape(dims, kind=BF16):
    return jax.ShapeDtypeStruct(dims, kind)


def call(kernel, outs, args, stored=(), kept=(), scratch=(), flops=0, grant=16):
    size = sum(a.size * a.dtype.itemsize for a in args) + sum(
        o.size * o.dtype.itemsize for o in outs
    )
    return pl.pallas_call(
        kernel,
        out_shape=tuple(outs),
        in_specs=[HBM if n in stored else VMEM for n in range(len(args))],
        out_specs=tuple([HBM if n in kept else VMEM for n in range(len(outs))]),
        scratch_shapes=scratch,
        compiler_params=pltpu.CompilerParams(vmem_limit_bytes=grant * 1024 * 1024),
        cost_estimate=pl.CostEstimate(flops=flops, bytes_accessed=size, transcendentals=0),
    )(*args)


def fetch(pairs, sems, first=0):
    copies = [
        pltpu.make_async_copy(source, target, sems.at[first + n])
        for n, (source, target) in enumerate(pairs)
    ]
    for copy in copies:
        copy.start()
    return copies


def dot(a, b, dims=((1,), (0,))):
    return lax.dot_general(a, b, (dims, ((), ())), preferred_element_type=F32)


def iota(dims, axis):
    return lax.broadcasted_iota(jnp.int32, dims, axis)


def turned(n):
    return n ^ (CHIPS - 1)


def pack_kernel(rep, flight, live_ref, tok_ref, grad_ref, ids_ref, rw_ref, *refs):
    stored, pays, placed_ref, all_ref = refs[:3], refs[3 : 3 + flight], refs[-9], refs[-8]
    live, ids_held, rw_held, data, rows, joined, sems = refs[-7:]
    r = lax.axis_index("rep")
    mine = lax.axis_index("ep") // SPLIT
    count, model = tok_ref.shape
    width = model // rep
    spacing = EXPERTS // flight
    small = fetch([(live_ref, live), (ids_ref, ids_held), (rw_ref, rw_held)], sems)
    units = stored[0].shape[1]
    piece = width // 2
    pairs = []
    for p in range(2):
        some = pl.ds(p * piece, piece)
        for n, ref in enumerate(stored):
            pairs.append((ref.at[some], joined.at[some, pl.ds(n * units, units)]))
    weight_copies = fetch(pairs, sems, 3)
    pairs = []
    for part, ref in enumerate((tok_ref, grad_ref)):
        for p in range(PARTS):
            some = pl.ds(p * (count // PARTS), count // PARTS)
            pairs.append((ref.at[some], data.at[part, some]))
    large = fetch(pairs, sems, 9)
    for copy in small:
        copy.wait()
    token = iota((1, count), 1)
    upper = (iota((count, count), 0) <= iota((count, count), 1)).astype(BF16)
    slot = iota((SLOT, count), 0).astype(F32)
    lane = iota((SLOT, LANES), 1)
    ids = ids_held[...]
    weights = rw_held[...].astype(F32)
    firsts = []
    for w in range(flight):
        expert = jnp.bitwise_xor(mine, w)
        match = ids == expert * spacing
        routed = jnp.any(match, axis=0, keepdims=True) & (token < live[r])
        weight = jnp.sum(jnp.where(match, weights, 0.0), axis=0, keepdims=True)
        routed = jnp.broadcast_to(jnp.where(routed, 1.0, 0.0), (SLOT, count))
        rank = dot(routed.astype(BF16), upper) - 1.0
        placed = jnp.where(rank == slot, routed, 0.0)
        column = jnp.sum(placed * weight, axis=1, keepdims=True)
        pays[w][:, 2 * model :] = jnp.where(lane == 0, column, 0.0).astype(BF16)
        placed = placed.astype(BF16)
        firsts.append(placed)
        placed_ref[w] = jnp.concatenate([placed] * CHIPS, axis=0)
    out_copies = []
    for p in range(2):
        for n in range(len(stored)):
            weight_copies[3 * p + n].wait()
        some = pl.ds(p * piece, piece)
        out_copies += fetch([(joined.at[some], all_ref.at[some])], sems, 9 + 2 * PARTS + p)
    for part in range(2):
        for p in range(PARTS):
            large[part * PARTS + p].wait()
        for w in range(flight):
            chosen = dot(firsts[w], data[part]).astype(BF16)
            for b in range(rep):
                rows[b] = chosen[:, b * width : (b + 1) * width]
            for k in range(rep):
                n = 2 * k + part
                pays[w][:, n * width : (n + 1) * width] = rows[jnp.bitwise_xor(r, k)]
    for copy in out_copies:
        copy.wait()


def half_kernel(start, all_ref, half_ref):
    half_ref[...] = all_ref[start : start + half_ref.shape[0]]


def hidden_kernel(rep, count, spans, cap_ref, *refs):
    blocks, pieces = refs[: 2 * count], refs[2 * count : 2 * count + len(spans)]
    outs, cap, sem = refs[2 * count + len(spans) : -2], refs[-2], refs[-1]
    own_ref, other_ref, grads_ref, here_ref, away_refs = *outs[:4], outs[4:]
    cap_copy = pltpu.make_async_copy(cap_ref, cap, sem)
    cap_copy.start()
    width = here_ref.shape[2]
    units = pieces[0].shape[1] // 3
    own_rows = count * SLOT
    r = lax.axis_index("rep")
    e = lax.axis_index("ep")
    mine = e // SPLIT
    inputs = [[], []]
    for k in range(rep):
        for part in range(2):
            n = 2 * k + part
            chosen = [b[:, n * width : (n + 1) * width] for b in blocks]
            chosen = jnp.concatenate(chosen, axis=0)
            inputs[part].append(chosen)
            if k == 0:
                here_ref[part] = chosen
            else:
                some = slice(part * own_rows, (part + 1) * own_rows)
                away_refs[k - 1][some, :width] = chosen[:own_rows]
    sum_x, sum_d = 0.0, 0.0
    for (k, start, stop), piece in zip(spans, pieces):
        sum_x = sum_x + dot(inputs[0][k][:, start:stop], piece[:, : 2 * units])
        sum_d = sum_d + dot(inputs[1][k][:, start:stop], piece[:, 2 * units :])

    cap_copy.wait()
    capacity = (BLOCK * cap[mine, r]).astype(F32)
    lane = iota((SLOT, LANES), 1)
    sources, rates, counts = [], [], []
    for n in range(2 * count):
        sources.append(jnp.bitwise_xor(e, CORES * turned(n % count) + n // count))
        rate = jnp.where(lane == 0, blocks[n][:, 2 * rep * width :].astype(F32), 0.0)
        rate = jnp.sum(rate, axis=1, keepdims=True)
        rates.append(rate)
        counts.append(jnp.sum(jnp.where(rate > 0.0, 1.0, 0.0), axis=0, keepdims=True))
    slot = iota((SLOT, 1), 0).astype(F32)
    rate_rows, kept_rows = [], []
    for n in range(2 * count):
        start = jnp.zeros((1, 1), F32)
        for other in range(2 * count):
            start = start + jnp.where(sources[other] < sources[n], counts[other], 0.0)
        kept = jnp.where((rates[n] > 0.0) & (start + slot < capacity), 1.0, 0.0)
        kept_rows.append(kept)
        rate_rows.append(rates[n] * kept)
    rate = jnp.concatenate(rate_rows, axis=0)
    kept = jnp.concatenate(kept_rows, axis=0)

    pre_gate, pre_up, back_hidden = sum_x[:, :units], sum_x[:, units:], sum_d
    sig = 1.0 / (1.0 + jnp.exp(-pre_gate))
    activated = pre_gate * sig
    hidden = activated * pre_up
    score = jnp.sum(hidden * back_hidden, axis=1, keepdims=True) * kept
    lane = iota((2 * own_rows, LANES), 1)
    scores = jnp.where(lane == e % CORES, score, 0.0).astype(BF16)
    scaled = back_hidden * rate
    gate_grad = (scaled * pre_up * sig * (1.0 + pre_gate * (1.0 - sig))).astype(BF16)
    up_grad = (scaled * activated).astype(BF16)
    weighted = (hidden * rate).astype(BF16)
    grads_ref[...] = jnp.concatenate([gate_grad, up_grad, weighted], axis=1)
    for ref in away_refs:
        ref[:, width:] = grads_ref[...]
    pair = jnp.concatenate([gate_grad, up_grad], axis=1)
    for (k, start, stop), piece in zip(spans, pieces):
        back = dot(pair, piece[:, : 2 * units], ((1,), (1,))).astype(BF16)
        some = slice(k * width + start, k * width + stop)
        own_ref[:, some] = back[:own_rows]
        other_ref[:, some] = back[own_rows:]
    own_ref[:, rep * width :] = scores[:own_rows]
    other_ref[:, rep * width :] = scores[own_rows:]


def sum_kernel(own_ref, got_ref, *outs):
    for j, out in enumerate(outs):
        some = slice(j * SLOT, (j + 1) * SLOT)
        out[...] = (own_ref[some].astype(F32) + got_ref[some].astype(F32)).astype(BF16)


def stack_kernel(*refs):
    for k, ref in enumerate(refs[:-1]):
        refs[-1][k] = ref[:, : refs[-1].shape[2]]


def weight_kernel(rep, here_ref, grads_ref, other_ref, *refs):
    away, outs, held, sems = refs[: rep - 1], refs[rep - 1 : -4], refs[-4:-1], refs[-1]
    units = outs[0].shape[1]
    width = here_ref.shape[2]
    half = grads_ref.shape[0] // 2
    copies = []
    for part, columns in enumerate((slice(0, 2 * units), slice(2 * units, 3 * units))):
        some = slice(part * half, (part + 1) * half)
        rows = [here_ref[part]]
        got = [grads_ref[:, columns]]
        for k, ref in enumerate(away):
            rows += [ref[some, :width], other_ref[k, some]]
            got.append(ref[:, width + columns.start : width + columns.stop])
        rows = jnp.concatenate(rows, axis=0)
        got = jnp.concatenate(got, axis=0)
        total = dot(got, rows, ((0,), (0,)))
        for n in range(total.shape[0] // units):
            held[2 * part + n][...] = total[n * units : (n + 1) * units].T.astype(BF16)
            copies += fetch([(held[2 * part + n], outs[2 * part + n])], sems, 2 * part + n)
    for copy in copies:
        copy.wait()


def token_kernel(rep, flight, ids_ref, placed_ref, *refs):
    backs, rest = refs[: flight * CHIPS], refs[flight * CHIPS :]
    out_ref, weight_ref, blocks, ids, sems = rest
    (ids_copy,) = fetch([(ids_ref, ids)], sems)
    r = lax.axis_index("rep")
    mine = lax.axis_index("ep") // SPLIT
    spacing = EXPERTS // flight
    width = out_ref.shape[1] // rep
    joined = [
        jnp.concatenate([b[...] for b in backs[w * CHIPS : (w + 1) * CHIPS]], axis=0)
        for w in range(flight)
    ]
    for k in range(rep):
        total = 0.0
        for w in range(flight):
            some = joined[w][:, k * width : (k + 1) * width]
            total = total + dot(placed_ref[w], some, ((0,), (0,)))
        blocks[jnp.bitwise_xor(r, k)] = total.astype(BF16)
    for b in range(rep):
        out_ref[:, b * width : (b + 1) * width] = blocks[b]
    result = jnp.zeros(weight_ref.shape, F32)
    ids_copy.wait()
    for w in range(flight):
        score = dot(joined[w][:, rep * width :], placed_ref[w], ((0,), (0,)))
        score = jnp.sum(score, axis=0, keepdims=True)
        match = ids[...] == jnp.bitwise_xor(mine, w) * spacing
        result = result + jnp.where(match, score, 0.0)
    weight_ref[...] = result


def local(
    tokens, out_grad, expert_ids, route_weight, live_count, cap_blocks, w_gate, w_up, w_down_t
):
    rep = lax.axis_size("rep")
    ep = lax.axis_size("ep")
    far = rep // 2
    flight = ep // SPLIT
    count = ep // CORES
    tok_count, model_dim = tokens.shape
    width, units = w_gate.shape
    rows = count * SLOT
    ids_rows, rw_rows, caps = expert_ids.T, route_weight.T, cap_blocks.T

    def send(array, rep_bits, ep_bits):
        mask = rep_bits * ep + ep_bits
        pairs = [(a, a ^ mask) for a in range(rep * ep)]
        return lax.ppermute(array, ("rep", "ep"), pairs)

    def after(array, *others):
        return lax.optimization_barrier((array,) + others)[0]

    packed = call(
        functools.partial(pack_kernel, rep, flight),
        [shape((SLOT, 2 * model_dim + LANES))] * flight
        + [shape((flight, CHIPS * SLOT, tok_count)), shape((width, 3 * units))],
        [live_count, tokens, out_grad, ids_rows, rw_rows, w_gate, w_up, w_down_t],
        stored=range(8),
        kept=(flight + 1,),
        scratch=[
            pltpu.SMEM(live_count.shape, jnp.int32),
            pltpu.VMEM(ids_rows.shape, jnp.int32),
            pltpu.VMEM(rw_rows.shape, BF16),
            pltpu.VMEM((2, tok_count, model_dim), BF16),
            pltpu.VMEM((rep, SLOT, width), BF16),
            pltpu.VMEM((width, 3 * units), BF16),
            pltpu.SemaphoreType.DMA((2 * PARTS + 11,)),
        ],
        grant=54,
    )
    pays, placed, weights = packed[:flight], packed[flight], packed[flight + 1]

    half = width // 2
    whole = {0: weights}
    halves = {}
    for k in range(1, rep):
        low, high = k & -k, 1 << (k.bit_length() - 1)
        if low == high:
            whole[k] = send(weights, k, 0)
            for h in range(2):
                kernel = functools.partial(half_kernel, h * half)
                (halves[k, h],) = call(kernel, [shape((half, 3 * units))], [whole[k]])
        else:
            halves[k, 0] = send(halves[k ^ low, 0], low, 0)
            halves[k, 1] = send(halves[k ^ high, 1], high, 0)
    spans, pieces = [], []
    for k in range(rep):
        if k in whole:
            spans.append((k, 0, width))
            pieces.append(whole[k])
        else:
            spans += [(k, 0, half), (k, half, width)]
            pieces += [halves[k, 0], halves[k, 1]]

    order = [turned(n) for n in range(count)]
    blocks = [send(pays[j // CHIPS], 0, CORES * j) if j else pays[0] for j in order]
    nearest = blocks[order.index(1)]
    ready = [after(b, nearest) if j == 0 else b for j, b in zip(order, blocks)]
    blocks = blocks + [send(block, 0, 1) for block in ready]
    results = call(
        functools.partial(hidden_kernel, rep, count, tuple(spans)),
        [shape((rows, model_dim + LANES))] * 2
        + [shape((2 * rows, 3 * units)), shape((2, 2 * rows, width))]
        + [shape((2 * rows, width + 3 * units))] * (rep - 1),
        [caps] + blocks + pieces,
        stored=(0,),
        scratch=[pltpu.SMEM(caps.shape, jnp.int32), pltpu.SemaphoreType.DMA(())],
        flops=2 * 2 * rows * model_dim * 5 * units,
    )
    own, other, grads, here, away = *results[:4], results[4:]
    summed = call(sum_kernel, [shape((SLOT, model_dim + LANES))] * count, [own, send(other, 0, 1)])
    backs = [send(part, 0, CORES * j) if j else part for j, part in zip(order, summed)]

    moved = [send(away[k - 1], k, 0) for k in range(1, rep)]
    (own_rows,) = call(stack_kernel, [shape((rep - 1, 2 * rows, width))], moved)
    other_rows = send(own_rows, 0, 1)
    grad_gate, grad_up, grad_down = call(
        functools.partial(weight_kernel, rep),
        [shape((width, units))] * 3,
        [here, grads, other_rows] + moved,
        kept=(0, 1, 2),
        scratch=[pltpu.VMEM((width, units), BF16)] * 3 + [pltpu.SemaphoreType.DMA((3,))],
        flops=2 * 2 * rep * rows * width * 3 * units,
    )
    grad_tokens, grad_weight = call(
        functools.partial(token_kernel, rep, flight),
        [shape((tok_count, model_dim)), shape(ids_rows.shape, F32)],
        [ids_rows, placed] + backs,
        stored=(0,),
        scratch=[
            pltpu.VMEM((rep, tok_count, width), BF16),
            pltpu.VMEM(ids_rows.shape, jnp.int32),
            pltpu.SemaphoreType.DMA((1,)),
        ],
        flops=1000 * 2 * tok_count * CHIPS * SLOT * model_dim,
    )
    return grad_tokens, grad_weight.T, grad_gate, grad_up, grad_down


def solution(mesh):
    return jax.shard_map(
        local,
        mesh=mesh,
        in_specs=(
            P(("rep", "ep"), None),
            P(("rep", "ep"), None),
            P(("rep", "ep"), None),
            P(("rep", "ep"), None),
            P(),
            P(),
            P("rep", "ep"),
            P("rep", "ep"),
            P("rep", "ep"),
        ),
        out_specs=(
            P(("rep", "ep"), None),
            P(("rep", "ep"), None),
            P("rep", "ep"),
            P("rep", "ep"),
            P("rep", "ep"),
        ),
        check_vma=False,
    )
```

```python
import functools

import jax
import jax.numpy as jnp
from jax import lax
from jax.experimental import pallas as pl
from jax.experimental.pallas import tpu as pltpu
from jax.sharding import PartitionSpec as P

EXPERTS = 128
SLOT = 16
BLOCK = 128
SPLIT = 8
CORES = 2
CHIPS = SPLIT // CORES
LANES = 128
F32 = jnp.float32
BF16 = jnp.bfloat16
PARTS = 4
HBM = pl.BlockSpec(memory_space=pltpu.HBM)
VMEM = pl.BlockSpec(memory_space=pltpu.VMEM)


def shape(dims, kind=BF16):
    return jax.ShapeDtypeStruct(dims, kind)


def call(kernel, outs, args, stored=(), kept=(), scratch=(), flops=0, grant=16):
    size = sum(a.size * a.dtype.itemsize for a in args) + sum(
        o.size * o.dtype.itemsize for o in outs
    )
    return pl.pallas_call(
        kernel,
        out_shape=tuple(outs),
        in_specs=[HBM if n in stored else VMEM for n in range(len(args))],
        out_specs=tuple([HBM if n in kept else VMEM for n in range(len(outs))]),
        scratch_shapes=scratch,
        compiler_params=pltpu.CompilerParams(vmem_limit_bytes=grant * 1024 * 1024),
        cost_estimate=pl.CostEstimate(flops=flops, bytes_accessed=size, transcendentals=0),
    )(*args)


def fetch(pairs, sems, first=0):
    copies = [
        pltpu.make_async_copy(source, target, sems.at[first + n])
        for n, (source, target) in enumerate(pairs)
    ]
    for copy in copies:
        copy.start()
    return copies


def dot(a, b, dims=((1,), (0,))):
    return lax.dot_general(a, b, (dims, ((), ())), preferred_element_type=F32)


def iota(dims, axis):
    return lax.broadcasted_iota(jnp.int32, dims, axis)


def turned(n):
    return n ^ (CHIPS - 1)


def pack_kernel(rep, flight, live_ref, tok_ref, grad_ref, ids_ref, rw_ref, *refs):
    stored, pays, placed_ref, all_ref = refs[:3], refs[3 : 3 + flight], refs[-9], refs[-8]
    live, ids_held, rw_held, data, rows, joined, sems = refs[-7:]
    r = lax.axis_index("rep")
    mine = lax.axis_index("ep") // SPLIT
    count, model = tok_ref.shape
    width = model // rep
    spacing = EXPERTS // flight
    small = fetch([(live_ref, live), (ids_ref, ids_held), (rw_ref, rw_held)], sems)
    units = stored[0].shape[1]
    piece = width // 2
    pairs = []
    for p in range(2):
        some = pl.ds(p * piece, piece)
        for n, ref in enumerate(stored):
            pairs.append((ref.at[some], joined.at[some, pl.ds(n * units, units)]))
    weight_copies = fetch(pairs, sems, 3)
    pairs = []
    for part, ref in enumerate((tok_ref, grad_ref)):
        for p in range(PARTS):
            some = pl.ds(p * (count // PARTS), count // PARTS)
            pairs.append((ref.at[some], data.at[part, some]))
    large = fetch(pairs, sems, 9)
    for copy in small:
        copy.wait()
    token = iota((1, count), 1)
    upper = (iota((count, count), 0) <= iota((count, count), 1)).astype(BF16)
    slot = iota((SLOT, count), 0).astype(F32)
    lane = iota((SLOT, LANES), 1)
    ids = ids_held[...]
    weights = rw_held[...].astype(F32)
    firsts = []
    for w in range(flight):
        expert = jnp.bitwise_xor(mine, w)
        match = ids == expert * spacing
        routed = jnp.any(match, axis=0, keepdims=True) & (token < live[r])
        weight = jnp.sum(jnp.where(match, weights, 0.0), axis=0, keepdims=True)
        routed = jnp.broadcast_to(jnp.where(routed, 1.0, 0.0), (SLOT, count))
        rank = dot(routed.astype(BF16), upper) - 1.0
        placed = jnp.where(rank == slot, routed, 0.0)
        column = jnp.sum(placed * weight, axis=1, keepdims=True)
        pays[w][:, 2 * model :] = jnp.where(lane == 0, column, 0.0).astype(BF16)
        placed = placed.astype(BF16)
        firsts.append(placed)
        placed_ref[w] = jnp.concatenate([placed] * CHIPS, axis=0)
    out_copies = []
    for p in range(2):
        for n in range(len(stored)):
            weight_copies[3 * p + n].wait()
        some = pl.ds(p * piece, piece)
        out_copies += fetch([(joined.at[some], all_ref.at[some])], sems, 9 + 2 * PARTS + p)
    for part in range(2):
        for p in range(PARTS):
            large[part * PARTS + p].wait()
        for w in range(flight):
            chosen = dot(firsts[w], data[part]).astype(BF16)
            for b in range(rep):
                rows[b] = chosen[:, b * width : (b + 1) * width]
            for k in range(rep):
                n = 2 * k + part
                pays[w][:, n * width : (n + 1) * width] = rows[jnp.bitwise_xor(r, k)]
    for copy in out_copies:
        copy.wait()


def near_groups(rep):
    return [k for k in range(1, rep) if k & (k - 1) == 0]


def far_groups(rep):
    return [k for k in range(1, rep) if k & (k - 1)]


def columns_kernel(groups, count, *refs):
    blocks, outs = refs[:count], refs[count:]
    rows, width = count * SLOT, outs[0].shape[1]
    for k, out in zip(groups, outs):
        for part in range(2):
            n = 2 * k + part
            for j in range(count):
                start = part * rows + j * SLOT
                out[start : start + SLOT] = blocks[j][:, n * width : (n + 1) * width]


def half_kernel(start, all_ref, half_ref):
    half_ref[...] = all_ref[start : start + half_ref.shape[0]]


def hidden_kernel(rep, count, spans, cap_ref, *refs):
    blocks, pieces = refs[: 2 * count], refs[2 * count : 2 * count + len(spans)]
    outs, cap, sem = refs[2 * count + len(spans) : -2], refs[-2], refs[-1]
    own_ref, other_ref, grads_ref, here_ref, away_refs = *outs[:4], outs[4:]
    far = far_groups(rep)
    cap_copy = pltpu.make_async_copy(cap_ref, cap, sem)
    cap_copy.start()
    width = here_ref.shape[2]
    units = pieces[0].shape[1] // 3
    own_rows = count * SLOT
    r = lax.axis_index("rep")
    e = lax.axis_index("ep")
    mine = e // SPLIT
    inputs = [[], []]
    for k in range(rep):
        for part in range(2):
            n = 2 * k + part
            chosen = [b[:, n * width : (n + 1) * width] for b in blocks]
            chosen = jnp.concatenate(chosen, axis=0)
            inputs[part].append(chosen)
            if k == 0:
                here_ref[part] = chosen
            elif k in far:
                some = slice(part * own_rows, (part + 1) * own_rows)
                away_refs[far.index(k)][some, :width] = chosen[:own_rows]
    sum_x, sum_d = 0.0, 0.0
    for (k, start, stop), piece in zip(spans, pieces):
        sum_x = sum_x + dot(inputs[0][k][:, start:stop], piece[:, : 2 * units])
        sum_d = sum_d + dot(inputs[1][k][:, start:stop], piece[:, 2 * units :])

    cap_copy.wait()
    capacity = (BLOCK * cap[mine, r]).astype(F32)
    lane = iota((SLOT, LANES), 1)
    sources, rates, counts = [], [], []
    for n in range(2 * count):
        sources.append(jnp.bitwise_xor(e, CORES * turned(n % count) + n // count))
        rate = jnp.where(lane == 0, blocks[n][:, 2 * rep * width :].astype(F32), 0.0)
        rate = jnp.sum(rate, axis=1, keepdims=True)
        rates.append(rate)
        counts.append(jnp.sum(jnp.where(rate > 0.0, 1.0, 0.0), axis=0, keepdims=True))
    slot = iota((SLOT, 1), 0).astype(F32)
    rate_rows, kept_rows = [], []
    for n in range(2 * count):
        start = jnp.zeros((1, 1), F32)
        for other in range(2 * count):
            start = start + jnp.where(sources[other] < sources[n], counts[other], 0.0)
        kept = jnp.where((rates[n] > 0.0) & (start + slot < capacity), 1.0, 0.0)
        kept_rows.append(kept)
        rate_rows.append(rates[n] * kept)
    rate = jnp.concatenate(rate_rows, axis=0)
    kept = jnp.concatenate(kept_rows, axis=0)

    pre_gate, pre_up, back_hidden = sum_x[:, :units], sum_x[:, units:], sum_d
    sig = 1.0 / (1.0 + jnp.exp(-pre_gate))
    activated = pre_gate * sig
    hidden = activated * pre_up
    score = jnp.sum(hidden * back_hidden, axis=1, keepdims=True) * kept
    lane = iota((2 * own_rows, LANES), 1)
    scores = jnp.where(lane == e % CORES, score, 0.0).astype(BF16)
    scaled = back_hidden * rate
    gate_grad = (scaled * pre_up * sig * (1.0 + pre_gate * (1.0 - sig))).astype(BF16)
    up_grad = (scaled * activated).astype(BF16)
    weighted = (hidden * rate).astype(BF16)
    grads_ref[...] = jnp.concatenate([gate_grad, up_grad, weighted], axis=1)
    for ref in away_refs:
        ref[:, width:] = grads_ref[...]
    pair = jnp.concatenate([gate_grad, up_grad], axis=1)
    for (k, start, stop), piece in zip(spans, pieces):
        back = dot(pair, piece[:, : 2 * units], ((1,), (1,))).astype(BF16)
        some = slice(k * width + start, k * width + stop)
        own_ref[:, some] = back[:own_rows]
        other_ref[:, some] = back[own_rows:]
    own_ref[:, rep * width :] = scores[:own_rows]
    other_ref[:, rep * width :] = scores[own_rows:]


def sum_kernel(own_ref, got_ref, *outs):
    for j, out in enumerate(outs):
        some = slice(j * SLOT, (j + 1) * SLOT)
        out[...] = (own_ref[some].astype(F32) + got_ref[some].astype(F32)).astype(BF16)


def stack_kernel(*refs):
    for k, ref in enumerate(refs[:-1]):
        refs[-1][k] = ref[:, : refs[-1].shape[2]]


def weight_kernel(rep, here_ref, grads_ref, near_ref, near_other, far_other, *refs):
    near, far = len(near_groups(rep)), len(far_groups(rep))
    near_grads, away, outs = refs[:near], refs[near : near + far], refs[near + far : -4]
    held, sems = refs[-4:-1], refs[-1]
    units = outs[0].shape[1]
    width = here_ref.shape[2]
    half = grads_ref.shape[0] // 2
    copies = []
    for part, columns in enumerate((slice(0, 2 * units), slice(2 * units, 3 * units))):
        some = slice(part * half, (part + 1) * half)
        rows = [here_ref[part]]
        got = [grads_ref[:, columns]]
        for k, ref in enumerate(near_grads):
            rows += [near_ref[k, some], near_other[k, some]]
            got.append(ref[:, columns])
        for k, ref in enumerate(away):
            rows += [ref[some, :width], far_other[k, some]]
            got.append(ref[:, width + columns.start : width + columns.stop])
        rows = jnp.concatenate(rows, axis=0)
        got = jnp.concatenate(got, axis=0)
        total = dot(got, rows, ((0,), (0,)))
        for n in range(total.shape[0] // units):
            held[2 * part + n][...] = total[n * units : (n + 1) * units].T.astype(BF16)
            copies += fetch([(held[2 * part + n], outs[2 * part + n])], sems, 2 * part + n)
    for copy in copies:
        copy.wait()


def token_kernel(rep, flight, ids_ref, placed_ref, *refs):
    backs, rest = refs[: flight * CHIPS], refs[flight * CHIPS :]
    out_ref, weight_ref, blocks, ids, sems = rest
    (ids_copy,) = fetch([(ids_ref, ids)], sems)
    r = lax.axis_index("rep")
    mine = lax.axis_index("ep") // SPLIT
    spacing = EXPERTS // flight
    width = out_ref.shape[1] // rep
    joined = [
        jnp.concatenate([b[...] for b in backs[w * CHIPS : (w + 1) * CHIPS]], axis=0)
        for w in range(flight)
    ]
    for k in range(rep):
        total = 0.0
        for w in range(flight):
            some = joined[w][:, k * width : (k + 1) * width]
            total = total + dot(placed_ref[w], some, ((0,), (0,)))
        blocks[jnp.bitwise_xor(r, k)] = total.astype(BF16)
    for b in range(rep):
        out_ref[:, b * width : (b + 1) * width] = blocks[b]
    result = jnp.zeros(weight_ref.shape, F32)
    ids_copy.wait()
    for w in range(flight):
        score = dot(joined[w][:, rep * width :], placed_ref[w], ((0,), (0,)))
        score = jnp.sum(score, axis=0, keepdims=True)
        match = ids[...] == jnp.bitwise_xor(mine, w) * spacing
        result = result + jnp.where(match, score, 0.0)
    weight_ref[...] = result


def local(
    tokens, out_grad, expert_ids, route_weight, live_count, cap_blocks, w_gate, w_up, w_down_t
):
    rep = lax.axis_size("rep")
    ep = lax.axis_size("ep")
    far = rep // 2
    flight = ep // SPLIT
    count = ep // CORES
    tok_count, model_dim = tokens.shape
    width, units = w_gate.shape
    rows = count * SLOT
    ids_rows, rw_rows, caps = expert_ids.T, route_weight.T, cap_blocks.T

    def send(array, rep_bits, ep_bits):
        mask = rep_bits * ep + ep_bits
        pairs = [(a, a ^ mask) for a in range(rep * ep)]
        return lax.ppermute(array, ("rep", "ep"), pairs)

    def after(array, *others):
        return lax.optimization_barrier((array,) + others)[0]

    packed = call(
        functools.partial(pack_kernel, rep, flight),
        [shape((SLOT, 2 * model_dim + LANES))] * flight
        + [shape((flight, CHIPS * SLOT, tok_count)), shape((width, 3 * units))],
        [live_count, tokens, out_grad, ids_rows, rw_rows, w_gate, w_up, w_down_t],
        stored=range(8),
        kept=(flight + 1,),
        scratch=[
            pltpu.SMEM(live_count.shape, jnp.int32),
            pltpu.VMEM(ids_rows.shape, jnp.int32),
            pltpu.VMEM(rw_rows.shape, BF16),
            pltpu.VMEM((2, tok_count, model_dim), BF16),
            pltpu.VMEM((rep, SLOT, width), BF16),
            pltpu.VMEM((width, 3 * units), BF16),
            pltpu.SemaphoreType.DMA((2 * PARTS + 11,)),
        ],
        grant=54,
    )
    pays, placed, weights = packed[:flight], packed[flight], packed[flight + 1]

    half = width // 2
    whole = {0: weights}
    halves, sent = {}, []
    for k in range(1, rep):
        low, high = k & -k, 1 << (k.bit_length() - 1)
        if low == high:
            whole[k] = send(weights, k, 0)
            for h in range(2):
                kernel = functools.partial(half_kernel, h * half)
                (halves[k, h],) = call(kernel, [shape((half, 3 * units))], [whole[k]])
                sent.append(halves[k, h])
        else:
            halves[k, 0] = send(halves[k ^ low, 0], low, 0)
            halves[k, 1] = send(halves[k ^ high, 1], high, 0)
    spans, pieces = [], []
    for k in range(rep):
        if k in whole:
            spans.append((k, 0, width))
            pieces.append(whole[k])
        else:
            spans += [(k, 0, half), (k, half, width)]
            pieces += [halves[k, 0], halves[k, 1]]

    order = [turned(n) for n in range(count)]
    blocks = [send(pays[j // CHIPS], 0, CORES * j) if j else pays[0] for j in order]
    near, far = near_groups(rep), far_groups(rep)
    columns = call(
        functools.partial(columns_kernel, near, count),
        [shape((2 * rows, width))] * len(near),
        [after(blocks[0], *sent)] + blocks[1:],
    )
    nearest = blocks[order.index(1)]
    ready = [after(b, nearest) if j == 0 else b for j, b in zip(order, blocks)]
    blocks = blocks + [send(block, 0, 1) for block in ready]
    results = call(
        functools.partial(hidden_kernel, rep, count, tuple(spans)),
        [shape((rows, model_dim + LANES))] * 2
        + [shape((2 * rows, 3 * units)), shape((2, 2 * rows, width))]
        + [shape((2 * rows, width + 3 * units))] * len(far_groups(rep)),
        [caps] + blocks + pieces,
        stored=(0,),
        scratch=[pltpu.SMEM(caps.shape, jnp.int32), pltpu.SemaphoreType.DMA(())],
        flops=2 * 2 * rows * model_dim * 5 * units,
    )
    own, other, grads, here, away = *results[:4], results[4:]
    moved = [send(part, k, 0) for k, part in zip(near, columns)]
    (near_rows,) = call(
        stack_kernel,
        [shape((len(near), 2 * rows, width))],
        moved,
        flops=64000 * rows * width,
    )
    near_other = send(near_rows, 0, 1)
    summed = call(
        sum_kernel,
        [shape((SLOT, model_dim + LANES))] * count,
        [after(own, near_rows), send(other, 0, 1)],
        flops=2 * rows * model_dim,
    )
    backs = [send(part, 0, CORES * j) if j else part for j, part in zip(order, summed)]

    moved = [send(part, k, 0) for k, part in zip(far, away)]
    ready = [after(moved[0], backs[0])] + moved[1:]
    (far_rows,) = call(stack_kernel, [shape((len(far), 2 * rows, width))], ready)
    far_other = send(far_rows, 0, 1)
    late = after(grads, summed[0])
    near_grads = [send(late, k, 0) for k in near]
    grad_gate, grad_up, grad_down = call(
        functools.partial(weight_kernel, rep),
        [shape((width, units))] * 3,
        [here, grads, near_rows, near_other, far_other] + near_grads + moved,
        kept=(0, 1, 2),
        scratch=[pltpu.VMEM((width, units), BF16)] * 3 + [pltpu.SemaphoreType.DMA((3,))],
        flops=2 * 2 * rep * rows * width * 3 * units,
    )
    grad_tokens, grad_weight = call(
        functools.partial(token_kernel, rep, flight),
        [shape((tok_count, model_dim)), shape(ids_rows.shape, F32)],
        [ids_rows, placed] + backs,
        stored=(0,),
        scratch=[
            pltpu.VMEM((rep, tok_count, width), BF16),
            pltpu.VMEM(ids_rows.shape, jnp.int32),
            pltpu.SemaphoreType.DMA((1,)),
        ],
        flops=1000 * 2 * tok_count * CHIPS * SLOT * model_dim,
    )
    return grad_tokens, grad_weight.T, grad_gate, grad_up, grad_down


def solution(mesh):
    return jax.shard_map(
        local,
        mesh=mesh,
        in_specs=(
            P(("rep", "ep"), None),
            P(("rep", "ep"), None),
            P(("rep", "ep"), None),
            P(("rep", "ep"), None),
            P(),
            P(),
            P("rep", "ep"),
            P("rep", "ep"),
            P("rep", "ep"),
        ),
        out_specs=(
            P(("rep", "ep"), None),
            P(("rep", "ep"), None),
            P("rep", "ep"),
            P("rep", "ep"),
            P("rep", "ep"),
        ),
        check_vma=False,
    )
```

```python
import functools

import jax
import jax.numpy as jnp
from jax import lax
from jax.experimental import pallas as pl
from jax.experimental.pallas import tpu as pltpu
from jax.sharding import PartitionSpec as P

EXPERTS = 128
SLOT = 16
BLOCK = 128
SPLIT = 8
CORES = 2
CHIPS = SPLIT // CORES
LANES = 128
F32 = jnp.float32
BF16 = jnp.bfloat16
PARTS = 4
HBM = pl.BlockSpec(memory_space=pltpu.HBM)
VMEM = pl.BlockSpec(memory_space=pltpu.VMEM)


def shape(dims, kind=BF16):
    return jax.ShapeDtypeStruct(dims, kind)


def call(kernel, outs, args, stored=(), kept=(), scratch=(), flops=0, grant=16):
    size = sum(a.size * a.dtype.itemsize for a in args) + sum(
        o.size * o.dtype.itemsize for o in outs
    )
    return pl.pallas_call(
        kernel,
        out_shape=tuple(outs),
        in_specs=[HBM if n in stored else VMEM for n in range(len(args))],
        out_specs=tuple([HBM if n in kept else VMEM for n in range(len(outs))]),
        scratch_shapes=scratch,
        compiler_params=pltpu.CompilerParams(vmem_limit_bytes=grant * 1024 * 1024),
        cost_estimate=pl.CostEstimate(flops=flops, bytes_accessed=size, transcendentals=0),
    )(*args)


def fetch(pairs, sems, first=0):
    copies = [
        pltpu.make_async_copy(source, target, sems.at[first + n])
        for n, (source, target) in enumerate(pairs)
    ]
    for copy in copies:
        copy.start()
    return copies


def dot(a, b, dims=((1,), (0,))):
    return lax.dot_general(a, b, (dims, ((), ())), preferred_element_type=F32)


def iota(dims, axis):
    return lax.broadcasted_iota(jnp.int32, dims, axis)


def turned(n):
    return n ^ (CHIPS - 1)


def pack_kernel(rep, flight, live_ref, tok_ref, grad_ref, ids_ref, rw_ref, *refs):
    stored, pays, placed_ref, all_ref = refs[:3], refs[3 : 3 + flight], refs[-9], refs[-8]
    live, ids_held, rw_held, data, rows, joined, sems = refs[-7:]
    r = lax.axis_index("rep")
    mine = lax.axis_index("ep") // SPLIT
    count, model = tok_ref.shape
    width = model // rep
    spacing = EXPERTS // flight
    small = fetch([(live_ref, live), (ids_ref, ids_held), (rw_ref, rw_held)], sems)
    units = stored[0].shape[1]
    piece = width // 2
    pairs = []
    for p in range(2):
        some = pl.ds(p * piece, piece)
        for n, ref in enumerate(stored):
            pairs.append((ref.at[some], joined.at[some, pl.ds(n * units, units)]))
    weight_copies = fetch(pairs, sems, 3)
    pairs = []
    for part, ref in enumerate((tok_ref, grad_ref)):
        for p in range(PARTS):
            some = pl.ds(p * (count // PARTS), count // PARTS)
            pairs.append((ref.at[some], data.at[part, some]))
    large = fetch(pairs, sems, 9)
    for copy in small:
        copy.wait()
    token = iota((1, count), 1)
    upper = (iota((count, count), 0) <= iota((count, count), 1)).astype(BF16)
    slot = iota((SLOT, count), 0).astype(F32)
    lane = iota((SLOT, LANES), 1)
    ids = ids_held[...]
    weights = rw_held[...].astype(F32)
    firsts = []
    for w in range(flight):
        expert = jnp.bitwise_xor(mine, w)
        match = ids == expert * spacing
        routed = jnp.any(match, axis=0, keepdims=True) & (token < live[r])
        weight = jnp.sum(jnp.where(match, weights, 0.0), axis=0, keepdims=True)
        routed = jnp.broadcast_to(jnp.where(routed, 1.0, 0.0), (SLOT, count))
        rank = dot(routed.astype(BF16), upper) - 1.0
        placed = jnp.where(rank == slot, routed, 0.0)
        column = jnp.sum(placed * weight, axis=1, keepdims=True)
        pays[w][:, 2 * model :] = jnp.where(lane == 0, column, 0.0).astype(BF16)
        placed = placed.astype(BF16)
        firsts.append(placed)
        placed_ref[w] = jnp.concatenate([placed] * CHIPS, axis=0)
    out_copies = []
    for p in range(2):
        for n in range(len(stored)):
            weight_copies[3 * p + n].wait()
        some = pl.ds(p * piece, piece)
        out_copies += fetch([(joined.at[some], all_ref.at[some])], sems, 9 + 2 * PARTS + p)
    for part in range(2):
        for p in range(PARTS):
            large[part * PARTS + p].wait()
        for w in range(flight):
            chosen = dot(firsts[w], data[part]).astype(BF16)
            for b in range(rep):
                rows[b] = chosen[:, b * width : (b + 1) * width]
            for k in range(rep):
                n = 2 * k + part
                pays[w][:, n * width : (n + 1) * width] = rows[jnp.bitwise_xor(r, k)]
    for copy in out_copies:
        copy.wait()


def half_kernel(start, all_ref, half_ref):
    half_ref[...] = all_ref[start : start + half_ref.shape[0]]


def hidden_kernel(rep, count, spans, cap_ref, *refs):
    blocks, pieces = refs[: 2 * count], refs[2 * count : 2 * count + len(spans)]
    outs, cap, sem = refs[2 * count + len(spans) : -2], refs[-2], refs[-1]
    own_ref, other_ref, grads_ref, here_ref, away_refs = *outs[:4], outs[4:]
    cap_copy = pltpu.make_async_copy(cap_ref, cap, sem)
    cap_copy.start()
    width = here_ref.shape[2]
    units = pieces[0].shape[1] // 3
    own_rows = count * SLOT
    r = lax.axis_index("rep")
    e = lax.axis_index("ep")
    mine = e // SPLIT
    inputs = [[], []]
    for k in range(rep):
        for part in range(2):
            n = 2 * k + part
            chosen = [b[:, n * width : (n + 1) * width] for b in blocks]
            chosen = jnp.concatenate(chosen, axis=0)
            inputs[part].append(chosen)
            if k == 0:
                here_ref[part] = chosen
            else:
                some = slice(part * own_rows, (part + 1) * own_rows)
                away_refs[k - 1][some, :width] = chosen[:own_rows]
    sum_x, sum_d = 0.0, 0.0
    for (k, start, stop), piece in zip(spans, pieces):
        sum_x = sum_x + dot(inputs[0][k][:, start:stop], piece[:, : 2 * units])
        sum_d = sum_d + dot(inputs[1][k][:, start:stop], piece[:, 2 * units :])

    cap_copy.wait()
    capacity = (BLOCK * cap[mine, r]).astype(F32)
    lane = iota((SLOT, LANES), 1)
    sources, rates, counts = [], [], []
    for n in range(2 * count):
        sources.append(jnp.bitwise_xor(e, CORES * turned(n % count) + n // count))
        rate = jnp.where(lane == 0, blocks[n][:, 2 * rep * width :].astype(F32), 0.0)
        rate = jnp.sum(rate, axis=1, keepdims=True)
        rates.append(rate)
        counts.append(jnp.sum(jnp.where(rate > 0.0, 1.0, 0.0), axis=0, keepdims=True))
    slot = iota((SLOT, 1), 0).astype(F32)
    rate_rows, kept_rows = [], []
    for n in range(2 * count):
        start = jnp.zeros((1, 1), F32)
        for other in range(2 * count):
            start = start + jnp.where(sources[other] < sources[n], counts[other], 0.0)
        kept = jnp.where((rates[n] > 0.0) & (start + slot < capacity), 1.0, 0.0)
        kept_rows.append(kept)
        rate_rows.append(rates[n] * kept)
    rate = jnp.concatenate(rate_rows, axis=0)
    kept = jnp.concatenate(kept_rows, axis=0)

    pre_gate, pre_up, back_hidden = sum_x[:, :units], sum_x[:, units:], sum_d
    sig = 1.0 / (1.0 + jnp.exp(-pre_gate))
    activated = pre_gate * sig
    hidden = activated * pre_up
    score = jnp.sum(hidden * back_hidden, axis=1, keepdims=True) * kept
    lane = iota((2 * own_rows, LANES), 1)
    scores = jnp.where(lane == e % CORES, score, 0.0).astype(BF16)
    scaled = back_hidden * rate
    gate_grad = (scaled * pre_up * sig * (1.0 + pre_gate * (1.0 - sig))).astype(BF16)
    up_grad = (scaled * activated).astype(BF16)
    weighted = (hidden * rate).astype(BF16)
    grads_ref[...] = jnp.concatenate([gate_grad, up_grad, weighted], axis=1)
    for ref in away_refs:
        ref[:, width:] = grads_ref[...]
    pair = jnp.concatenate([gate_grad, up_grad], axis=1)
    for (k, start, stop), piece in zip(spans, pieces):
        back = dot(pair, piece[:, : 2 * units], ((1,), (1,))).astype(BF16)
        some = slice(k * width + start, k * width + stop)
        own_ref[:, some] = back[:own_rows]
        other_ref[:, some] = back[own_rows:]
    own_ref[:, rep * width :] = scores[:own_rows]
    other_ref[:, rep * width :] = scores[own_rows:]


def sum_kernel(own_ref, got_ref, *outs):
    for j, out in enumerate(outs):
        some = slice(j * SLOT, (j + 1) * SLOT)
        out[...] = (own_ref[some].astype(F32) + got_ref[some].astype(F32)).astype(BF16)


def stack_kernel(*refs):
    for k, ref in enumerate(refs[:-1]):
        refs[-1][k] = ref[:, : refs[-1].shape[2]]


def weight_kernel(rep, here_ref, grads_ref, other_ref, *refs):
    away, outs, held, sems = refs[: rep - 1], refs[rep - 1 : -4], refs[-4:-1], refs[-1]
    units = outs[0].shape[1]
    width = here_ref.shape[2]
    half = grads_ref.shape[0] // 2
    copies = []
    for part, columns in enumerate((slice(0, 2 * units), slice(2 * units, 3 * units))):
        some = slice(part * half, (part + 1) * half)
        rows = [here_ref[part]]
        got = [grads_ref[:, columns]]
        for k, ref in enumerate(away):
            rows += [ref[some, :width], other_ref[k, some]]
            got.append(ref[:, width + columns.start : width + columns.stop])
        rows = jnp.concatenate(rows, axis=0)
        got = jnp.concatenate(got, axis=0)
        total = dot(got, rows, ((0,), (0,)))
        for n in range(total.shape[0] // units):
            held[2 * part + n][...] = total[n * units : (n + 1) * units].T.astype(BF16)
            copies += fetch([(held[2 * part + n], outs[2 * part + n])], sems, 2 * part + n)
    for copy in copies:
        copy.wait()


def token_kernel(rep, flight, ids_ref, placed_ref, *refs):
    backs, rest = refs[: flight * CHIPS], refs[flight * CHIPS :]
    out_ref, weight_ref, blocks, ids, sems = rest
    (ids_copy,) = fetch([(ids_ref, ids)], sems)
    r = lax.axis_index("rep")
    mine = lax.axis_index("ep") // SPLIT
    spacing = EXPERTS // flight
    width = out_ref.shape[1] // rep
    joined = [
        jnp.concatenate([b[...] for b in backs[w * CHIPS : (w + 1) * CHIPS]], axis=0)
        for w in range(flight)
    ]
    for k in range(rep):
        total = 0.0
        for w in range(flight):
            some = joined[w][:, k * width : (k + 1) * width]
            total = total + dot(placed_ref[w], some, ((0,), (0,)))
        blocks[jnp.bitwise_xor(r, k)] = total.astype(BF16)
    for b in range(rep):
        out_ref[:, b * width : (b + 1) * width] = blocks[b]
    result = jnp.zeros(weight_ref.shape, F32)
    ids_copy.wait()
    for w in range(flight):
        score = dot(joined[w][:, rep * width :], placed_ref[w], ((0,), (0,)))
        score = jnp.sum(score, axis=0, keepdims=True)
        match = ids[...] == jnp.bitwise_xor(mine, w) * spacing
        result = result + jnp.where(match, score, 0.0)
    weight_ref[...] = result


def local(
    tokens, out_grad, expert_ids, route_weight, live_count, cap_blocks, w_gate, w_up, w_down_t
):
    rep = lax.axis_size("rep")
    ep = lax.axis_size("ep")
    far = rep // 2
    flight = ep // SPLIT
    count = ep // CORES
    tok_count, model_dim = tokens.shape
    width, units = w_gate.shape
    rows = count * SLOT
    ids_rows, rw_rows, caps = expert_ids.T, route_weight.T, cap_blocks.T

    def send(array, rep_bits, ep_bits):
        mask = rep_bits * ep + ep_bits
        pairs = [(a, a ^ mask) for a in range(rep * ep)]
        return lax.ppermute(array, ("rep", "ep"), pairs)

    def after(array, *others):
        return lax.optimization_barrier((array,) + others)[0]

    packed = call(
        functools.partial(pack_kernel, rep, flight),
        [shape((SLOT, 2 * model_dim + LANES))] * flight
        + [shape((flight, CHIPS * SLOT, tok_count)), shape((width, 3 * units))],
        [live_count, tokens, out_grad, ids_rows, rw_rows, w_gate, w_up, w_down_t],
        stored=range(8),
        kept=(flight + 1,),
        scratch=[
            pltpu.SMEM(live_count.shape, jnp.int32),
            pltpu.VMEM(ids_rows.shape, jnp.int32),
            pltpu.VMEM(rw_rows.shape, BF16),
            pltpu.VMEM((2, tok_count, model_dim), BF16),
            pltpu.VMEM((rep, SLOT, width), BF16),
            pltpu.VMEM((width, 3 * units), BF16),
            pltpu.SemaphoreType.DMA((2 * PARTS + 11,)),
        ],
        grant=54,
    )
    pays, placed, weights = packed[:flight], packed[flight], packed[flight + 1]

    half = width // 2
    whole = {0: weights}
    halves = {}
    for k in range(1, rep):
        low, high = k & -k, 1 << (k.bit_length() - 1)
        if low == high:
            whole[k] = send(weights, k, 0)
            for h in range(2):
                kernel = functools.partial(half_kernel, h * half)
                (halves[k, h],) = call(kernel, [shape((half, 3 * units))], [whole[k]])
        else:
            halves[k, 0] = send(halves[k ^ low, 0], low, 0)
            halves[k, 1] = send(halves[k ^ high, 1], high, 0)
    spans, pieces = [], []
    for k in range(rep):
        if k in whole:
            spans.append((k, 0, width))
            pieces.append(whole[k])
        else:
            spans += [(k, 0, half), (k, half, width)]
            pieces += [halves[k, 0], halves[k, 1]]

    order = [turned(n) for n in range(count)]
    blocks = [send(pays[j // CHIPS], 0, CORES * j) if j else pays[0] for j in order]
    nearest = blocks[order.index(1)]
    ready = [after(b, nearest) if j == 0 else b for j, b in zip(order, blocks)]
    blocks = blocks + [send(block, 0, 1) for block in ready]
    results = call(
        functools.partial(hidden_kernel, rep, count, tuple(spans)),
        [shape((rows, model_dim + LANES))] * 2
        + [shape((2 * rows, 3 * units)), shape((2, 2 * rows, width))]
        + [shape((2 * rows, width + 3 * units))] * (rep - 1),
        [caps] + blocks + pieces,
        stored=(0,),
        scratch=[pltpu.SMEM(caps.shape, jnp.int32), pltpu.SemaphoreType.DMA(())],
        flops=2 * 2 * rows * model_dim * 5 * units,
    )
    own, other, grads, here, away = *results[:4], results[4:]
    summed = call(sum_kernel, [shape((SLOT, model_dim + LANES))] * count, [own, send(other, 0, 1)])
    backs = [send(part, 0, CORES * j) if j else part for j, part in zip(order, summed)]

    moved = [
        send(part if k & (k - 1) else after(part, summed[-2]), k, 0) for k, part in enumerate(away, 1)
    ]
    (own_rows,) = call(stack_kernel, [shape((rep - 1, 2 * rows, width))], moved)
    other_rows = send(own_rows, 0, 1)
    grad_gate, grad_up, grad_down = call(
        functools.partial(weight_kernel, rep),
        [shape((width, units))] * 3,
        [here, grads, other_rows] + moved,
        kept=(0, 1, 2),
        scratch=[pltpu.VMEM((width, units), BF16)] * 3 + [pltpu.SemaphoreType.DMA((3,))],
        flops=2 * 2 * rep * rows * width * 3 * units,
    )
    grad_tokens, grad_weight = call(
        functools.partial(token_kernel, rep, flight),
        [shape((tok_count, model_dim)), shape(ids_rows.shape, F32)],
        [ids_rows, placed] + backs,
        stored=(0,),
        scratch=[
            pltpu.VMEM((rep, tok_count, width), BF16),
            pltpu.VMEM(ids_rows.shape, jnp.int32),
            pltpu.SemaphoreType.DMA((1,)),
        ],
        flops=1000 * 2 * tok_count * CHIPS * SLOT * model_dim,
    )
    return grad_tokens, grad_weight.T, grad_gate, grad_up, grad_down


def solution(mesh):
    return jax.shard_map(
        local,
        mesh=mesh,
        in_specs=(
            P(("rep", "ep"), None),
            P(("rep", "ep"), None),
            P(("rep", "ep"), None),
            P(("rep", "ep"), None),
            P(),
            P(),
            P("rep", "ep"),
            P("rep", "ep"),
            P("rep", "ep"),
        ),
        out_specs=(
            P(("rep", "ep"), None),
            P(("rep", "ep"), None),
            P("rep", "ep"),
            P("rep", "ep"),
            P("rep", "ep"),
        ),
        check_vma=False,
    )
```

```python
import functools

import jax
import jax.numpy as jnp
from jax import lax
from jax.experimental import pallas as pl
from jax.experimental.pallas import tpu as pltpu
from jax.sharding import PartitionSpec as P

EXPERTS = 128
SLOT = 16
BLOCK = 128
SPLIT = 8
CORES = 2
CHIPS = SPLIT // CORES
LANES = 128
F32 = jnp.float32
BF16 = jnp.bfloat16
PARTS = 4
HBM = pl.BlockSpec(memory_space=pltpu.HBM)
VMEM = pl.BlockSpec(memory_space=pltpu.VMEM)


def shape(dims, kind=BF16):
    return jax.ShapeDtypeStruct(dims, kind)


def call(kernel, outs, args, stored=(), kept=(), scratch=(), flops=0, grant=16):
    size = sum(a.size * a.dtype.itemsize for a in args) + sum(
        o.size * o.dtype.itemsize for o in outs
    )
    return pl.pallas_call(
        kernel,
        out_shape=tuple(outs),
        in_specs=[HBM if n in stored else VMEM for n in range(len(args))],
        out_specs=tuple([HBM if n in kept else VMEM for n in range(len(outs))]),
        scratch_shapes=scratch,
        compiler_params=pltpu.CompilerParams(vmem_limit_bytes=grant * 1024 * 1024),
        cost_estimate=pl.CostEstimate(flops=flops, bytes_accessed=size, transcendentals=0),
    )(*args)


def fetch(pairs, sems, first=0):
    copies = [
        pltpu.make_async_copy(source, target, sems.at[first + n])
        for n, (source, target) in enumerate(pairs)
    ]
    for copy in copies:
        copy.start()
    return copies


def dot(a, b, dims=((1,), (0,))):
    return lax.dot_general(a, b, (dims, ((), ())), preferred_element_type=F32)


def iota(dims, axis):
    return lax.broadcasted_iota(jnp.int32, dims, axis)


def turned(n):
    return n ^ (CHIPS - 1)


def pack_kernel(rep, flight, live_ref, tok_ref, grad_ref, ids_ref, rw_ref, *refs):
    stored, pays, placed_ref, all_ref = refs[:3], refs[3 : 3 + flight], refs[-9], refs[-8]
    live, ids_held, rw_held, data, rows, joined, sems = refs[-7:]
    r = lax.axis_index("rep")
    mine = lax.axis_index("ep") // SPLIT
    count, model = tok_ref.shape
    width = model // rep
    spacing = EXPERTS // flight
    small = fetch([(live_ref, live), (ids_ref, ids_held), (rw_ref, rw_held)], sems)
    units = stored[0].shape[1]
    piece = width // 2
    pairs = []
    for p in range(2):
        some = pl.ds(p * piece, piece)
        for n, ref in enumerate(stored):
            pairs.append((ref.at[some], joined.at[some, pl.ds(n * units, units)]))
    weight_copies = fetch(pairs, sems, 3)
    pairs = []
    for part, ref in enumerate((tok_ref, grad_ref)):
        for p in range(PARTS):
            some = pl.ds(p * (count // PARTS), count // PARTS)
            pairs.append((ref.at[some], data.at[part, some]))
    large = fetch(pairs, sems, 9)
    for copy in small:
        copy.wait()
    token = iota((1, count), 1)
    upper = (iota((count, count), 0) <= iota((count, count), 1)).astype(BF16)
    slot = iota((SLOT, count), 0).astype(F32)
    lane = iota((SLOT, LANES), 1)
    ids = ids_held[...]
    weights = rw_held[...].astype(F32)
    firsts = []
    for w in range(flight):
        expert = jnp.bitwise_xor(mine, w)
        match = ids == expert * spacing
        routed = jnp.any(match, axis=0, keepdims=True) & (token < live[r])
        weight = jnp.sum(jnp.where(match, weights, 0.0), axis=0, keepdims=True)
        routed = jnp.broadcast_to(jnp.where(routed, 1.0, 0.0), (SLOT, count))
        rank = dot(routed.astype(BF16), upper) - 1.0
        placed = jnp.where(rank == slot, routed, 0.0)
        column = jnp.sum(placed * weight, axis=1, keepdims=True)
        pays[w][:, 2 * model :] = jnp.where(lane == 0, column, 0.0).astype(BF16)
        placed = placed.astype(BF16)
        firsts.append(placed)
        placed_ref[w] = jnp.concatenate([placed] * CHIPS, axis=0)
    out_copies = []
    for p in range(2):
        for n in range(len(stored)):
            weight_copies[3 * p + n].wait()
        some = pl.ds(p * piece, piece)
        out_copies += fetch([(joined.at[some], all_ref.at[some])], sems, 9 + 2 * PARTS + p)
    for part in range(2):
        for p in range(PARTS):
            large[part * PARTS + p].wait()
        for w in range(flight):
            chosen = dot(firsts[w], data[part]).astype(BF16)
            for b in range(rep):
                rows[b] = chosen[:, b * width : (b + 1) * width]
            for k in range(rep):
                n = 2 * k + part
                pays[w][:, n * width : (n + 1) * width] = rows[jnp.bitwise_xor(r, k)]
    for copy in out_copies:
        copy.wait()


def near_groups(rep):
    return [k for k in range(1, rep) if k & (k - 1) == 0]


def far_groups(rep):
    return [k for k in range(1, rep) if k & (k - 1)]


def columns_kernel(groups, count, *refs):
    blocks, outs = refs[:count], refs[count:]
    rows, width = count * SLOT, outs[0].shape[1]
    for k, out in zip(groups, outs):
        for part in range(2):
            n = 2 * k + part
            for j in range(count):
                start = part * rows + j * SLOT
                out[start : start + SLOT] = blocks[j][:, n * width : (n + 1) * width]


def half_kernel(start, all_ref, half_ref):
    half_ref[...] = all_ref[start : start + half_ref.shape[0]]


def hidden_kernel(rep, count, spans, cap_ref, *refs):
    blocks, pieces = refs[: 2 * count], refs[2 * count : 2 * count + len(spans)]
    outs, cap, sem = refs[2 * count + len(spans) : -2], refs[-2], refs[-1]
    own_ref, other_ref, grads_ref, here_ref, away_refs = *outs[:4], outs[4:]
    far = far_groups(rep)
    cap_copy = pltpu.make_async_copy(cap_ref, cap, sem)
    cap_copy.start()
    width = here_ref.shape[2]
    units = pieces[0].shape[1] // 3
    own_rows = count * SLOT
    r = lax.axis_index("rep")
    e = lax.axis_index("ep")
    mine = e // SPLIT
    inputs = [[], []]
    for k in range(rep):
        for part in range(2):
            n = 2 * k + part
            chosen = [b[:, n * width : (n + 1) * width] for b in blocks]
            chosen = jnp.concatenate(chosen, axis=0)
            inputs[part].append(chosen)
            if k == 0:
                here_ref[part] = chosen
            elif k in far:
                some = slice(part * own_rows, (part + 1) * own_rows)
                away_refs[far.index(k)][some, :width] = chosen[:own_rows]
    sum_x, sum_d = 0.0, 0.0
    for (k, start, stop), piece in zip(spans, pieces):
        sum_x = sum_x + dot(inputs[0][k][:, start:stop], piece[:, : 2 * units])
        sum_d = sum_d + dot(inputs[1][k][:, start:stop], piece[:, 2 * units :])

    cap_copy.wait()
    capacity = (BLOCK * cap[mine, r]).astype(F32)
    lane = iota((SLOT, LANES), 1)
    sources, rates, counts = [], [], []
    for n in range(2 * count):
        sources.append(jnp.bitwise_xor(e, CORES * turned(n % count) + n // count))
        rate = jnp.where(lane == 0, blocks[n][:, 2 * rep * width :].astype(F32), 0.0)
        rate = jnp.sum(rate, axis=1, keepdims=True)
        rates.append(rate)
        counts.append(jnp.sum(jnp.where(rate > 0.0, 1.0, 0.0), axis=0, keepdims=True))
    slot = iota((SLOT, 1), 0).astype(F32)
    rate_rows, kept_rows = [], []
    for n in range(2 * count):
        start = jnp.zeros((1, 1), F32)
        for other in range(2 * count):
            start = start + jnp.where(sources[other] < sources[n], counts[other], 0.0)
        kept = jnp.where((rates[n] > 0.0) & (start + slot < capacity), 1.0, 0.0)
        kept_rows.append(kept)
        rate_rows.append(rates[n] * kept)
    rate = jnp.concatenate(rate_rows, axis=0)
    kept = jnp.concatenate(kept_rows, axis=0)

    pre_gate, pre_up, back_hidden = sum_x[:, :units], sum_x[:, units:], sum_d
    sig = 1.0 / (1.0 + jnp.exp(-pre_gate))
    activated = pre_gate * sig
    hidden = activated * pre_up
    score = jnp.sum(hidden * back_hidden, axis=1, keepdims=True) * kept
    lane = iota((2 * own_rows, LANES), 1)
    scores = jnp.where(lane == e % CORES, score, 0.0).astype(BF16)
    scaled = back_hidden * rate
    gate_grad = (scaled * pre_up * sig * (1.0 + pre_gate * (1.0 - sig))).astype(BF16)
    up_grad = (scaled * activated).astype(BF16)
    weighted = (hidden * rate).astype(BF16)
    grads_ref[...] = jnp.concatenate([gate_grad, up_grad, weighted], axis=1)
    for ref in away_refs:
        ref[:, width:] = grads_ref[...]
    pair = jnp.concatenate([gate_grad, up_grad], axis=1)
    for (k, start, stop), piece in zip(spans, pieces):
        back = dot(pair, piece[:, : 2 * units], ((1,), (1,))).astype(BF16)
        some = slice(k * width + start, k * width + stop)
        own_ref[:, some] = back[:own_rows]
        other_ref[:, some] = back[own_rows:]
    own_ref[:, rep * width :] = scores[:own_rows]
    other_ref[:, rep * width :] = scores[own_rows:]


def sum_kernel(own_ref, got_ref, *outs):
    for j, out in enumerate(outs):
        some = slice(j * SLOT, (j + 1) * SLOT)
        out[...] = (own_ref[some].astype(F32) + got_ref[some].astype(F32)).astype(BF16)


def stack_kernel(*refs):
    for k, ref in enumerate(refs[:-1]):
        refs[-1][k] = ref[:, : refs[-1].shape[2]]


def weight_kernel(rep, here_ref, grads_ref, near_ref, near_other, far_other, *refs):
    near, far = len(near_groups(rep)), len(far_groups(rep))
    near_grads, away, outs = refs[:near], refs[near : near + far], refs[near + far : -4]
    held, sems = refs[-4:-1], refs[-1]
    units = outs[0].shape[1]
    width = here_ref.shape[2]
    half = grads_ref.shape[0] // 2
    copies = []
    for part, columns in enumerate((slice(0, 2 * units), slice(2 * units, 3 * units))):
        some = slice(part * half, (part + 1) * half)
        rows = [here_ref[part]]
        got = [grads_ref[:, columns]]
        for k, ref in enumerate(near_grads):
            rows += [near_ref[k, some], near_other[k, some]]
            got.append(ref[:, columns])
        for k, ref in enumerate(away):
            rows += [ref[some, :width], far_other[k, some]]
            got.append(ref[:, width + columns.start : width + columns.stop])
        rows = jnp.concatenate(rows, axis=0)
        got = jnp.concatenate(got, axis=0)
        total = dot(got, rows, ((0,), (0,)))
        for n in range(total.shape[0] // units):
            held[2 * part + n][...] = total[n * units : (n + 1) * units].T.astype(BF16)
            copies += fetch([(held[2 * part + n], outs[2 * part + n])], sems, 2 * part + n)
    for copy in copies:
        copy.wait()


def token_kernel(rep, flight, ids_ref, placed_ref, *refs):
    backs, rest = refs[: flight * CHIPS], refs[flight * CHIPS :]
    out_ref, weight_ref, blocks, ids, sems = rest
    (ids_copy,) = fetch([(ids_ref, ids)], sems)
    r = lax.axis_index("rep")
    mine = lax.axis_index("ep") // SPLIT
    spacing = EXPERTS // flight
    width = out_ref.shape[1] // rep
    joined = [
        jnp.concatenate([b[...] for b in backs[w * CHIPS : (w + 1) * CHIPS]], axis=0)
        for w in range(flight)
    ]
    for k in range(rep):
        total = 0.0
        for w in range(flight):
            some = joined[w][:, k * width : (k + 1) * width]
            total = total + dot(placed_ref[w], some, ((0,), (0,)))
        blocks[jnp.bitwise_xor(r, k)] = total.astype(BF16)
    for b in range(rep):
        out_ref[:, b * width : (b + 1) * width] = blocks[b]
    result = jnp.zeros(weight_ref.shape, F32)
    ids_copy.wait()
    for w in range(flight):
        score = dot(joined[w][:, rep * width :], placed_ref[w], ((0,), (0,)))
        score = jnp.sum(score, axis=0, keepdims=True)
        match = ids[...] == jnp.bitwise_xor(mine, w) * spacing
        result = result + jnp.where(match, score, 0.0)
    weight_ref[...] = result


def local(
    tokens, out_grad, expert_ids, route_weight, live_count, cap_blocks, w_gate, w_up, w_down_t
):
    rep = lax.axis_size("rep")
    ep = lax.axis_size("ep")
    far = rep // 2
    flight = ep // SPLIT
    count = ep // CORES
    tok_count, model_dim = tokens.shape
    width, units = w_gate.shape
    rows = count * SLOT
    ids_rows, rw_rows, caps = expert_ids.T, route_weight.T, cap_blocks.T

    def send(array, rep_bits, ep_bits):
        mask = rep_bits * ep + ep_bits
        pairs = [(a, a ^ mask) for a in range(rep * ep)]
        return lax.ppermute(array, ("rep", "ep"), pairs)

    def after(array, *others):
        return lax.optimization_barrier((array,) + others)[0]

    packed = call(
        functools.partial(pack_kernel, rep, flight),
        [shape((SLOT, 2 * model_dim + LANES))] * flight
        + [shape((flight, CHIPS * SLOT, tok_count)), shape((width, 3 * units))],
        [live_count, tokens, out_grad, ids_rows, rw_rows, w_gate, w_up, w_down_t],
        stored=range(8),
        kept=(flight + 1,),
        scratch=[
            pltpu.SMEM(live_count.shape, jnp.int32),
            pltpu.VMEM(ids_rows.shape, jnp.int32),
            pltpu.VMEM(rw_rows.shape, BF16),
            pltpu.VMEM((2, tok_count, model_dim), BF16),
            pltpu.VMEM((rep, SLOT, width), BF16),
            pltpu.VMEM((width, 3 * units), BF16),
            pltpu.SemaphoreType.DMA((2 * PARTS + 11,)),
        ],
        grant=54,
    )
    pays, placed, weights = packed[:flight], packed[flight], packed[flight + 1]

    half = width // 2
    whole = {0: weights}
    halves, sent = {}, []
    for k in range(1, rep):
        low, high = k & -k, 1 << (k.bit_length() - 1)
        if low == high:
            whole[k] = send(weights, k, 0)
            for h in range(2):
                kernel = functools.partial(half_kernel, h * half)
                (halves[k, h],) = call(kernel, [shape((half, 3 * units))], [whole[k]])
                sent.append(halves[k, h])
        else:
            halves[k, 0] = send(halves[k ^ low, 0], low, 0)
            halves[k, 1] = send(halves[k ^ high, 1], high, 0)
    spans, pieces = [], []
    for k in range(rep):
        if k in whole:
            spans.append((k, 0, width))
            pieces.append(whole[k])
        else:
            spans += [(k, 0, half), (k, half, width)]
            pieces += [halves[k, 0], halves[k, 1]]

    order = [turned(n) for n in range(count)]
    blocks = [send(pays[j // CHIPS], 0, CORES * j) if j else pays[0] for j in order]
    near, far = near_groups(rep), far_groups(rep)
    columns = call(
        functools.partial(columns_kernel, near, count),
        [shape((2 * rows, width))] * len(near),
        [after(blocks[0], *sent)] + blocks[1:],
    )
    nearest = blocks[order.index(1)]
    ready = [after(b, nearest) if j == 0 else b for j, b in zip(order, blocks)]
    blocks = blocks + [send(block, 0, 1) for block in ready]
    results = call(
        functools.partial(hidden_kernel, rep, count, tuple(spans)),
        [shape((rows, model_dim + LANES))] * 2
        + [shape((2 * rows, 3 * units)), shape((2, 2 * rows, width))]
        + [shape((2 * rows, width + 3 * units))] * len(far_groups(rep)),
        [caps] + blocks + pieces,
        stored=(0,),
        scratch=[pltpu.SMEM(caps.shape, jnp.int32), pltpu.SemaphoreType.DMA(())],
        flops=2 * 2 * rows * model_dim * 5 * units,
    )
    own, other, grads, here, away = *results[:4], results[4:]
    moved = [send(part, k, 0) for k, part in zip(near, columns)]
    (near_rows,) = call(
        stack_kernel,
        [shape((len(near), 2 * rows, width))],
        moved,
        flops=32000 * rows * width,
    )
    near_other = send(near_rows, 0, 1)
    summed = call(
        sum_kernel,
        [shape((SLOT, model_dim + LANES))] * count,
        [after(own, near_rows), send(other, 0, 1)],
        flops=2 * rows * model_dim,
    )
    backs = [send(part, 0, CORES * j) if j else part for j, part in zip(order, summed)]

    moved = [send(after(part, summed[-2]), k, 0) for k, part in zip(far, away)]
    (far_rows,) = call(stack_kernel, [shape((len(far), 2 * rows, width))], moved)
    far_other = send(far_rows, 0, 1)
    late = after(grads, near_other)
    near_grads = [send(late, k, 0) for k in near]
    grad_gate, grad_up, grad_down = call(
        functools.partial(weight_kernel, rep),
        [shape((width, units))] * 3,
        [here, grads, near_rows, near_other, far_other] + near_grads + moved,
        kept=(0, 1, 2),
        scratch=[pltpu.VMEM((width, units), BF16)] * 3 + [pltpu.SemaphoreType.DMA((3,))],
        flops=2 * 2 * rep * rows * width * 3 * units,
    )
    grad_tokens, grad_weight = call(
        functools.partial(token_kernel, rep, flight),
        [shape((tok_count, model_dim)), shape(ids_rows.shape, F32)],
        [ids_rows, placed] + backs,
        stored=(0,),
        scratch=[
            pltpu.VMEM((rep, tok_count, width), BF16),
            pltpu.VMEM(ids_rows.shape, jnp.int32),
            pltpu.SemaphoreType.DMA((1,)),
        ],
        flops=1000 * 2 * tok_count * CHIPS * SLOT * model_dim,
    )
    return grad_tokens, grad_weight.T, grad_gate, grad_up, grad_down


def solution(mesh):
    return jax.shard_map(
        local,
        mesh=mesh,
        in_specs=(
            P(("rep", "ep"), None),
            P(("rep", "ep"), None),
            P(("rep", "ep"), None),
            P(("rep", "ep"), None),
            P(),
            P(),
            P("rep", "ep"),
            P("rep", "ep"),
            P("rep", "ep"),
        ),
        out_specs=(
            P(("rep", "ep"), None),
            P(("rep", "ep"), None),
            P("rep", "ep"),
            P("rep", "ep"),
            P("rep", "ep"),
        ),
        check_vma=False,
    )
```

```python
import functools

import jax
import jax.numpy as jnp
from jax import lax
from jax.experimental import pallas as pl
from jax.experimental.pallas import tpu as pltpu
from jax.sharding import PartitionSpec as P

EXPERTS = 128
SLOT = 16
BLOCK = 128
SPLIT = 8
CORES = 2
CHIPS = SPLIT // CORES
LANES = 128
F32 = jnp.float32
BF16 = jnp.bfloat16
PARTS = 4
HBM = pl.BlockSpec(memory_space=pltpu.HBM)
VMEM = pl.BlockSpec(memory_space=pltpu.VMEM)


def shape(dims, kind=BF16):
    return jax.ShapeDtypeStruct(dims, kind)


def call(kernel, outs, args, stored=(), kept=(), scratch=(), flops=0, grant=16):
    size = sum(a.size * a.dtype.itemsize for a in args) + sum(
        o.size * o.dtype.itemsize for o in outs
    )
    return pl.pallas_call(
        kernel,
        out_shape=tuple(outs),
        in_specs=[HBM if n in stored else VMEM for n in range(len(args))],
        out_specs=tuple([HBM if n in kept else VMEM for n in range(len(outs))]),
        scratch_shapes=scratch,
        compiler_params=pltpu.CompilerParams(vmem_limit_bytes=grant * 1024 * 1024),
        cost_estimate=pl.CostEstimate(flops=flops, bytes_accessed=size, transcendentals=0),
    )(*args)


def fetch(pairs, sems, first=0):
    copies = [
        pltpu.make_async_copy(source, target, sems.at[first + n])
        for n, (source, target) in enumerate(pairs)
    ]
    for copy in copies:
        copy.start()
    return copies


def dot(a, b, dims=((1,), (0,))):
    return lax.dot_general(a, b, (dims, ((), ())), preferred_element_type=F32)


def iota(dims, axis):
    return lax.broadcasted_iota(jnp.int32, dims, axis)


def turned(n):
    return n ^ (CHIPS - 1)


def pack_kernel(rep, flight, live_ref, tok_ref, grad_ref, ids_ref, rw_ref, *refs):
    stored, pays, placed_ref, all_ref = refs[:3], refs[3 : 3 + flight], refs[-9], refs[-8]
    live, ids_held, rw_held, data, rows, joined, sems = refs[-7:]
    r = lax.axis_index("rep")
    mine = lax.axis_index("ep") // SPLIT
    count, model = tok_ref.shape
    width = model // rep
    spacing = EXPERTS // flight
    small = fetch([(live_ref, live), (ids_ref, ids_held), (rw_ref, rw_held)], sems)
    units = stored[0].shape[1]
    piece = width // 2
    pairs = []
    for p in range(2):
        some = pl.ds(p * piece, piece)
        for n, ref in enumerate(stored):
            pairs.append((ref.at[some], joined.at[some, pl.ds(n * units, units)]))
    weight_copies = fetch(pairs, sems, 3)
    pairs = []
    for part, ref in enumerate((tok_ref, grad_ref)):
        for p in range(PARTS):
            some = pl.ds(p * (count // PARTS), count // PARTS)
            pairs.append((ref.at[some], data.at[part, some]))
    large = fetch(pairs, sems, 9)
    for copy in small:
        copy.wait()
    token = iota((1, count), 1)
    upper = (iota((count, count), 0) <= iota((count, count), 1)).astype(BF16)
    slot = iota((SLOT, count), 0).astype(F32)
    lane = iota((SLOT, LANES), 1)
    ids = ids_held[...]
    weights = rw_held[...].astype(F32)
    firsts = []
    for w in range(flight):
        expert = jnp.bitwise_xor(mine, w)
        match = ids == expert * spacing
        routed = jnp.any(match, axis=0, keepdims=True) & (token < live[r])
        weight = jnp.sum(jnp.where(match, weights, 0.0), axis=0, keepdims=True)
        routed = jnp.broadcast_to(jnp.where(routed, 1.0, 0.0), (SLOT, count))
        rank = dot(routed.astype(BF16), upper) - 1.0
        placed = jnp.where(rank == slot, routed, 0.0)
        column = jnp.sum(placed * weight, axis=1, keepdims=True)
        pays[w][:, 2 * model :] = jnp.where(lane == 0, column, 0.0).astype(BF16)
        placed = placed.astype(BF16)
        firsts.append(placed)
        placed_ref[w] = jnp.concatenate([placed] * CHIPS, axis=0)
    out_copies = []
    for p in range(2):
        for n in range(len(stored)):
            weight_copies[3 * p + n].wait()
        some = pl.ds(p * piece, piece)
        out_copies += fetch([(joined.at[some], all_ref.at[some])], sems, 9 + 2 * PARTS + p)
    for part in range(2):
        for p in range(PARTS):
            large[part * PARTS + p].wait()
        for w in range(flight):
            chosen = dot(firsts[w], data[part]).astype(BF16)
            for b in range(rep):
                rows[b] = chosen[:, b * width : (b + 1) * width]
            for k in range(rep):
                n = 2 * k + part
                pays[w][:, n * width : (n + 1) * width] = rows[jnp.bitwise_xor(r, k)]
    for copy in out_copies:
        copy.wait()


def columns_kernel(rep, count, *refs):
    blocks, odd_ref, outs = refs[:count], refs[count], refs[count + 1 :]
    rows, width = count * SLOT, odd_ref.shape[2]
    for k in range(1, rep):
        out = odd_ref.at[k // 2] if k % 2 else outs[k // 2 - 1]
        for part in range(2):
            n = 2 * k + part
            for j in range(count):
                start = part * rows + j * SLOT
                out[start : start + SLOT] = blocks[j][:, n * width : (n + 1) * width]


def split_kernel(all_ref, *outs):
    rows = outs[0].shape[0]
    for n, out in enumerate(outs):
        start = n % 2 * rows
        out[...] = all_ref[n // 2 + 1, start : start + rows]


def half_kernel(start, all_ref, half_ref):
    half_ref[...] = all_ref[start : start + half_ref.shape[0]]


def hidden_kernel(rep, count, spans, cap_ref, *refs):
    blocks, pieces = refs[: 2 * count], refs[2 * count : 2 * count + len(spans)]
    outs, cap, sem = refs[2 * count + len(spans) : -2], refs[-2], refs[-1]
    own_refs, other_refs, grads_ref, here_ref = outs[:2], outs[2:4], outs[4], outs[5]
    cap_copy = pltpu.make_async_copy(cap_ref, cap, sem)
    cap_copy.start()
    width = here_ref.shape[2]
    units = pieces[0].shape[1] // 3
    part_rows = count * SLOT // 2
    r = lax.axis_index("rep")
    e = lax.axis_index("ep")
    mine = e // SPLIT
    inputs = [[], []]
    for k in range(rep):
        for part in range(2):
            n = 2 * k + part
            chosen = [b[:, n * width : (n + 1) * width] for b in blocks]
            chosen = jnp.concatenate(chosen, axis=0)
            inputs[part].append(chosen)
            if k == 0:
                here_ref[part] = chosen
    sum_x, sum_d = 0.0, 0.0
    for (k, start, stop), piece in zip(spans, pieces):
        sum_x = sum_x + dot(inputs[0][k][:, start:stop], piece[:, : 2 * units])
        sum_d = sum_d + dot(inputs[1][k][:, start:stop], piece[:, 2 * units :])

    cap_copy.wait()
    capacity = (BLOCK * cap[mine, r]).astype(F32)
    lane = iota((SLOT, LANES), 1)
    sources, rates, counts = [], [], []
    for n in range(2 * count):
        sources.append(jnp.bitwise_xor(e, CORES * turned(n % count) + n // count))
        rate = jnp.where(lane == 0, blocks[n][:, 2 * rep * width :].astype(F32), 0.0)
        rate = jnp.sum(rate, axis=1, keepdims=True)
        rates.append(rate)
        counts.append(jnp.sum(jnp.where(rate > 0.0, 1.0, 0.0), axis=0, keepdims=True))
    slot = iota((SLOT, 1), 0).astype(F32)
    rate_rows, kept_rows = [], []
    for n in range(2 * count):
        start = jnp.zeros((1, 1), F32)
        for other in range(2 * count):
            start = start + jnp.where(sources[other] < sources[n], counts[other], 0.0)
        kept = jnp.where((rates[n] > 0.0) & (start + slot < capacity), 1.0, 0.0)
        kept_rows.append(kept)
        rate_rows.append(rates[n] * kept)
    rate = jnp.concatenate(rate_rows, axis=0)
    kept = jnp.concatenate(kept_rows, axis=0)

    pre_gate, pre_up, back_hidden = sum_x[:, :units], sum_x[:, units:], sum_d
    sig = 1.0 / (1.0 + jnp.exp(-pre_gate))
    activated = pre_gate * sig
    hidden = activated * pre_up
    score = jnp.sum(hidden * back_hidden, axis=1, keepdims=True) * kept
    lane = iota((4 * part_rows, LANES), 1)
    scores = jnp.where(lane == e % CORES, score, 0.0).astype(BF16)
    scaled = back_hidden * rate
    gate_grad = (scaled * pre_up * sig * (1.0 + pre_gate * (1.0 - sig))).astype(BF16)
    up_grad = (scaled * activated).astype(BF16)
    weighted = (hidden * rate).astype(BF16)
    grads_ref[...] = jnp.concatenate([gate_grad, up_grad, weighted], axis=1)
    pair = jnp.concatenate([gate_grad, up_grad], axis=1)
    for (k, start, stop), piece in zip(spans, pieces):
        back = dot(pair, piece[:, : 2 * units], ((1,), (1,))).astype(BF16)
        some = slice(k * width + start, k * width + stop)
        for n, ref in enumerate(own_refs + other_refs):
            ref[:, some] = back[n * part_rows : (n + 1) * part_rows]
    for n, ref in enumerate(own_refs + other_refs):
        ref[:, rep * width :] = scores[n * part_rows : (n + 1) * part_rows]


def sum_kernel(own_ref, got_ref, *outs):
    for j, out in enumerate(outs):
        some = slice(j * SLOT, (j + 1) * SLOT)
        out[...] = (own_ref[some].astype(F32) + got_ref[some].astype(F32)).astype(BF16)


def stack_kernel(odd_ref, *refs):
    out, count = refs[-1], len(refs) // 3
    rows = out.shape[1] // 2
    out[0] = odd_ref[0]
    for n in range(count):
        out[2 * n + 1] = refs[n][...]
        out[2 * n + 2, :rows] = refs[count + 2 * n][...]
        out[2 * n + 2, rows:] = refs[count + 2 * n + 1][...]


def weight_kernel(rep, here_ref, own_ref, other_ref, *refs):
    grads, outs, held, sems = refs[:-7], refs[-7:-4], refs[-4:-1], refs[-1]
    units = outs[0].shape[1]
    half = own_ref.shape[1] // 2
    copies = []
    for part, columns in enumerate((slice(0, 2 * units), slice(2 * units, 3 * units))):
        some = slice(part * half, (part + 1) * half)
        rows = [here_ref[part]]
        for k in range(rep - 1):
            rows += [own_ref[k, some], other_ref[k, some]]
        rows = jnp.concatenate(rows, axis=0)
        got = jnp.concatenate([ref[:, columns] for ref in grads], axis=0)
        total = dot(got, rows, ((0,), (0,)))
        for n in range(total.shape[0] // units):
            held[2 * part + n][...] = total[n * units : (n + 1) * units].T.astype(BF16)
            copies += fetch([(held[2 * part + n], outs[2 * part + n])], sems, 2 * part + n)
    for copy in copies:
        copy.wait()


def token_kernel(rep, flight, ids_ref, placed_ref, *refs):
    backs, rest = refs[: flight * CHIPS], refs[flight * CHIPS :]
    out_ref, weight_ref, blocks, ids, sems = rest
    (ids_copy,) = fetch([(ids_ref, ids)], sems)
    r = lax.axis_index("rep")
    mine = lax.axis_index("ep") // SPLIT
    spacing = EXPERTS // flight
    width = out_ref.shape[1] // rep
    joined = [
        jnp.concatenate([b[...] for b in backs[w * CHIPS : (w + 1) * CHIPS]], axis=0)
        for w in range(flight)
    ]
    for k in range(rep):
        total = 0.0
        for w in range(flight):
            some = joined[w][:, k * width : (k + 1) * width]
            total = total + dot(placed_ref[w], some, ((0,), (0,)))
        blocks[jnp.bitwise_xor(r, k)] = total.astype(BF16)
    for b in range(rep):
        out_ref[:, b * width : (b + 1) * width] = blocks[b]
    result = jnp.zeros(weight_ref.shape, F32)
    ids_copy.wait()
    for w in range(flight):
        score = dot(joined[w][:, rep * width :], placed_ref[w], ((0,), (0,)))
        score = jnp.sum(score, axis=0, keepdims=True)
        match = ids[...] == jnp.bitwise_xor(mine, w) * spacing
        result = result + jnp.where(match, score, 0.0)
    weight_ref[...] = result


def local(
    tokens, out_grad, expert_ids, route_weight, live_count, cap_blocks, w_gate, w_up, w_down_t
):
    rep = lax.axis_size("rep")
    ep = lax.axis_size("ep")
    far = rep // 2
    flight = ep // SPLIT
    count = ep // CORES
    tok_count, model_dim = tokens.shape
    width, units = w_gate.shape
    rows = count * SLOT
    ids_rows, rw_rows, caps = expert_ids.T, route_weight.T, cap_blocks.T

    def send(array, rep_bits, ep_bits):
        mask = rep_bits * ep + ep_bits
        pairs = [(a, a ^ mask) for a in range(rep * ep)]
        return lax.ppermute(array, ("rep", "ep"), pairs)

    def after(array, *others):
        return lax.optimization_barrier((array,) + others)[0]

    packed = call(
        functools.partial(pack_kernel, rep, flight),
        [shape((SLOT, 2 * model_dim + LANES))] * flight
        + [shape((flight, CHIPS * SLOT, tok_count)), shape((width, 3 * units))],
        [live_count, tokens, out_grad, ids_rows, rw_rows, w_gate, w_up, w_down_t],
        stored=range(8),
        kept=(flight + 1,),
        scratch=[
            pltpu.SMEM(live_count.shape, jnp.int32),
            pltpu.VMEM(ids_rows.shape, jnp.int32),
            pltpu.VMEM(rw_rows.shape, BF16),
            pltpu.VMEM((2, tok_count, model_dim), BF16),
            pltpu.VMEM((rep, SLOT, width), BF16),
            pltpu.VMEM((width, 3 * units), BF16),
            pltpu.SemaphoreType.DMA((2 * PARTS + 11,)),
        ],
        grant=54,
    )
    pays, placed, weights = packed[:flight], packed[flight], packed[flight + 1]

    half = width // 2
    whole = {0: weights}
    halves, sent = {}, []
    for k in range(1, rep):
        low, high = k & -k, 1 << (k.bit_length() - 1)
        if low == high:
            whole[k] = send(weights, k, 0)
            for h in range(2):
                kernel = functools.partial(half_kernel, h * half)
                (halves[k, h],) = call(kernel, [shape((half, 3 * units))], [whole[k]])
                sent.append(halves[k, h])
        else:
            halves[k, 0] = send(halves[k ^ low, 0], low, 0)
            halves[k, 1] = send(halves[k ^ high, 1], high, 0)
    spans, pieces = [], []
    for k in range(rep):
        if k in whole:
            spans.append((k, 0, width))
            pieces.append(whole[k])
        else:
            spans += [(k, 0, half), (k, half, width)]
            pieces += [halves[k, 0], halves[k, 1]]

    order = [turned(n) for n in range(count)]
    blocks = [send(pays[j // CHIPS], 0, CORES * j) if j else pays[0] for j in order]
    far = rep // 2
    odd, *even = call(
        functools.partial(columns_kernel, rep, count),
        [shape((far, 2 * rows, width))] + [shape((2 * rows, width))] * (far - 1),
        [after(blocks[0], *sent)] + blocks[1:],
    )
    odd = send(odd, 1, 0)
    even = [send(part, 2 * k, 0) for k, part in enumerate(even, 1)]
    nearest = blocks[order.index(1)]
    ready = [after(b, nearest) if j == 0 else b for j, b in zip(order, blocks)]
    blocks = blocks + [send(block, 0, 1) for block in ready]
    results = call(
        functools.partial(hidden_kernel, rep, count, tuple(spans)),
        [shape((rows // 2, model_dim + LANES))] * 4
        + [shape((2 * rows, 3 * units)), shape((2, 2 * rows, width))],
        [caps] + blocks + pieces,
        stored=(0,),
        scratch=[pltpu.SMEM(caps.shape, jnp.int32), pltpu.SemaphoreType.DMA(())],
        flops=2 * 2 * rows * model_dim * 5 * units,
    )
    own, other, grads, here = results[:2], results[2:4], results[4], results[5]
    summed = []
    for mine, theirs in zip(own, other):
        summed += call(
            sum_kernel,
            [shape((SLOT, model_dim + LANES))] * (count // 2),
            [mine, send(theirs, 0, 1)],
            flops=2500 * rows * model_dim,
        )
    backs = [send(part, 0, CORES * j) if j else part for j, part in zip(order, summed)]

    passed = call(
        split_kernel, [shape((rows, width))] * (2 * far - 2), [after(odd, summed[-1])], flops=2 * rows * width
    )
    passed = [send(part, 2 * (n // 2 + 1), 0) for n, part in enumerate(passed)]
    (own_rows,) = call(stack_kernel, [shape((rep - 1, 2 * rows, width))], [odd] + even + passed)
    other_rows = send(own_rows, 0, 1)
    group_grads = [grads] + [send(grads, k, 0) for k in range(1, rep)]
    grad_gate, grad_up, grad_down = call(
        functools.partial(weight_kernel, rep),
        [shape((width, units))] * 3,
        [here, own_rows, other_rows] + group_grads,
        kept=(0, 1, 2),
        scratch=[pltpu.VMEM((width, units), BF16)] * 3 + [pltpu.SemaphoreType.DMA((3,))],
        flops=2 * 2 * rep * rows * width * 3 * units,
    )
    grad_tokens, grad_weight = call(
        functools.partial(token_kernel, rep, flight),
        [shape((tok_count, model_dim)), shape(ids_rows.shape, F32)],
        [ids_rows, placed] + backs,
        stored=(0,),
        scratch=[
            pltpu.VMEM((rep, tok_count, width), BF16),
            pltpu.VMEM(ids_rows.shape, jnp.int32),
            pltpu.SemaphoreType.DMA((1,)),
        ],
        flops=1000 * 2 * tok_count * CHIPS * SLOT * model_dim,
    )
    return grad_tokens, grad_weight.T, grad_gate, grad_up, grad_down


def solution(mesh):
    return jax.shard_map(
        local,
        mesh=mesh,
        in_specs=(
            P(("rep", "ep"), None),
            P(("rep", "ep"), None),
            P(("rep", "ep"), None),
            P(("rep", "ep"), None),
            P(),
            P(),
            P("rep", "ep"),
            P("rep", "ep"),
            P("rep", "ep"),
        ),
        out_specs=(
            P(("rep", "ep"), None),
            P(("rep", "ep"), None),
            P("rep", "ep"),
            P("rep", "ep"),
            P("rep", "ep"),
        ),
        check_vma=False,
    )
```

```python
import functools

import jax
import jax.numpy as jnp
from jax import lax
from jax.experimental import pallas as pl
from jax.experimental.pallas import tpu as pltpu
from jax.sharding import PartitionSpec as P

EXPERTS = 128
SLOT = 16
BLOCK = 128
SPLIT = 8
CORES = 2
CHIPS = SPLIT // CORES
LANES = 128
F32 = jnp.float32
BF16 = jnp.bfloat16
PARTS = 4
HBM = pl.BlockSpec(memory_space=pltpu.HBM)
VMEM = pl.BlockSpec(memory_space=pltpu.VMEM)


def shape(dims, kind=BF16):
    return jax.ShapeDtypeStruct(dims, kind)


def call(kernel, outs, args, stored=(), kept=(), scratch=(), flops=0, grant=16):
    size = sum(a.size * a.dtype.itemsize for a in args) + sum(
        o.size * o.dtype.itemsize for o in outs
    )
    return pl.pallas_call(
        kernel,
        out_shape=tuple(outs),
        in_specs=[HBM if n in stored else VMEM for n in range(len(args))],
        out_specs=tuple([HBM if n in kept else VMEM for n in range(len(outs))]),
        scratch_shapes=scratch,
        compiler_params=pltpu.CompilerParams(vmem_limit_bytes=grant * 1024 * 1024),
        cost_estimate=pl.CostEstimate(flops=flops, bytes_accessed=size, transcendentals=0),
    )(*args)


def fetch(pairs, sems, first=0):
    copies = [
        pltpu.make_async_copy(source, target, sems.at[first + n])
        for n, (source, target) in enumerate(pairs)
    ]
    for copy in copies:
        copy.start()
    return copies


def dot(a, b, dims=((1,), (0,))):
    return lax.dot_general(a, b, (dims, ((), ())), preferred_element_type=F32)


def iota(dims, axis):
    return lax.broadcasted_iota(jnp.int32, dims, axis)


def turned(n):
    return n ^ (CHIPS - 1)


def pack_kernel(rep, flight, live_ref, tok_ref, grad_ref, ids_ref, rw_ref, *refs):
    stored, pays, placed_ref, all_ref = refs[:3], refs[3 : 3 + flight], refs[-9], refs[-8]
    live, ids_held, rw_held, data, rows, joined, sems = refs[-7:]
    r = lax.axis_index("rep")
    mine = lax.axis_index("ep") // SPLIT
    count, model = tok_ref.shape
    width = model // rep
    spacing = EXPERTS // flight
    small = fetch([(live_ref, live), (ids_ref, ids_held), (rw_ref, rw_held)], sems)
    units = stored[0].shape[1]
    piece = width // 2
    pairs = []
    for p in range(2):
        some = pl.ds(p * piece, piece)
        for n, ref in enumerate(stored):
            pairs.append((ref.at[some], joined.at[some, pl.ds(n * units, units)]))
    weight_copies = fetch(pairs, sems, 3)
    pairs = []
    for part, ref in enumerate((tok_ref, grad_ref)):
        for p in range(PARTS):
            some = pl.ds(p * (count // PARTS), count // PARTS)
            pairs.append((ref.at[some], data.at[part, some]))
    large = fetch(pairs, sems, 9)
    for copy in small:
        copy.wait()
    token = iota((1, count), 1)
    upper = (iota((count, count), 0) <= iota((count, count), 1)).astype(BF16)
    slot = iota((SLOT, count), 0).astype(F32)
    lane = iota((SLOT, LANES), 1)
    ids = ids_held[...]
    weights = rw_held[...].astype(F32)
    firsts = []
    for w in range(flight):
        expert = jnp.bitwise_xor(mine, w)
        match = ids == expert * spacing
        routed = jnp.any(match, axis=0, keepdims=True) & (token < live[r])
        weight = jnp.sum(jnp.where(match, weights, 0.0), axis=0, keepdims=True)
        routed = jnp.broadcast_to(jnp.where(routed, 1.0, 0.0), (SLOT, count))
        rank = dot(routed.astype(BF16), upper) - 1.0
        placed = jnp.where(rank == slot, routed, 0.0)
        column = jnp.sum(placed * weight, axis=1, keepdims=True)
        pays[w][:, 2 * model :] = jnp.where(lane == 0, column, 0.0).astype(BF16)
        placed = placed.astype(BF16)
        firsts.append(placed)
        placed_ref[w] = jnp.concatenate([placed] * CHIPS, axis=0)
    out_copies = []
    for p in range(2):
        for n in range(len(stored)):
            weight_copies[3 * p + n].wait()
        some = pl.ds(p * piece, piece)
        out_copies += fetch([(joined.at[some], all_ref.at[some])], sems, 9 + 2 * PARTS + p)
    for part in range(2):
        for p in range(PARTS):
            large[part * PARTS + p].wait()
        for w in range(flight):
            chosen = dot(firsts[w], data[part]).astype(BF16)
            for b in range(rep):
                rows[b] = chosen[:, b * width : (b + 1) * width]
            for k in range(rep):
                n = 2 * k + part
                pays[w][:, n * width : (n + 1) * width] = rows[jnp.bitwise_xor(r, k)]
    for copy in out_copies:
        copy.wait()


def half_kernel(start, all_ref, half_ref):
    half_ref[...] = all_ref[start : start + half_ref.shape[0]]


def hidden_kernel(rep, count, spans, cap_ref, *refs):
    blocks, pieces = refs[: 2 * count], refs[2 * count : 2 * count + len(spans)]
    outs, cap, sem = refs[2 * count + len(spans) : -2], refs[-2], refs[-1]
    own_ref, other_ref, grads_ref, here_ref, away_refs = *outs[:4], outs[4:]
    cap_copy = pltpu.make_async_copy(cap_ref, cap, sem)
    cap_copy.start()
    width = here_ref.shape[2]
    units = pieces[0].shape[1] // 3
    own_rows = count * SLOT
    r = lax.axis_index("rep")
    e = lax.axis_index("ep")
    mine = e // SPLIT
    inputs = [[], []]
    for k in range(rep):
        for part in range(2):
            n = 2 * k + part
            chosen = [b[:, n * width : (n + 1) * width] for b in blocks]
            chosen = jnp.concatenate(chosen, axis=0)
            inputs[part].append(chosen)
            if k == 0:
                here_ref[part] = chosen
            else:
                some = slice(part * own_rows, (part + 1) * own_rows)
                away_refs[k - 1][some, :width] = chosen[:own_rows]
    sum_x, sum_d = 0.0, 0.0
    for (k, start, stop), piece in zip(spans, pieces):
        sum_x = sum_x + dot(inputs[0][k][:, start:stop], piece[:, : 2 * units])
        sum_d = sum_d + dot(inputs[1][k][:, start:stop], piece[:, 2 * units :])

    cap_copy.wait()
    capacity = (BLOCK * cap[mine, r]).astype(F32)
    lane = iota((SLOT, LANES), 1)
    sources, rates, counts = [], [], []
    for n in range(2 * count):
        sources.append(jnp.bitwise_xor(e, CORES * turned(n % count) + n // count))
        rate = jnp.where(lane == 0, blocks[n][:, 2 * rep * width :].astype(F32), 0.0)
        rate = jnp.sum(rate, axis=1, keepdims=True)
        rates.append(rate)
        counts.append(jnp.sum(jnp.where(rate > 0.0, 1.0, 0.0), axis=0, keepdims=True))
    slot = iota((SLOT, 1), 0).astype(F32)
    rate_rows, kept_rows = [], []
    for n in range(2 * count):
        start = jnp.zeros((1, 1), F32)
        for other in range(2 * count):
            start = start + jnp.where(sources[other] < sources[n], counts[other], 0.0)
        kept = jnp.where((rates[n] > 0.0) & (start + slot < capacity), 1.0, 0.0)
        kept_rows.append(kept)
        rate_rows.append(rates[n] * kept)
    rate = jnp.concatenate(rate_rows, axis=0)
    kept = jnp.concatenate(kept_rows, axis=0)

    pre_gate, pre_up, back_hidden = sum_x[:, :units], sum_x[:, units:], sum_d
    sig = 1.0 / (1.0 + jnp.exp(-pre_gate))
    activated = pre_gate * sig
    hidden = activated * pre_up
    score = jnp.sum(hidden * back_hidden, axis=1, keepdims=True) * kept
    lane = iota((2 * own_rows, LANES), 1)
    scores = jnp.where(lane == e % CORES, score, 0.0).astype(BF16)
    scaled = back_hidden * rate
    gate_grad = (scaled * pre_up * sig * (1.0 + pre_gate * (1.0 - sig))).astype(BF16)
    up_grad = (scaled * activated).astype(BF16)
    weighted = (hidden * rate).astype(BF16)
    grads_ref[...] = jnp.concatenate([gate_grad, up_grad, weighted], axis=1)
    for ref in away_refs:
        ref[:, width:] = grads_ref[...]
    pair = jnp.concatenate([gate_grad, up_grad], axis=1)
    for (k, start, stop), piece in zip(spans, pieces):
        back = dot(pair, piece[:, : 2 * units], ((1,), (1,))).astype(BF16)
        some = slice(k * width + start, k * width + stop)
        own_ref[:, some] = back[:own_rows]
        other_ref[:, some] = back[own_rows:]
    own_ref[:, rep * width :] = scores[:own_rows]
    other_ref[:, rep * width :] = scores[own_rows:]


def sum_kernel(own_ref, got_ref, *outs):
    for j, out in enumerate(outs):
        some = slice(j * SLOT, (j + 1) * SLOT)
        out[...] = (own_ref[some].astype(F32) + got_ref[some].astype(F32)).astype(BF16)


def stack_kernel(*refs):
    for k, ref in enumerate(refs[:-1]):
        refs[-1][k] = ref[:, : refs[-1].shape[2]]


def weight_kernel(rep, here_ref, grads_ref, own_ref, other_ref, *refs):
    away, outs, held, sems = refs[: rep - 1], refs[rep - 1 : -4], refs[-4:-1], refs[-1]
    units = outs[0].shape[1]
    width = here_ref.shape[2]
    half = grads_ref.shape[0] // 2
    copies = []
    for part, columns in enumerate((slice(0, 2 * units), slice(2 * units, 3 * units))):
        some = slice(part * half, (part + 1) * half)
        got = [ref[:, width + columns.start : width + columns.stop] for ref in away]
        total = dot(grads_ref[:, columns], here_ref[part], ((0,), (0,)))
        for core, ref in enumerate((own_ref, other_ref)):
            mine = slice(core * half, (core + 1) * half)
            chosen = jnp.concatenate([g[mine] for g in got], axis=0)
            rows = ref[:, some].reshape(chosen.shape[0], width)
            total = total + dot(chosen, rows, ((0,), (0,)))
        for n in range(total.shape[0] // units):
            held[2 * part + n][...] = total[n * units : (n + 1) * units].T.astype(BF16)
            copies += fetch([(held[2 * part + n], outs[2 * part + n])], sems, 2 * part + n)
    for copy in copies:
        copy.wait()


def token_kernel(rep, flight, ids_ref, placed_ref, *refs):
    backs, rest = refs[: flight * CHIPS], refs[flight * CHIPS :]
    out_ref, weight_ref, blocks, joined_out, ids, sems = rest
    (ids_copy,) = fetch([(ids_ref, ids)], sems)
    copies = []
    r = lax.axis_index("rep")
    mine = lax.axis_index("ep") // SPLIT
    spacing = EXPERTS // flight
    width = out_ref.shape[1] // rep
    joined = [
        jnp.concatenate([b[...] for b in backs[w * CHIPS : (w + 1) * CHIPS]], axis=0)
        for w in range(flight)
    ]
    for k in range(rep):
        total = 0.0
        for w in range(flight):
            some = joined[w][:, k * width : (k + 1) * width]
            total = total + dot(placed_ref[w], some, ((0,), (0,)))
        group = jnp.bitwise_xor(r, k)
        blocks[group] = total.astype(BF16)
        if width % LANES == 0:
            some = pl.ds(pl.multiple_of(group * width, LANES), width)
            copies += fetch([(blocks.at[group], out_ref.at[:, some])], sems, k + 1)
    if width % LANES:
        for b in range(rep):
            joined_out[:, b * width : (b + 1) * width] = blocks[b]
        copies += fetch([(joined_out, out_ref)], sems, 1)
    result = jnp.zeros(weight_ref.shape, F32)
    ids_copy.wait()
    for w in range(flight):
        score = dot(joined[w][:, rep * width :], placed_ref[w], ((0,), (0,)))
        score = jnp.sum(score, axis=0, keepdims=True)
        match = ids[...] == jnp.bitwise_xor(mine, w) * spacing
        result = result + jnp.where(match, score, 0.0)
    weight_ref[...] = result
    for copy in copies:
        copy.wait()


def local(
    tokens, out_grad, expert_ids, route_weight, live_count, cap_blocks, w_gate, w_up, w_down_t
):
    rep = lax.axis_size("rep")
    ep = lax.axis_size("ep")
    far = rep // 2
    flight = ep // SPLIT
    count = ep // CORES
    tok_count, model_dim = tokens.shape
    width, units = w_gate.shape
    rows = count * SLOT
    ids_rows, rw_rows, caps = expert_ids.T, route_weight.T, cap_blocks.T

    def send(array, rep_bits, ep_bits):
        mask = rep_bits * ep + ep_bits
        pairs = [(a, a ^ mask) for a in range(rep * ep)]
        return lax.ppermute(array, ("rep", "ep"), pairs)

    def after(array, *others):
        return lax.optimization_barrier((array,) + others)[0]

    packed = call(
        functools.partial(pack_kernel, rep, flight),
        [shape((SLOT, 2 * model_dim + LANES))] * flight
        + [shape((flight, CHIPS * SLOT, tok_count)), shape((width, 3 * units))],
        [live_count, tokens, out_grad, ids_rows, rw_rows, w_gate, w_up, w_down_t],
        stored=range(8),
        kept=(flight + 1,),
        scratch=[
            pltpu.SMEM(live_count.shape, jnp.int32),
            pltpu.VMEM(ids_rows.shape, jnp.int32),
            pltpu.VMEM(rw_rows.shape, BF16),
            pltpu.VMEM((2, tok_count, model_dim), BF16),
            pltpu.VMEM((rep, SLOT, width), BF16),
            pltpu.VMEM((width, 3 * units), BF16),
            pltpu.SemaphoreType.DMA((2 * PARTS + 11,)),
        ],
        grant=54,
    )
    pays, placed, weights = packed[:flight], packed[flight], packed[flight + 1]

    half = width // 2
    whole = {0: weights}
    halves = {}
    for k in range(1, rep):
        low, high = k & -k, 1 << (k.bit_length() - 1)
        if low == high:
            whole[k] = send(weights, k, 0)
            for h in range(2):
                kernel = functools.partial(half_kernel, h * half)
                (halves[k, h],) = call(kernel, [shape((half, 3 * units))], [whole[k]])
        else:
            halves[k, 0] = send(halves[k ^ low, 0], low, 0)
            halves[k, 1] = send(halves[k ^ high, 1], high, 0)
    spans, pieces = [], []
    for k in range(rep):
        if k in whole:
            spans.append((k, 0, width))
            pieces.append(whole[k])
        else:
            spans += [(k, 0, half), (k, half, width)]
            pieces += [halves[k, 0], halves[k, 1]]

    order = [turned(n) for n in range(count)]
    blocks = [send(pays[j // CHIPS], 0, CORES * j) if j else pays[0] for j in order]
    nearest = blocks[order.index(1)]
    ready = [after(b, nearest) if j == 0 else b for j, b in zip(order, blocks)]
    blocks = blocks + [send(block, 0, 1) for block in ready]
    results = call(
        functools.partial(hidden_kernel, rep, count, tuple(spans)),
        [shape((rows, model_dim + LANES))] * 2
        + [shape((2 * rows, 3 * units)), shape((2, 2 * rows, width))]
        + [shape((2 * rows, width + 3 * units))] * (rep - 1),
        [caps] + blocks + pieces,
        stored=(0,),
        scratch=[pltpu.SMEM(caps.shape, jnp.int32), pltpu.SemaphoreType.DMA(())],
        flops=2 * 2 * rows * model_dim * 5 * units,
    )
    own, other, grads, here, away = *results[:4], results[4:]
    summed = call(sum_kernel, [shape((SLOT, model_dim + LANES))] * count, [own, send(other, 0, 1)])
    backs = [send(part, 0, CORES * j) if j else part for j, part in zip(order, summed)]

    moved = [
        send(part if k & (k - 1) else after(part, summed[-2]), k, 0) for k, part in enumerate(away, 1)
    ]
    (own_rows,) = call(stack_kernel, [shape((rep - 1, 2 * rows, width))], moved)
    other_rows = send(own_rows, 0, 1)
    grad_gate, grad_up, grad_down = call(
        functools.partial(weight_kernel, rep),
        [shape((width, units))] * 3,
        [here, grads, own_rows, other_rows] + moved,
        kept=(0, 1, 2),
        scratch=[pltpu.VMEM((width, units), BF16)] * 3 + [pltpu.SemaphoreType.DMA((3,))],
        flops=2 * 2 * rep * rows * width * 3 * units,
    )
    grad_tokens, grad_weight = call(
        functools.partial(token_kernel, rep, flight),
        [shape((tok_count, model_dim)), shape(ids_rows.shape, F32)],
        [ids_rows, placed] + backs,
        stored=(0,),
        kept=(0,),
        scratch=[
            pltpu.VMEM((rep, tok_count, width), BF16),
            pltpu.VMEM((tok_count, model_dim), BF16),
            pltpu.VMEM(ids_rows.shape, jnp.int32),
            pltpu.SemaphoreType.DMA((rep + 1,)),
        ],
        flops=1000 * 2 * tok_count * CHIPS * SLOT * model_dim,
    )
    return grad_tokens, grad_weight.T, grad_gate, grad_up, grad_down


def solution(mesh):
    return jax.shard_map(
        local,
        mesh=mesh,
        in_specs=(
            P(("rep", "ep"), None),
            P(("rep", "ep"), None),
            P(("rep", "ep"), None),
            P(("rep", "ep"), None),
            P(),
            P(),
            P("rep", "ep"),
            P("rep", "ep"),
            P("rep", "ep"),
        ),
        out_specs=(
            P(("rep", "ep"), None),
            P(("rep", "ep"), None),
            P("rep", "ep"),
            P("rep", "ep"),
            P("rep", "ep"),
        ),
        check_vma=False,
    )
```

```python
import functools

import jax
import jax.numpy as jnp
from jax import lax
from jax.experimental import pallas as pl
from jax.experimental.pallas import tpu as pltpu
from jax.sharding import PartitionSpec as P

EXPERTS = 128
SLOT = 16
BLOCK = 128
SPLIT = 8
CORES = 2
CHIPS = SPLIT // CORES
LANES = 128
F32 = jnp.float32
BF16 = jnp.bfloat16
PARTS = 4
HBM = pl.BlockSpec(memory_space=pltpu.HBM)
VMEM = pl.BlockSpec(memory_space=pltpu.VMEM)


def shape(dims, kind=BF16):
    return jax.ShapeDtypeStruct(dims, kind)


def call(kernel, outs, args, stored=(), kept=(), scratch=(), flops=0, grant=16):
    size = sum(a.size * a.dtype.itemsize for a in args) + sum(
        o.size * o.dtype.itemsize for o in outs
    )
    return pl.pallas_call(
        kernel,
        out_shape=tuple(outs),
        in_specs=[HBM if n in stored else VMEM for n in range(len(args))],
        out_specs=tuple([HBM if n in kept else VMEM for n in range(len(outs))]),
        scratch_shapes=scratch,
        compiler_params=pltpu.CompilerParams(vmem_limit_bytes=grant * 1024 * 1024),
        cost_estimate=pl.CostEstimate(flops=flops, bytes_accessed=size, transcendentals=0),
    )(*args)


def fetch(pairs, sems, first=0):
    copies = [
        pltpu.make_async_copy(source, target, sems.at[first + n])
        for n, (source, target) in enumerate(pairs)
    ]
    for copy in copies:
        copy.start()
    return copies


def dot(a, b, dims=((1,), (0,))):
    return lax.dot_general(a, b, (dims, ((), ())), preferred_element_type=F32)


def iota(dims, axis):
    return lax.broadcasted_iota(jnp.int32, dims, axis)


def turned(n):
    return n ^ (CHIPS - 1)


def pack_kernel(rep, flight, live_ref, tok_ref, grad_ref, ids_ref, rw_ref, *refs):
    stored, pays, placed_ref, all_ref = refs[:3], refs[3 : 3 + flight], refs[-9], refs[-8]
    live, ids_held, rw_held, data, rows, joined, sems = refs[-7:]
    r = lax.axis_index("rep")
    mine = lax.axis_index("ep") // SPLIT
    count, model = tok_ref.shape
    width = model // rep
    spacing = EXPERTS // flight
    small = fetch([(live_ref, live), (ids_ref, ids_held), (rw_ref, rw_held)], sems)
    units = stored[0].shape[1]
    piece = width // 2
    pairs = []
    for p in range(2):
        some = pl.ds(p * piece, piece)
        for n, ref in enumerate(stored):
            pairs.append((ref.at[some], joined.at[some, pl.ds(n * units, units)]))
    weight_copies = fetch(pairs, sems, 3)
    pairs = []
    for part, ref in enumerate((tok_ref, grad_ref)):
        for p in range(PARTS):
            some = pl.ds(p * (count // PARTS), count // PARTS)
            pairs.append((ref.at[some], data.at[part, some]))
    large = fetch(pairs, sems, 9)
    for copy in small:
        copy.wait()
    token = iota((1, count), 1)
    upper = (iota((count, count), 0) <= iota((count, count), 1)).astype(BF16)
    slot = iota((SLOT, count), 0).astype(F32)
    lane = iota((SLOT, LANES), 1)
    ids = ids_held[...]
    weights = rw_held[...].astype(F32)
    firsts = []
    for w in range(flight):
        expert = jnp.bitwise_xor(mine, w)
        match = ids == expert * spacing
        routed = jnp.any(match, axis=0, keepdims=True) & (token < live[r])
        weight = jnp.sum(jnp.where(match, weights, 0.0), axis=0, keepdims=True)
        routed = jnp.broadcast_to(jnp.where(routed, 1.0, 0.0), (SLOT, count))
        rank = dot(routed.astype(BF16), upper) - 1.0
        placed = jnp.where(rank == slot, routed, 0.0)
        column = jnp.sum(placed * weight, axis=1, keepdims=True)
        pays[w][:, 2 * model :] = jnp.where(lane == 0, column, 0.0).astype(BF16)
        placed = placed.astype(BF16)
        firsts.append(placed)
        placed_ref[w] = jnp.concatenate([placed] * CHIPS, axis=0)
    out_copies = []
    for p in range(2):
        for n in range(len(stored)):
            weight_copies[3 * p + n].wait()
        some = pl.ds(p * piece, piece)
        out_copies += fetch([(joined.at[some], all_ref.at[some])], sems, 9 + 2 * PARTS + p)
    for part in range(2):
        for p in range(PARTS):
            large[part * PARTS + p].wait()
        for w in range(flight):
            chosen = dot(firsts[w], data[part]).astype(BF16)
            for b in range(rep):
                rows[b] = chosen[:, b * width : (b + 1) * width]
            for k in range(rep):
                n = 2 * k + part
                pays[w][:, n * width : (n + 1) * width] = rows[jnp.bitwise_xor(r, k)]
    for copy in out_copies:
        copy.wait()


def columns_kernel(rep, count, *refs):
    blocks, odd_ref, outs = refs[:count], refs[count], refs[count + 1 :]
    rows, width = count * SLOT, odd_ref.shape[2]
    for k in range(1, rep):
        out = odd_ref.at[k // 2] if k % 2 else outs[k // 2 - 1]
        for part in range(2):
            n = 2 * k + part
            for j in range(count):
                start = part * rows + j * SLOT
                out[start : start + SLOT] = blocks[j][:, n * width : (n + 1) * width]


def split_kernel(all_ref, *outs):
    rows = outs[0].shape[0]
    for n, out in enumerate(outs):
        start = n % 2 * rows
        out[...] = all_ref[n // 2 + 1, start : start + rows]


def half_kernel(start, all_ref, half_ref):
    half_ref[...] = all_ref[start : start + half_ref.shape[0]]


def hidden_kernel(rep, count, spans, cap_ref, *refs):
    blocks, pieces = refs[: 2 * count], refs[2 * count : 2 * count + len(spans)]
    outs, cap, sem = refs[2 * count + len(spans) : -2], refs[-2], refs[-1]
    own_refs, other_refs, grads_ref, here_ref = outs[:2], outs[2:4], outs[4], outs[5]
    cap_copy = pltpu.make_async_copy(cap_ref, cap, sem)
    cap_copy.start()
    width = here_ref.shape[2]
    units = pieces[0].shape[1] // 3
    part_rows = count * SLOT // 2
    r = lax.axis_index("rep")
    e = lax.axis_index("ep")
    mine = e // SPLIT
    inputs = [[], []]
    for k in range(rep):
        for part in range(2):
            n = 2 * k + part
            chosen = [b[:, n * width : (n + 1) * width] for b in blocks]
            chosen = jnp.concatenate(chosen, axis=0)
            inputs[part].append(chosen)
            if k == 0:
                here_ref[part] = chosen
    sum_x, sum_d = 0.0, 0.0
    for (k, start, stop), piece in zip(spans, pieces):
        sum_x = sum_x + dot(inputs[0][k][:, start:stop], piece[:, : 2 * units])
        sum_d = sum_d + dot(inputs[1][k][:, start:stop], piece[:, 2 * units :])

    cap_copy.wait()
    capacity = (BLOCK * cap[mine, r]).astype(F32)
    lane = iota((SLOT, LANES), 1)
    sources, rates, counts = [], [], []
    for n in range(2 * count):
        sources.append(jnp.bitwise_xor(e, CORES * turned(n % count) + n // count))
        rate = jnp.where(lane == 0, blocks[n][:, 2 * rep * width :].astype(F32), 0.0)
        rate = jnp.sum(rate, axis=1, keepdims=True)
        rates.append(rate)
        counts.append(jnp.sum(jnp.where(rate > 0.0, 1.0, 0.0), axis=0, keepdims=True))
    slot = iota((SLOT, 1), 0).astype(F32)
    rate_rows, kept_rows = [], []
    for n in range(2 * count):
        start = jnp.zeros((1, 1), F32)
        for other in range(2 * count):
            start = start + jnp.where(sources[other] < sources[n], counts[other], 0.0)
        kept = jnp.where((rates[n] > 0.0) & (start + slot < capacity), 1.0, 0.0)
        kept_rows.append(kept)
        rate_rows.append(rates[n] * kept)
    rate = jnp.concatenate(rate_rows, axis=0)
    kept = jnp.concatenate(kept_rows, axis=0)

    pre_gate, pre_up, back_hidden = sum_x[:, :units], sum_x[:, units:], sum_d
    sig = 1.0 / (1.0 + jnp.exp(-pre_gate))
    activated = pre_gate * sig
    hidden = activated * pre_up
    score = jnp.sum(hidden * back_hidden, axis=1, keepdims=True) * kept
    lane = iota((4 * part_rows, LANES), 1)
    scores = jnp.where(lane == e % CORES, score, 0.0).astype(BF16)
    scaled = back_hidden * rate
    gate_grad = (scaled * pre_up * sig * (1.0 + pre_gate * (1.0 - sig))).astype(BF16)
    up_grad = (scaled * activated).astype(BF16)
    weighted = (hidden * rate).astype(BF16)
    grads_ref[...] = jnp.concatenate([gate_grad, up_grad, weighted], axis=1)
    pair = jnp.concatenate([gate_grad, up_grad], axis=1)
    for (k, start, stop), piece in zip(spans, pieces):
        back = dot(pair, piece[:, : 2 * units], ((1,), (1,))).astype(BF16)
        some = slice(k * width + start, k * width + stop)
        for n, ref in enumerate(own_refs + other_refs):
            ref[:, some] = back[n * part_rows : (n + 1) * part_rows]
    for n, ref in enumerate(own_refs + other_refs):
        ref[:, rep * width :] = scores[n * part_rows : (n + 1) * part_rows]


def sum_kernel(own_ref, got_ref, *outs):
    for j, out in enumerate(outs):
        some = slice(j * SLOT, (j + 1) * SLOT)
        out[...] = (own_ref[some].astype(F32) + got_ref[some].astype(F32)).astype(BF16)


def stack_kernel(odd_ref, *refs):
    out, count = refs[-1], len(refs) // 3
    rows = out.shape[1] // 2
    out[0] = odd_ref[0]
    for n in range(count):
        out[2 * n + 1] = refs[n][...]
        out[2 * n + 2, :rows] = refs[count + 2 * n][...]
        out[2 * n + 2, rows:] = refs[count + 2 * n + 1][...]


def weight_kernel(rep, here_ref, own_ref, other_ref, *refs):
    grads, outs, held, sems = refs[:-7], refs[-7:-4], refs[-4:-1], refs[-1]
    units = outs[0].shape[1]
    half = own_ref.shape[1] // 2
    copies = []
    for part, columns in enumerate((slice(0, 2 * units), slice(2 * units, 3 * units))):
        some = slice(part * half, (part + 1) * half)
        rows = [here_ref[part]]
        for k in range(rep - 1):
            rows += [own_ref[k, some], other_ref[k, some]]
        rows = jnp.concatenate(rows, axis=0)
        got = jnp.concatenate([ref[:, columns] for ref in grads], axis=0)
        total = dot(got, rows, ((0,), (0,)))
        for n in range(total.shape[0] // units):
            held[2 * part + n][...] = total[n * units : (n + 1) * units].T.astype(BF16)
            copies += fetch([(held[2 * part + n], outs[2 * part + n])], sems, 2 * part + n)
    for copy in copies:
        copy.wait()


def token_kernel(rep, flight, ids_ref, placed_ref, *refs):
    backs, rest = refs[: flight * CHIPS], refs[flight * CHIPS :]
    out_ref, weight_ref, blocks, ids, sems = rest
    (ids_copy,) = fetch([(ids_ref, ids)], sems)
    r = lax.axis_index("rep")
    mine = lax.axis_index("ep") // SPLIT
    spacing = EXPERTS // flight
    width = out_ref.shape[1] // rep
    joined = [
        jnp.concatenate([b[...] for b in backs[w * CHIPS : (w + 1) * CHIPS]], axis=0)
        for w in range(flight)
    ]
    for k in range(rep):
        total = 0.0
        for w in range(flight):
            some = joined[w][:, k * width : (k + 1) * width]
            total = total + dot(placed_ref[w], some, ((0,), (0,)))
        blocks[jnp.bitwise_xor(r, k)] = total.astype(BF16)
    for b in range(rep):
        out_ref[:, b * width : (b + 1) * width] = blocks[b]
    result = jnp.zeros(weight_ref.shape, F32)
    ids_copy.wait()
    for w in range(flight):
        score = dot(joined[w][:, rep * width :], placed_ref[w], ((0,), (0,)))
        score = jnp.sum(score, axis=0, keepdims=True)
        match = ids[...] == jnp.bitwise_xor(mine, w) * spacing
        result = result + jnp.where(match, score, 0.0)
    weight_ref[...] = result


def local(
    tokens, out_grad, expert_ids, route_weight, live_count, cap_blocks, w_gate, w_up, w_down_t
):
    rep = lax.axis_size("rep")
    ep = lax.axis_size("ep")
    far = rep // 2
    flight = ep // SPLIT
    count = ep // CORES
    tok_count, model_dim = tokens.shape
    width, units = w_gate.shape
    rows = count * SLOT
    ids_rows, rw_rows, caps = expert_ids.T, route_weight.T, cap_blocks.T

    def send(array, rep_bits, ep_bits):
        mask = rep_bits * ep + ep_bits
        pairs = [(a, a ^ mask) for a in range(rep * ep)]
        return lax.ppermute(array, ("rep", "ep"), pairs)

    def after(array, *others):
        return lax.optimization_barrier((array,) + others)[0]

    packed = call(
        functools.partial(pack_kernel, rep, flight),
        [shape((SLOT, 2 * model_dim + LANES))] * flight
        + [shape((flight, CHIPS * SLOT, tok_count)), shape((width, 3 * units))],
        [live_count, tokens, out_grad, ids_rows, rw_rows, w_gate, w_up, w_down_t],
        stored=range(8),
        kept=(flight + 1,),
        scratch=[
            pltpu.SMEM(live_count.shape, jnp.int32),
            pltpu.VMEM(ids_rows.shape, jnp.int32),
            pltpu.VMEM(rw_rows.shape, BF16),
            pltpu.VMEM((2, tok_count, model_dim), BF16),
            pltpu.VMEM((rep, SLOT, width), BF16),
            pltpu.VMEM((width, 3 * units), BF16),
            pltpu.SemaphoreType.DMA((2 * PARTS + 11,)),
        ],
        grant=54,
    )
    pays, placed, weights = packed[:flight], packed[flight], packed[flight + 1]

    half = width // 2
    whole = {0: weights}
    halves, sent = {}, []
    for k in range(1, rep):
        low, high = k & -k, 1 << (k.bit_length() - 1)
        if low == high:
            whole[k] = send(weights, k, 0)
            for h in range(2):
                kernel = functools.partial(half_kernel, h * half)
                (halves[k, h],) = call(kernel, [shape((half, 3 * units))], [whole[k]])
                sent.append(halves[k, h])
        else:
            halves[k, 0] = send(halves[k ^ low, 0], low, 0)
            halves[k, 1] = send(halves[k ^ high, 1], high, 0)
    spans, pieces = [], []
    for k in range(rep):
        if k in whole:
            spans.append((k, 0, width))
            pieces.append(whole[k])
        else:
            spans += [(k, 0, half), (k, half, width)]
            pieces += [halves[k, 0], halves[k, 1]]

    order = [turned(n) for n in range(count)]
    blocks = [send(pays[j // CHIPS], 0, CORES * j) if j else pays[0] for j in order]
    far = rep // 2
    odd, *even = call(
        functools.partial(columns_kernel, rep, count),
        [shape((far, 2 * rows, width))] + [shape((2 * rows, width))] * (far - 1),
        [after(blocks[0], *sent)] + blocks[1:],
    )
    odd = send(odd, 1, 0)
    even = [send(part, 2 * k, 0) for k, part in enumerate(even, 1)]
    nearest = blocks[order.index(1)]
    ready = [after(b, nearest) if j == 0 else b for j, b in zip(order, blocks)]
    blocks = blocks + [send(block, 0, 1) for block in ready]
    results = call(
        functools.partial(hidden_kernel, rep, count, tuple(spans)),
        [shape((rows // 2, model_dim + LANES))] * 4
        + [shape((2 * rows, 3 * units)), shape((2, 2 * rows, width))],
        [caps] + blocks + pieces,
        stored=(0,),
        scratch=[pltpu.SMEM(caps.shape, jnp.int32), pltpu.SemaphoreType.DMA(())],
        flops=2 * 2 * rows * model_dim * 5 * units,
    )
    own, other, grads, here = results[:2], results[2:4], results[4], results[5]
    summed = []
    for mine, theirs in zip(own, other):
        summed += call(
            sum_kernel,
            [shape((SLOT, model_dim + LANES))] * (count // 2),
            [mine, send(theirs, 0, 1)],
            flops=2500 * rows * model_dim,
        )
    backs = [send(part, 0, CORES * j) if j else part for j, part in zip(order, summed)]

    passed = call(
        split_kernel, [shape((rows, width))] * (2 * far - 2), [after(odd, summed[-1])], flops=2 * rows * width
    )
    passed = [send(part, 2 * (n // 2 + 1), 0) for n, part in enumerate(passed)]
    (own_rows,) = call(stack_kernel, [shape((rep - 1, 2 * rows, width))], [odd] + even + passed)
    other_rows = send(own_rows, 0, 1)
    group_grads = [grads]
    bit = 1
    while bit < rep:
        array = group_grads[0] if bit == 1 else jnp.concatenate(group_grads, axis=0)
        group_grads.append(send(array, bit, 0))
        bit *= 2
    grad_gate, grad_up, grad_down = call(
        functools.partial(weight_kernel, rep),
        [shape((width, units))] * 3,
        [here, own_rows, other_rows] + group_grads,
        kept=(0, 1, 2),
        scratch=[pltpu.VMEM((width, units), BF16)] * 3 + [pltpu.SemaphoreType.DMA((3,))],
        flops=2 * 2 * rep * rows * width * 3 * units,
    )
    grad_tokens, grad_weight = call(
        functools.partial(token_kernel, rep, flight),
        [shape((tok_count, model_dim)), shape(ids_rows.shape, F32)],
        [ids_rows, placed] + backs,
        stored=(0,),
        scratch=[
            pltpu.VMEM((rep, tok_count, width), BF16),
            pltpu.VMEM(ids_rows.shape, jnp.int32),
            pltpu.SemaphoreType.DMA((1,)),
        ],
        flops=1000 * 2 * tok_count * CHIPS * SLOT * model_dim,
    )
    return grad_tokens, grad_weight.T, grad_gate, grad_up, grad_down


def solution(mesh):
    return jax.shard_map(
        local,
        mesh=mesh,
        in_specs=(
            P(("rep", "ep"), None),
            P(("rep", "ep"), None),
            P(("rep", "ep"), None),
            P(("rep", "ep"), None),
            P(),
            P(),
            P("rep", "ep"),
            P("rep", "ep"),
            P("rep", "ep"),
        ),
        out_specs=(
            P(("rep", "ep"), None),
            P(("rep", "ep"), None),
            P("rep", "ep"),
            P("rep", "ep"),
            P("rep", "ep"),
        ),
        check_vma=False,
    )
```

```python
import functools

import jax
import jax.numpy as jnp
from jax import lax
from jax.experimental import pallas as pl
from jax.experimental.pallas import tpu as pltpu
from jax.sharding import PartitionSpec as P

EXPERTS = 128
SLOT = 16
BLOCK = 128
SPLIT = 8
CORES = 2
CHIPS = SPLIT // CORES
LANES = 128
F32 = jnp.float32
BF16 = jnp.bfloat16
PARTS = 4
HBM = pl.BlockSpec(memory_space=pltpu.HBM)
VMEM = pl.BlockSpec(memory_space=pltpu.VMEM)


def shape(dims, kind=BF16):
    return jax.ShapeDtypeStruct(dims, kind)


def call(kernel, outs, args, stored=(), kept=(), scratch=(), flops=0, grant=16):
    size = sum(a.size * a.dtype.itemsize for a in args) + sum(
        o.size * o.dtype.itemsize for o in outs
    )
    return pl.pallas_call(
        kernel,
        out_shape=tuple(outs),
        in_specs=[HBM if n in stored else VMEM for n in range(len(args))],
        out_specs=tuple([HBM if n in kept else VMEM for n in range(len(outs))]),
        scratch_shapes=scratch,
        compiler_params=pltpu.CompilerParams(vmem_limit_bytes=grant * 1024 * 1024),
        cost_estimate=pl.CostEstimate(flops=flops, bytes_accessed=size, transcendentals=0),
    )(*args)


def fetch(pairs, sems, first=0):
    copies = [
        pltpu.make_async_copy(source, target, sems.at[first + n])
        for n, (source, target) in enumerate(pairs)
    ]
    for copy in copies:
        copy.start()
    return copies


def dot(a, b, dims=((1,), (0,))):
    return lax.dot_general(a, b, (dims, ((), ())), preferred_element_type=F32)


def iota(dims, axis):
    return lax.broadcasted_iota(jnp.int32, dims, axis)


def turned(n):
    return n ^ (CHIPS - 1)


def pack_kernel(rep, flight, live_ref, tok_ref, grad_ref, ids_ref, rw_ref, *refs):
    stored, pays, placed_ref, all_ref = refs[:3], refs[3 : 3 + flight], refs[-9], refs[-8]
    live, ids_held, rw_held, data, rows, joined, sems = refs[-7:]
    r = lax.axis_index("rep")
    mine = lax.axis_index("ep") // SPLIT
    count, model = tok_ref.shape
    width = model // rep
    spacing = EXPERTS // flight
    small = fetch([(live_ref, live), (ids_ref, ids_held), (rw_ref, rw_held)], sems)
    units = stored[0].shape[1]
    piece = width // 2
    pairs = []
    for p in range(2):
        some = pl.ds(p * piece, piece)
        for n, ref in enumerate(stored):
            pairs.append((ref.at[some], joined.at[some, pl.ds(n * units, units)]))
    weight_copies = fetch(pairs, sems, 3)
    pairs = []
    for part, ref in enumerate((tok_ref, grad_ref)):
        for p in range(PARTS):
            some = pl.ds(p * (count // PARTS), count // PARTS)
            pairs.append((ref.at[some], data.at[part, some]))
    large = fetch(pairs, sems, 9)
    for copy in small:
        copy.wait()
    token = iota((1, count), 1)
    upper = (iota((count, count), 0) <= iota((count, count), 1)).astype(BF16)
    slot = iota((SLOT, count), 0).astype(F32)
    lane = iota((SLOT, LANES), 1)
    ids = ids_held[...]
    weights = rw_held[...].astype(F32)
    firsts = []
    for w in range(flight):
        expert = jnp.bitwise_xor(mine, w)
        match = ids == expert * spacing
        routed = jnp.any(match, axis=0, keepdims=True) & (token < live[r])
        weight = jnp.sum(jnp.where(match, weights, 0.0), axis=0, keepdims=True)
        routed = jnp.broadcast_to(jnp.where(routed, 1.0, 0.0), (SLOT, count))
        rank = dot(routed.astype(BF16), upper) - 1.0
        placed = jnp.where(rank == slot, routed, 0.0)
        column = jnp.sum(placed * weight, axis=1, keepdims=True)
        pays[w][:, 2 * model :] = jnp.where(lane == 0, column, 0.0).astype(BF16)
        placed = placed.astype(BF16)
        firsts.append(placed)
        placed_ref[w] = jnp.concatenate([placed] * CHIPS, axis=0)
    out_copies = []
    for p in range(2):
        for n in range(len(stored)):
            weight_copies[3 * p + n].wait()
        some = pl.ds(p * piece, piece)
        out_copies += fetch([(joined.at[some], all_ref.at[some])], sems, 9 + 2 * PARTS + p)
    for part in range(2):
        for p in range(PARTS):
            large[part * PARTS + p].wait()
        for w in range(flight):
            chosen = dot(firsts[w], data[part]).astype(BF16)
            for b in range(rep):
                rows[b] = chosen[:, b * width : (b + 1) * width]
            for k in range(rep):
                n = 2 * k + part
                pays[w][:, n * width : (n + 1) * width] = rows[jnp.bitwise_xor(r, k)]
    for copy in out_copies:
        copy.wait()


def half_kernel(start, all_ref, half_ref):
    half_ref[...] = all_ref[start : start + half_ref.shape[0]]


def hidden_kernel(rep, count, spans, cap_ref, *refs):
    blocks, pieces = refs[: 2 * count], refs[2 * count : 2 * count + len(spans)]
    outs, cap, sem = refs[2 * count + len(spans) : -2], refs[-2], refs[-1]
    own_ref, other_ref, grads_ref, here_ref, away_refs = *outs[:4], outs[4:]
    cap_copy = pltpu.make_async_copy(cap_ref, cap, sem)
    cap_copy.start()
    width = here_ref.shape[2]
    units = pieces[0].shape[1] // 3
    own_rows = count * SLOT
    r = lax.axis_index("rep")
    e = lax.axis_index("ep")
    mine = e // SPLIT
    inputs = [[], []]
    for k in range(rep):
        for part in range(2):
            n = 2 * k + part
            chosen = [b[:, n * width : (n + 1) * width] for b in blocks]
            chosen = jnp.concatenate(chosen, axis=0)
            inputs[part].append(chosen)
            if k == 0:
                here_ref[part] = chosen
            else:
                some = slice(part * own_rows, (part + 1) * own_rows)
                away_refs[k - 1][some, :width] = chosen[:own_rows]
    sum_x, sum_d = 0.0, 0.0
    for (k, start, stop), piece in zip(spans, pieces):
        sum_x = sum_x + dot(inputs[0][k][:, start:stop], piece[:, : 2 * units])
        sum_d = sum_d + dot(inputs[1][k][:, start:stop], piece[:, 2 * units :])

    cap_copy.wait()
    capacity = (BLOCK * cap[mine, r]).astype(F32)
    lane = iota((SLOT, LANES), 1)
    sources, rates, counts = [], [], []
    for n in range(2 * count):
        sources.append(jnp.bitwise_xor(e, CORES * turned(n % count) + n // count))
        rate = jnp.where(lane == 0, blocks[n][:, 2 * rep * width :].astype(F32), 0.0)
        rate = jnp.sum(rate, axis=1, keepdims=True)
        rates.append(rate)
        counts.append(jnp.sum(jnp.where(rate > 0.0, 1.0, 0.0), axis=0, keepdims=True))
    slot = iota((SLOT, 1), 0).astype(F32)
    rate_rows, kept_rows = [], []
    for n in range(2 * count):
        start = jnp.zeros((1, 1), F32)
        for other in range(2 * count):
            start = start + jnp.where(sources[other] < sources[n], counts[other], 0.0)
        kept = jnp.where((rates[n] > 0.0) & (start + slot < capacity), 1.0, 0.0)
        kept_rows.append(kept)
        rate_rows.append(rates[n] * kept)
    rate = jnp.concatenate(rate_rows, axis=0)
    kept = jnp.concatenate(kept_rows, axis=0)

    pre_gate, pre_up, back_hidden = sum_x[:, :units], sum_x[:, units:], sum_d
    sig = 1.0 / (1.0 + jnp.exp(-pre_gate))
    activated = pre_gate * sig
    hidden = activated * pre_up
    score = jnp.sum(hidden * back_hidden, axis=1, keepdims=True) * kept
    lane = iota((2 * own_rows, LANES), 1)
    scores = jnp.where(lane == e % CORES, score, 0.0).astype(BF16)
    scaled = back_hidden * rate
    gate_grad = (scaled * pre_up * sig * (1.0 + pre_gate * (1.0 - sig))).astype(BF16)
    up_grad = (scaled * activated).astype(BF16)
    weighted = (hidden * rate).astype(BF16)
    grads_ref[...] = jnp.concatenate([gate_grad, up_grad, weighted], axis=1)
    for ref in away_refs:
        ref[:, width:] = grads_ref[...]
    pair = jnp.concatenate([gate_grad, up_grad], axis=1)
    for (k, start, stop), piece in zip(spans, pieces):
        back = dot(pair, piece[:, : 2 * units], ((1,), (1,))).astype(BF16)
        some = slice(k * width + start, k * width + stop)
        own_ref[:, some] = back[:own_rows]
        other_ref[:, some] = back[own_rows:]
    own_ref[:, rep * width :] = scores[:own_rows]
    other_ref[:, rep * width :] = scores[own_rows:]


def sum_kernel(own_ref, got_ref, *outs):
    for j, out in enumerate(outs):
        some = slice(j * SLOT, (j + 1) * SLOT)
        out[...] = (own_ref[some].astype(F32) + got_ref[some].astype(F32)).astype(BF16)


def stack_kernel(*refs):
    for k, ref in enumerate(refs[:-1]):
        refs[-1][k] = ref[:, : refs[-1].shape[2]]


def weight_kernel(rep, here_ref, grads_ref, near_ref, far_ref, *refs):
    away, outs, held, sems = refs[: rep - 1], refs[rep - 1 : -4], refs[-4:-1], refs[-1]
    units = outs[0].shape[1]
    width = here_ref.shape[2]
    half = grads_ref.shape[0] // 2
    copies = []
    for part, columns in enumerate((slice(0, 2 * units), slice(2 * units, 3 * units))):
        some = slice(part * half, (part + 1) * half)
        rows = [here_ref[part]]
        got = [grads_ref[:, columns]]
        others = [ref[k, some] for ref in (near_ref, far_ref) for k in range(ref.shape[0])]
        for other, ref in zip(others, away):
            rows += [ref[some, :width], other]
            got.append(ref[:, width + columns.start : width + columns.stop])
        rows = jnp.concatenate(rows, axis=0)
        got = jnp.concatenate(got, axis=0)
        total = dot(got, rows, ((0,), (0,)))
        for n in range(total.shape[0] // units):
            held[2 * part + n][...] = total[n * units : (n + 1) * units].T.astype(BF16)
            copies += fetch([(held[2 * part + n], outs[2 * part + n])], sems, 2 * part + n)
    for copy in copies:
        copy.wait()


def token_kernel(rep, flight, ids_ref, placed_ref, *refs):
    backs, rest = refs[: flight * CHIPS], refs[flight * CHIPS :]
    out_ref, weight_ref, blocks, ids, sems = rest
    (ids_copy,) = fetch([(ids_ref, ids)], sems)
    r = lax.axis_index("rep")
    mine = lax.axis_index("ep") // SPLIT
    spacing = EXPERTS // flight
    width = out_ref.shape[1] // rep
    joined = [
        jnp.concatenate([b[...] for b in backs[w * CHIPS : (w + 1) * CHIPS]], axis=0)
        for w in range(flight)
    ]
    for k in range(rep):
        total = 0.0
        for w in range(flight):
            some = joined[w][:, k * width : (k + 1) * width]
            total = total + dot(placed_ref[w], some, ((0,), (0,)))
        blocks[jnp.bitwise_xor(r, k)] = total.astype(BF16)
    for b in range(rep):
        out_ref[:, b * width : (b + 1) * width] = blocks[b]
    result = jnp.zeros(weight_ref.shape, F32)
    ids_copy.wait()
    for w in range(flight):
        score = dot(joined[w][:, rep * width :], placed_ref[w], ((0,), (0,)))
        score = jnp.sum(score, axis=0, keepdims=True)
        match = ids[...] == jnp.bitwise_xor(mine, w) * spacing
        result = result + jnp.where(match, score, 0.0)
    weight_ref[...] = result


def local(
    tokens, out_grad, expert_ids, route_weight, live_count, cap_blocks, w_gate, w_up, w_down_t
):
    rep = lax.axis_size("rep")
    ep = lax.axis_size("ep")
    far = rep // 2
    flight = ep // SPLIT
    count = ep // CORES
    tok_count, model_dim = tokens.shape
    width, units = w_gate.shape
    rows = count * SLOT
    ids_rows, rw_rows, caps = expert_ids.T, route_weight.T, cap_blocks.T

    def send(array, rep_bits, ep_bits):
        mask = rep_bits * ep + ep_bits
        pairs = [(a, a ^ mask) for a in range(rep * ep)]
        return lax.ppermute(array, ("rep", "ep"), pairs)

    def after(array, *others):
        return lax.optimization_barrier((array,) + others)[0]

    packed = call(
        functools.partial(pack_kernel, rep, flight),
        [shape((SLOT, 2 * model_dim + LANES))] * flight
        + [shape((flight, CHIPS * SLOT, tok_count)), shape((width, 3 * units))],
        [live_count, tokens, out_grad, ids_rows, rw_rows, w_gate, w_up, w_down_t],
        stored=range(8),
        kept=(flight + 1,),
        scratch=[
            pltpu.SMEM(live_count.shape, jnp.int32),
            pltpu.VMEM(ids_rows.shape, jnp.int32),
            pltpu.VMEM(rw_rows.shape, BF16),
            pltpu.VMEM((2, tok_count, model_dim), BF16),
            pltpu.VMEM((rep, SLOT, width), BF16),
            pltpu.VMEM((width, 3 * units), BF16),
            pltpu.SemaphoreType.DMA((2 * PARTS + 11,)),
        ],
        grant=54,
    )
    pays, placed, weights = packed[:flight], packed[flight], packed[flight + 1]

    half = width // 2
    whole = {0: weights}
    halves = {}
    for k in range(1, rep):
        low, high = k & -k, 1 << (k.bit_length() - 1)
        if low == high:
            whole[k] = send(weights, k, 0)
            for h in range(2):
                kernel = functools.partial(half_kernel, h * half)
                (halves[k, h],) = call(kernel, [shape((half, 3 * units))], [whole[k]])
        else:
            halves[k, 0] = send(halves[k ^ low, 0], low, 0)
            halves[k, 1] = send(halves[k ^ high, 1], high, 0)
    spans, pieces = [], []
    for k in range(rep):
        if k in whole:
            spans.append((k, 0, width))
            pieces.append(whole[k])
        else:
            spans += [(k, 0, half), (k, half, width)]
            pieces += [halves[k, 0], halves[k, 1]]

    order = [turned(n) for n in range(count)]
    blocks = [send(pays[j // CHIPS], 0, CORES * j) if j else pays[0] for j in order]
    nearest = blocks[order.index(1)]
    ready = [after(b, nearest) if j == 0 else b for j, b in zip(order, blocks)]
    blocks = blocks + [send(block, 0, 1) for block in ready]
    results = call(
        functools.partial(hidden_kernel, rep, count, tuple(spans)),
        [shape((rows, model_dim + LANES))] * 2
        + [shape((2 * rows, 3 * units)), shape((2, 2 * rows, width))]
        + [shape((2 * rows, width + 3 * units))] * (rep - 1),
        [caps] + blocks + pieces,
        stored=(0,),
        scratch=[pltpu.SMEM(caps.shape, jnp.int32), pltpu.SemaphoreType.DMA(())],
        flops=2 * 2 * rows * model_dim * 5 * units,
    )
    own, other, grads, here, away = *results[:4], results[4:]
    summed = call(sum_kernel, [shape((SLOT, model_dim + LANES))] * count, [own, send(other, 0, 1)])
    backs = [send(part, 0, CORES * j) if j else part for j, part in zip(order, summed)]

    near = [k for k in range(1, rep) if k & (k - 1) == 0]
    far = [k for k in range(1, rep) if k & (k - 1)]
    near_moved = [send(away[k - 1], k, 0) for k in near]
    (stacked,) = call(stack_kernel, [shape((len(near), 2 * rows, width))], near_moved)
    near_other = send(stacked, 0, 1)
    far_moved = [send(after(away[k - 1], summed[-2]), k, 0) for k in far]
    ready = [after(far_moved[0], stacked)] + far_moved[1:]
    (stacked,) = call(stack_kernel, [shape((len(far), 2 * rows, width))], ready)
    far_other = send(stacked, 0, 1)
    grad_gate, grad_up, grad_down = call(
        functools.partial(weight_kernel, rep),
        [shape((width, units))] * 3,
        [here, grads, near_other, far_other] + near_moved + far_moved,
        kept=(0, 1, 2),
        scratch=[pltpu.VMEM((width, units), BF16)] * 3 + [pltpu.SemaphoreType.DMA((3,))],
        flops=2 * 2 * rep * rows * width * 3 * units,
    )
    grad_tokens, grad_weight = call(
        functools.partial(token_kernel, rep, flight),
        [shape((tok_count, model_dim)), shape(ids_rows.shape, F32)],
        [ids_rows, placed] + backs,
        stored=(0,),
        scratch=[
            pltpu.VMEM((rep, tok_count, width), BF16),
            pltpu.VMEM(ids_rows.shape, jnp.int32),
            pltpu.SemaphoreType.DMA((1,)),
        ],
        flops=1000 * 2 * tok_count * CHIPS * SLOT * model_dim,
    )
    return grad_tokens, grad_weight.T, grad_gate, grad_up, grad_down


def solution(mesh):
    return jax.shard_map(
        local,
        mesh=mesh,
        in_specs=(
            P(("rep", "ep"), None),
            P(("rep", "ep"), None),
            P(("rep", "ep"), None),
            P(("rep", "ep"), None),
            P(),
            P(),
            P("rep", "ep"),
            P("rep", "ep"),
            P("rep", "ep"),
        ),
        out_specs=(
            P(("rep", "ep"), None),
            P(("rep", "ep"), None),
            P("rep", "ep"),
            P("rep", "ep"),
            P("rep", "ep"),
        ),
        check_vma=False,
    )
```

```python
import functools

import jax
import jax.numpy as jnp
from jax import lax
from jax.experimental import pallas as pl
from jax.experimental.pallas import tpu as pltpu
from jax.sharding import PartitionSpec as P

EXPERTS = 128
SLOT = 16
BLOCK = 128
SPLIT = 8
CORES = 2
CHIPS = SPLIT // CORES
LANES = 128
F32 = jnp.float32
BF16 = jnp.bfloat16
PARTS = 4
HBM = pl.BlockSpec(memory_space=pltpu.HBM)
VMEM = pl.BlockSpec(memory_space=pltpu.VMEM)


def shape(dims, kind=BF16):
    return jax.ShapeDtypeStruct(dims, kind)


def call(kernel, outs, args, stored=(), kept=(), scratch=(), flops=0, grant=16):
    size = sum(a.size * a.dtype.itemsize for a in args) + sum(
        o.size * o.dtype.itemsize for o in outs
    )
    return pl.pallas_call(
        kernel,
        out_shape=tuple(outs),
        in_specs=[HBM if n in stored else VMEM for n in range(len(args))],
        out_specs=tuple([HBM if n in kept else VMEM for n in range(len(outs))]),
        scratch_shapes=scratch,
        compiler_params=pltpu.CompilerParams(vmem_limit_bytes=grant * 1024 * 1024),
        cost_estimate=pl.CostEstimate(flops=flops, bytes_accessed=size, transcendentals=0),
    )(*args)


def fetch(pairs, sems, first=0):
    copies = [
        pltpu.make_async_copy(source, target, sems.at[first + n])
        for n, (source, target) in enumerate(pairs)
    ]
    for copy in copies:
        copy.start()
    return copies


def dot(a, b, dims=((1,), (0,))):
    return lax.dot_general(a, b, (dims, ((), ())), preferred_element_type=F32)


def iota(dims, axis):
    return lax.broadcasted_iota(jnp.int32, dims, axis)


def turned(n):
    return n ^ (CHIPS - 1)


def pack_kernel(rep, flight, live_ref, tok_ref, grad_ref, ids_ref, rw_ref, *refs):
    stored, pays, placed_ref, all_ref = refs[:3], refs[3 : 3 + flight], refs[-9], refs[-8]
    live, ids_held, rw_held, data, rows, joined, sems = refs[-7:]
    r = lax.axis_index("rep")
    mine = lax.axis_index("ep") // SPLIT
    count, model = tok_ref.shape
    width = model // rep
    spacing = EXPERTS // flight
    small = fetch([(live_ref, live), (ids_ref, ids_held), (rw_ref, rw_held)], sems)
    units = stored[0].shape[1]
    piece = width // 2
    pairs = []
    for p in range(2):
        some = pl.ds(p * piece, piece)
        for n, ref in enumerate(stored):
            pairs.append((ref.at[some], joined.at[some, pl.ds(n * units, units)]))
    weight_copies = fetch(pairs, sems, 3)
    pairs = []
    for part, ref in enumerate((tok_ref, grad_ref)):
        for p in range(PARTS):
            some = pl.ds(p * (count // PARTS), count // PARTS)
            pairs.append((ref.at[some], data.at[part, some]))
    large = fetch(pairs, sems, 9)
    for copy in small:
        copy.wait()
    token = iota((1, count), 1)
    upper = (iota((count, count), 0) <= iota((count, count), 1)).astype(BF16)
    slot = iota((SLOT, count), 0).astype(F32)
    lane = iota((SLOT, LANES), 1)
    ids = ids_held[...]
    weights = rw_held[...].astype(F32)
    firsts = []
    for w in range(flight):
        expert = jnp.bitwise_xor(mine, w)
        match = ids == expert * spacing
        routed = jnp.any(match, axis=0, keepdims=True) & (token < live[r])
        weight = jnp.sum(jnp.where(match, weights, 0.0), axis=0, keepdims=True)
        routed = jnp.broadcast_to(jnp.where(routed, 1.0, 0.0), (SLOT, count))
        rank = dot(routed.astype(BF16), upper) - 1.0
        placed = jnp.where(rank == slot, routed, 0.0)
        column = jnp.sum(placed * weight, axis=1, keepdims=True)
        pays[w][:, 2 * model :] = jnp.where(lane == 0, column, 0.0).astype(BF16)
        placed = placed.astype(BF16)
        firsts.append(placed)
        placed_ref[w] = jnp.concatenate([placed] * CHIPS, axis=0)
    out_copies = []
    for p in range(2):
        for n in range(len(stored)):
            weight_copies[3 * p + n].wait()
        some = pl.ds(p * piece, piece)
        out_copies += fetch([(joined.at[some], all_ref.at[some])], sems, 9 + 2 * PARTS + p)
    for part in range(2):
        for p in range(PARTS):
            large[part * PARTS + p].wait()
        for w in range(flight):
            chosen = dot(firsts[w], data[part]).astype(BF16)
            for b in range(rep):
                rows[b] = chosen[:, b * width : (b + 1) * width]
            for k in range(rep):
                n = 2 * k + part
                pays[w][:, n * width : (n + 1) * width] = rows[jnp.bitwise_xor(r, k)]
    for copy in out_copies:
        copy.wait()


def half_kernel(start, all_ref, half_ref):
    half_ref[...] = all_ref[start : start + half_ref.shape[0]]


def hidden_kernel(rep, count, spans, cap_ref, *refs):
    blocks, pieces = refs[: 2 * count], refs[2 * count : 2 * count + len(spans)]
    outs, cap, sem = refs[2 * count + len(spans) : -2], refs[-2], refs[-1]
    own_ref, other_ref, grads_ref, here_ref, away_refs = *outs[:4], outs[4:]
    cap_copy = pltpu.make_async_copy(cap_ref, cap, sem)
    cap_copy.start()
    width = here_ref.shape[2]
    units = pieces[0].shape[1] // 3
    own_rows = count * SLOT
    r = lax.axis_index("rep")
    e = lax.axis_index("ep")
    mine = e // SPLIT
    inputs = [[], []]
    for k in range(rep):
        for part in range(2):
            n = 2 * k + part
            chosen = [b[:, n * width : (n + 1) * width] for b in blocks]
            chosen = jnp.concatenate(chosen, axis=0)
            inputs[part].append(chosen)
            if k == 0:
                here_ref[part] = chosen
            else:
                some = slice(part * own_rows, (part + 1) * own_rows)
                away_refs[k - 1][some, :width] = chosen[:own_rows]
    sum_x, sum_d = 0.0, 0.0
    for (k, start, stop), piece in zip(spans, pieces):
        sum_x = sum_x + dot(inputs[0][k][:, start:stop], piece[:, : 2 * units])
        sum_d = sum_d + dot(inputs[1][k][:, start:stop], piece[:, 2 * units :])

    cap_copy.wait()
    capacity = (BLOCK * cap[mine, r]).astype(F32)
    lane = iota((SLOT, LANES), 1)
    sources, rates, counts = [], [], []
    for n in range(2 * count):
        sources.append(jnp.bitwise_xor(e, CORES * turned(n % count) + n // count))
        rate = jnp.where(lane == 0, blocks[n][:, 2 * rep * width :].astype(F32), 0.0)
        rate = jnp.sum(rate, axis=1, keepdims=True)
        rates.append(rate)
        counts.append(jnp.sum(jnp.where(rate > 0.0, 1.0, 0.0), axis=0, keepdims=True))
    slot = iota((SLOT, 1), 0).astype(F32)
    rate_rows, kept_rows = [], []
    for n in range(2 * count):
        start = jnp.zeros((1, 1), F32)
        for other in range(2 * count):
            start = start + jnp.where(sources[other] < sources[n], counts[other], 0.0)
        kept = jnp.where((rates[n] > 0.0) & (start + slot < capacity), 1.0, 0.0)
        kept_rows.append(kept)
        rate_rows.append(rates[n] * kept)
    rate = jnp.concatenate(rate_rows, axis=0)
    kept = jnp.concatenate(kept_rows, axis=0)

    pre_gate, pre_up, back_hidden = sum_x[:, :units], sum_x[:, units:], sum_d
    sig = 1.0 / (1.0 + jnp.exp(-pre_gate))
    activated = pre_gate * sig
    hidden = activated * pre_up
    score = jnp.sum(hidden * back_hidden, axis=1, keepdims=True) * kept
    lane = iota((2 * own_rows, LANES), 1)
    scores = jnp.where(lane == e % CORES, score, 0.0).astype(BF16)
    scaled = back_hidden * rate
    gate_grad = (scaled * pre_up * sig * (1.0 + pre_gate * (1.0 - sig))).astype(BF16)
    up_grad = (scaled * activated).astype(BF16)
    weighted = (hidden * rate).astype(BF16)
    grads_ref[...] = jnp.concatenate([gate_grad, up_grad, weighted], axis=1)
    for ref in away_refs:
        ref[:, width:] = grads_ref[...]
    pair = jnp.concatenate([gate_grad, up_grad], axis=1)
    for (k, start, stop), piece in zip(spans, pieces):
        back = dot(pair, piece[:, : 2 * units], ((1,), (1,))).astype(BF16)
        some = slice(k * width + start, k * width + stop)
        own_ref[:, some] = back[:own_rows]
        other_ref[:, some] = back[own_rows:]
    own_ref[:, rep * width :] = scores[:own_rows]
    other_ref[:, rep * width :] = scores[own_rows:]


def sum_kernel(own_ref, got_ref, *outs):
    for j, out in enumerate(outs):
        some = slice(j * SLOT, (j + 1) * SLOT)
        out[...] = (own_ref[some].astype(F32) + got_ref[some].astype(F32)).astype(BF16)


def stack_kernel(*refs):
    for k, ref in enumerate(refs[:-1]):
        refs[-1][k] = ref[:, : refs[-1].shape[2]]


def weight_kernel(rep, here_ref, grads_ref, near_ref, far_ref, *refs):
    away, outs, held, sems = refs[: rep - 1], refs[rep - 1 : -4], refs[-4:-1], refs[-1]
    units = outs[0].shape[1]
    width = here_ref.shape[2]
    half = grads_ref.shape[0] // 2
    copies = []
    for part, columns in enumerate((slice(0, 2 * units), slice(2 * units, 3 * units))):
        some = slice(part * half, (part + 1) * half)
        rows = [here_ref[part]]
        got = [grads_ref[:, columns]]
        others = [ref[k, some] for ref in (near_ref, far_ref) for k in range(ref.shape[0])]
        for other, ref in zip(others, away):
            rows += [ref[some, :width], other]
            got.append(ref[:, width + columns.start : width + columns.stop])
        rows = jnp.concatenate(rows, axis=0)
        got = jnp.concatenate(got, axis=0)
        total = dot(got, rows, ((0,), (0,)))
        for n in range(total.shape[0] // units):
            held[2 * part + n][...] = total[n * units : (n + 1) * units].T.astype(BF16)
            copies += fetch([(held[2 * part + n], outs[2 * part + n])], sems, 2 * part + n)
    for copy in copies:
        copy.wait()


def token_kernel(rep, flight, ids_ref, placed_ref, *refs):
    backs, rest = refs[: flight * CHIPS], refs[flight * CHIPS :]
    out_ref, weight_ref, blocks, ids, sems = rest
    (ids_copy,) = fetch([(ids_ref, ids)], sems)
    r = lax.axis_index("rep")
    mine = lax.axis_index("ep") // SPLIT
    spacing = EXPERTS // flight
    width = out_ref.shape[1] // rep
    joined = [
        jnp.concatenate([b[...] for b in backs[w * CHIPS : (w + 1) * CHIPS]], axis=0)
        for w in range(flight)
    ]
    for k in range(rep):
        total = 0.0
        for w in range(flight):
            some = joined[w][:, k * width : (k + 1) * width]
            total = total + dot(placed_ref[w], some, ((0,), (0,)))
        blocks[jnp.bitwise_xor(r, k)] = total.astype(BF16)
    for b in range(rep):
        out_ref[:, b * width : (b + 1) * width] = blocks[b]
    result = jnp.zeros(weight_ref.shape, F32)
    ids_copy.wait()
    for w in range(flight):
        score = dot(joined[w][:, rep * width :], placed_ref[w], ((0,), (0,)))
        score = jnp.sum(score, axis=0, keepdims=True)
        match = ids[...] == jnp.bitwise_xor(mine, w) * spacing
        result = result + jnp.where(match, score, 0.0)
    weight_ref[...] = result


def local(
    tokens, out_grad, expert_ids, route_weight, live_count, cap_blocks, w_gate, w_up, w_down_t
):
    rep = lax.axis_size("rep")
    ep = lax.axis_size("ep")
    far = rep // 2
    flight = ep // SPLIT
    count = ep // CORES
    tok_count, model_dim = tokens.shape
    width, units = w_gate.shape
    rows = count * SLOT
    ids_rows, rw_rows, caps = expert_ids.T, route_weight.T, cap_blocks.T

    def send(array, rep_bits, ep_bits):
        mask = rep_bits * ep + ep_bits
        pairs = [(a, a ^ mask) for a in range(rep * ep)]
        return lax.ppermute(array, ("rep", "ep"), pairs)

    def after(array, *others):
        return lax.optimization_barrier((array,) + others)[0]

    packed = call(
        functools.partial(pack_kernel, rep, flight),
        [shape((SLOT, 2 * model_dim + LANES))] * flight
        + [shape((flight, CHIPS * SLOT, tok_count)), shape((width, 3 * units))],
        [live_count, tokens, out_grad, ids_rows, rw_rows, w_gate, w_up, w_down_t],
        stored=range(8),
        kept=(flight + 1,),
        scratch=[
            pltpu.SMEM(live_count.shape, jnp.int32),
            pltpu.VMEM(ids_rows.shape, jnp.int32),
            pltpu.VMEM(rw_rows.shape, BF16),
            pltpu.VMEM((2, tok_count, model_dim), BF16),
            pltpu.VMEM((rep, SLOT, width), BF16),
            pltpu.VMEM((width, 3 * units), BF16),
            pltpu.SemaphoreType.DMA((2 * PARTS + 11,)),
        ],
        grant=54,
    )
    pays, placed, weights = packed[:flight], packed[flight], packed[flight + 1]

    half = width // 2
    whole = {0: weights}
    halves = {}
    for k in range(1, rep):
        low, high = k & -k, 1 << (k.bit_length() - 1)
        if low == high:
            whole[k] = send(weights, k, 0)
            for h in range(2):
                kernel = functools.partial(half_kernel, h * half)
                (halves[k, h],) = call(kernel, [shape((half, 3 * units))], [whole[k]])
        else:
            halves[k, 0] = send(halves[k ^ low, 0], low, 0)
            halves[k, 1] = send(halves[k ^ high, 1], high, 0)
    spans, pieces = [], []
    for k in range(rep):
        if k in whole:
            spans.append((k, 0, width))
            pieces.append(whole[k])
        else:
            spans += [(k, 0, half), (k, half, width)]
            pieces += [halves[k, 0], halves[k, 1]]

    order = [turned(n) for n in range(count)]
    blocks = [send(pays[j // CHIPS], 0, CORES * j) if j else pays[0] for j in order]
    nearest = blocks[order.index(1)]
    ready = [after(b, nearest) if j == 0 else b for j, b in zip(order, blocks)]
    blocks = blocks + [send(block, 0, 1) for block in ready]
    results = call(
        functools.partial(hidden_kernel, rep, count, tuple(spans)),
        [shape((rows, model_dim + LANES))] * 2
        + [shape((2 * rows, 3 * units)), shape((2, 2 * rows, width))]
        + [shape((2 * rows, width + 3 * units))] * (rep - 1),
        [caps] + blocks + pieces,
        stored=(0,),
        scratch=[pltpu.SMEM(caps.shape, jnp.int32), pltpu.SemaphoreType.DMA(())],
        flops=2 * 2 * rows * model_dim * 5 * units,
    )
    own, other, grads, here, away = *results[:4], results[4:]
    summed = call(sum_kernel, [shape((SLOT, model_dim + LANES))] * count, [own, send(other, 0, 1)])
    backs = [send(part, 0, CORES * j) if j else part for j, part in zip(order, summed)]

    near = [k for k in range(1, rep) if k & (k - 1) == 0]
    far = [k for k in range(1, rep) if k & (k - 1)]
    near_moved = [send(away[k - 1], k, 0) for k in near]
    (stacked,) = call(stack_kernel, [shape((len(near), 2 * rows, width))], near_moved)
    near_other = send(stacked, 0, 1)
    grad_tokens, grad_weight = call(
        functools.partial(token_kernel, rep, flight),
        [shape((tok_count, model_dim)), shape(ids_rows.shape, F32)],
        [ids_rows, placed] + backs,
        stored=(0,),
        scratch=[
            pltpu.VMEM((rep, tok_count, width), BF16),
            pltpu.VMEM(ids_rows.shape, jnp.int32),
            pltpu.SemaphoreType.DMA((1,)),
        ],
        flops=40 * 2 * tok_count * CHIPS * SLOT * model_dim,
    )
    far_moved = [send(after(away[k - 1], summed[-2]), k, 0) for k in far]
    ready = [after(far_moved[0], stacked, grad_weight)] + far_moved[1:]
    (stacked,) = call(stack_kernel, [shape((len(far), 2 * rows, width))], ready)
    far_other = send(stacked, 0, 1)
    grad_gate, grad_up, grad_down = call(
        functools.partial(weight_kernel, rep),
        [shape((width, units))] * 3,
        [here, grads, near_other, far_other] + near_moved + far_moved,
        kept=(0, 1, 2),
        scratch=[pltpu.VMEM((width, units), BF16)] * 3 + [pltpu.SemaphoreType.DMA((3,))],
        flops=2 * 2 * rep * rows * width * 3 * units,
    )
    return grad_tokens, grad_weight.T, grad_gate, grad_up, grad_down


def solution(mesh):
    return jax.shard_map(
        local,
        mesh=mesh,
        in_specs=(
            P(("rep", "ep"), None),
            P(("rep", "ep"), None),
            P(("rep", "ep"), None),
            P(("rep", "ep"), None),
            P(),
            P(),
            P("rep", "ep"),
            P("rep", "ep"),
            P("rep", "ep"),
        ),
        out_specs=(
            P(("rep", "ep"), None),
            P(("rep", "ep"), None),
            P("rep", "ep"),
            P("rep", "ep"),
            P("rep", "ep"),
        ),
        check_vma=False,
    )
```

```python
import functools

import jax
import jax.numpy as jnp
from jax import lax
from jax.experimental import pallas as pl
from jax.experimental.pallas import tpu as pltpu
from jax.sharding import PartitionSpec as P

EXPERTS = 128
SLOT = 16
BLOCK = 128
SPLIT = 8
CORES = 2
CHIPS = SPLIT // CORES
LANES = 128
F32 = jnp.float32
BF16 = jnp.bfloat16
PARTS = 4
HBM = pl.BlockSpec(memory_space=pltpu.HBM)
VMEM = pl.BlockSpec(memory_space=pltpu.VMEM)


def shape(dims, kind=BF16):
    return jax.ShapeDtypeStruct(dims, kind)


def call(kernel, outs, args, stored=(), kept=(), scratch=(), flops=0, grant=16):
    size = sum(a.size * a.dtype.itemsize for a in args) + sum(
        o.size * o.dtype.itemsize for o in outs
    )
    return pl.pallas_call(
        kernel,
        out_shape=tuple(outs),
        in_specs=[HBM if n in stored else VMEM for n in range(len(args))],
        out_specs=tuple([HBM if n in kept else VMEM for n in range(len(outs))]),
        scratch_shapes=scratch,
        compiler_params=pltpu.CompilerParams(vmem_limit_bytes=grant * 1024 * 1024),
        cost_estimate=pl.CostEstimate(flops=flops, bytes_accessed=size, transcendentals=0),
    )(*args)


def fetch(pairs, sems, first=0):
    copies = [
        pltpu.make_async_copy(source, target, sems.at[first + n])
        for n, (source, target) in enumerate(pairs)
    ]
    for copy in copies:
        copy.start()
    return copies


def dot(a, b, dims=((1,), (0,))):
    return lax.dot_general(a, b, (dims, ((), ())), preferred_element_type=F32)


def iota(dims, axis):
    return lax.broadcasted_iota(jnp.int32, dims, axis)


def turned(n):
    return n ^ (CHIPS - 1)


def pack_kernel(rep, flight, live_ref, tok_ref, grad_ref, ids_ref, rw_ref, *refs):
    stored, pays, placed_ref, all_ref = refs[:3], refs[3 : 3 + flight], refs[-9], refs[-8]
    live, ids_held, rw_held, data, rows, joined, sems = refs[-7:]
    r = lax.axis_index("rep")
    mine = lax.axis_index("ep") // SPLIT
    count, model = tok_ref.shape
    width = model // rep
    spacing = EXPERTS // flight
    small = fetch([(live_ref, live), (ids_ref, ids_held), (rw_ref, rw_held)], sems)
    units = stored[0].shape[1]
    piece = width // 2
    pairs = []
    for p in range(2):
        some = pl.ds(p * piece, piece)
        for n, ref in enumerate(stored):
            pairs.append((ref.at[some], joined.at[some, pl.ds(n * units, units)]))
    weight_copies = fetch(pairs, sems, 3)
    pairs = []
    for part, ref in enumerate((tok_ref, grad_ref)):
        for p in range(PARTS):
            some = pl.ds(p * (count // PARTS), count // PARTS)
            pairs.append((ref.at[some], data.at[part, some]))
    large = fetch(pairs, sems, 9)
    for copy in small:
        copy.wait()
    token = iota((1, count), 1)
    upper = (iota((count, count), 0) <= iota((count, count), 1)).astype(BF16)
    slot = iota((SLOT, count), 0).astype(F32)
    lane = iota((SLOT, LANES), 1)
    ids = ids_held[...]
    weights = rw_held[...].astype(F32)
    firsts = []
    for w in range(flight):
        expert = jnp.bitwise_xor(mine, w)
        match = ids == expert * spacing
        routed = jnp.any(match, axis=0, keepdims=True) & (token < live[r])
        weight = jnp.sum(jnp.where(match, weights, 0.0), axis=0, keepdims=True)
        routed = jnp.broadcast_to(jnp.where(routed, 1.0, 0.0), (SLOT, count))
        rank = dot(routed.astype(BF16), upper) - 1.0
        placed = jnp.where(rank == slot, routed, 0.0)
        column = jnp.sum(placed * weight, axis=1, keepdims=True)
        pays[w][:, 2 * model :] = jnp.where(lane == 0, column, 0.0).astype(BF16)
        placed = placed.astype(BF16)
        firsts.append(placed)
        placed_ref[w] = jnp.concatenate([placed] * CHIPS, axis=0)
    out_copies = []
    for p in range(2):
        for n in range(len(stored)):
            weight_copies[3 * p + n].wait()
        some = pl.ds(p * piece, piece)
        out_copies += fetch([(joined.at[some], all_ref.at[some])], sems, 9 + 2 * PARTS + p)
    for part in range(2):
        for p in range(PARTS):
            large[part * PARTS + p].wait()
        for w in range(flight):
            chosen = dot(firsts[w], data[part]).astype(BF16)
            for b in range(rep):
                rows[b] = chosen[:, b * width : (b + 1) * width]
            for k in range(rep):
                n = 2 * k + part
                pays[w][:, n * width : (n + 1) * width] = rows[jnp.bitwise_xor(r, k)]
    for copy in out_copies:
        copy.wait()


def half_kernel(start, all_ref, half_ref):
    half_ref[...] = all_ref[start : start + half_ref.shape[0]]


def hidden_kernel(rep, count, spans, cap_ref, *refs):
    blocks, pieces = refs[: 2 * count], refs[2 * count : 2 * count + len(spans)]
    outs, cap, sem = refs[2 * count + len(spans) : -2], refs[-2], refs[-1]
    own_ref, other_ref, grads_ref, here_ref, away_refs = *outs[:4], outs[4:]
    cap_copy = pltpu.make_async_copy(cap_ref, cap, sem)
    cap_copy.start()
    width = here_ref.shape[2]
    units = pieces[0].shape[1] // 3
    own_rows = count * SLOT
    r = lax.axis_index("rep")
    e = lax.axis_index("ep")
    mine = e // SPLIT
    inputs = [[], []]
    for k in range(rep):
        for part in range(2):
            n = 2 * k + part
            chosen = [b[:, n * width : (n + 1) * width] for b in blocks]
            chosen = jnp.concatenate(chosen, axis=0)
            inputs[part].append(chosen)
            if k == 0:
                here_ref[part] = chosen
            else:
                some = slice(part * own_rows, (part + 1) * own_rows)
                away_refs[k - 1][some, :width] = chosen[:own_rows]
    sum_x, sum_d = 0.0, 0.0
    for (k, start, stop), piece in zip(spans, pieces):
        sum_x = sum_x + dot(inputs[0][k][:, start:stop], piece[:, : 2 * units])
        sum_d = sum_d + dot(inputs[1][k][:, start:stop], piece[:, 2 * units :])

    cap_copy.wait()
    capacity = (BLOCK * cap[mine, r]).astype(F32)
    lane = iota((SLOT, LANES), 1)
    sources, rates, counts = [], [], []
    for n in range(2 * count):
        sources.append(jnp.bitwise_xor(e, CORES * turned(n % count) + n // count))
        rate = jnp.where(lane == 0, blocks[n][:, 2 * rep * width :].astype(F32), 0.0)
        rate = jnp.sum(rate, axis=1, keepdims=True)
        rates.append(rate)
        counts.append(jnp.sum(jnp.where(rate > 0.0, 1.0, 0.0), axis=0, keepdims=True))
    slot = iota((SLOT, 1), 0).astype(F32)
    rate_rows, kept_rows = [], []
    for n in range(2 * count):
        start = jnp.zeros((1, 1), F32)
        for other in range(2 * count):
            start = start + jnp.where(sources[other] < sources[n], counts[other], 0.0)
        kept = jnp.where((rates[n] > 0.0) & (start + slot < capacity), 1.0, 0.0)
        kept_rows.append(kept)
        rate_rows.append(rates[n] * kept)
    rate = jnp.concatenate(rate_rows, axis=0)
    kept = jnp.concatenate(kept_rows, axis=0)

    pre_gate, pre_up, back_hidden = sum_x[:, :units], sum_x[:, units:], sum_d
    sig = 1.0 / (1.0 + jnp.exp(-pre_gate))
    activated = pre_gate * sig
    hidden = activated * pre_up
    score = jnp.sum(hidden * back_hidden, axis=1, keepdims=True) * kept
    lane = iota((2 * own_rows, LANES), 1)
    scores = jnp.where(lane == e % CORES, score, 0.0).astype(BF16)
    scaled = back_hidden * rate
    gate_grad = (scaled * pre_up * sig * (1.0 + pre_gate * (1.0 - sig))).astype(BF16)
    up_grad = (scaled * activated).astype(BF16)
    weighted = (hidden * rate).astype(BF16)
    grads_ref[...] = jnp.concatenate([gate_grad, up_grad, weighted], axis=1)
    for ref in away_refs:
        ref[:, width:] = grads_ref[...]
    pair = jnp.concatenate([gate_grad, up_grad], axis=1)
    for (k, start, stop), piece in zip(spans, pieces):
        back = dot(pair, piece[:, : 2 * units], ((1,), (1,))).astype(BF16)
        some = slice(k * width + start, k * width + stop)
        own_ref[:, some] = back[:own_rows]
        other_ref[:, some] = back[own_rows:]
    own_ref[:, rep * width :] = scores[:own_rows]
    other_ref[:, rep * width :] = scores[own_rows:]


def sum_kernel(own_ref, got_ref, *outs):
    for j, out in enumerate(outs):
        some = slice(j * SLOT, (j + 1) * SLOT)
        out[...] = (own_ref[some].astype(F32) + got_ref[some].astype(F32)).astype(BF16)


def stack_kernel(*refs):
    for k, ref in enumerate(refs[:-1]):
        refs[-1][k] = ref[:, : refs[-1].shape[2]]


def weight_kernel(rep, here_ref, grads_ref, near_ref, far_ref, *refs):
    away, outs, held, sems = refs[: rep - 1], refs[rep - 1 : -4], refs[-4:-1], refs[-1]
    units = outs[0].shape[1]
    width = here_ref.shape[2]
    half = grads_ref.shape[0] // 2
    copies = []
    for part, columns in enumerate((slice(0, 2 * units), slice(2 * units, 3 * units))):
        some = slice(part * half, (part + 1) * half)
        rows = [here_ref[part]]
        got = [grads_ref[:, columns]]
        others = [ref[k, some] for ref in (near_ref, far_ref) for k in range(ref.shape[0])]
        for other, ref in zip(others, away):
            rows += [ref[some, :width], other]
            got.append(ref[:, width + columns.start : width + columns.stop])
        rows = jnp.concatenate(rows, axis=0)
        got = jnp.concatenate(got, axis=0)
        total = dot(got, rows, ((0,), (0,)))
        for n in range(total.shape[0] // units):
            held[2 * part + n][...] = total[n * units : (n + 1) * units].T.astype(BF16)
            copies += fetch([(held[2 * part + n], outs[2 * part + n])], sems, 2 * part + n)
    for copy in copies:
        copy.wait()


def token_kernel(rep, flight, ids_ref, placed_ref, *refs):
    backs, rest = refs[: flight * CHIPS], refs[flight * CHIPS :]
    out_ref, weight_ref, blocks, ids, sems = rest
    (ids_copy,) = fetch([(ids_ref, ids)], sems)
    r = lax.axis_index("rep")
    mine = lax.axis_index("ep") // SPLIT
    spacing = EXPERTS // flight
    width = out_ref.shape[1] // rep
    joined = [
        jnp.concatenate([b[...] for b in backs[w * CHIPS : (w + 1) * CHIPS]], axis=0)
        for w in range(flight)
    ]
    for k in range(rep):
        total = 0.0
        for w in range(flight):
            some = joined[w][:, k * width : (k + 1) * width]
            total = total + dot(placed_ref[w], some, ((0,), (0,)))
        blocks[jnp.bitwise_xor(r, k)] = total.astype(BF16)
    for b in range(rep):
        out_ref[:, b * width : (b + 1) * width] = blocks[b]
    result = jnp.zeros(weight_ref.shape, F32)
    ids_copy.wait()
    for w in range(flight):
        score = dot(joined[w][:, rep * width :], placed_ref[w], ((0,), (0,)))
        score = jnp.sum(score, axis=0, keepdims=True)
        match = ids[...] == jnp.bitwise_xor(mine, w) * spacing
        result = result + jnp.where(match, score, 0.0)
    weight_ref[...] = result


def local(
    tokens, out_grad, expert_ids, route_weight, live_count, cap_blocks, w_gate, w_up, w_down_t
):
    rep = lax.axis_size("rep")
    ep = lax.axis_size("ep")
    far = rep // 2
    flight = ep // SPLIT
    count = ep // CORES
    tok_count, model_dim = tokens.shape
    width, units = w_gate.shape
    rows = count * SLOT
    ids_rows, rw_rows, caps = expert_ids.T, route_weight.T, cap_blocks.T

    def send(array, rep_bits, ep_bits):
        mask = rep_bits * ep + ep_bits
        pairs = [(a, a ^ mask) for a in range(rep * ep)]
        return lax.ppermute(array, ("rep", "ep"), pairs)

    def after(array, *others):
        return lax.optimization_barrier((array,) + others)[0]

    packed = call(
        functools.partial(pack_kernel, rep, flight),
        [shape((SLOT, 2 * model_dim + LANES))] * flight
        + [shape((flight, CHIPS * SLOT, tok_count)), shape((width, 3 * units))],
        [live_count, tokens, out_grad, ids_rows, rw_rows, w_gate, w_up, w_down_t],
        stored=range(8),
        kept=(flight + 1,),
        scratch=[
            pltpu.SMEM(live_count.shape, jnp.int32),
            pltpu.VMEM(ids_rows.shape, jnp.int32),
            pltpu.VMEM(rw_rows.shape, BF16),
            pltpu.VMEM((2, tok_count, model_dim), BF16),
            pltpu.VMEM((rep, SLOT, width), BF16),
            pltpu.VMEM((width, 3 * units), BF16),
            pltpu.SemaphoreType.DMA((2 * PARTS + 11,)),
        ],
        grant=54,
    )
    pays, placed, weights = packed[:flight], packed[flight], packed[flight + 1]

    half = width // 2 if width % LANES else -(-width // (2 * LANES)) * LANES
    whole = {0: weights}
    halves = {}
    for k in range(1, rep):
        low, high = k & -k, 1 << (k.bit_length() - 1)
        if low == high:
            whole[k] = send(weights, k, 0)
            for h in range(2):
                kernel = functools.partial(half_kernel, h * half)
                size = width - half if h else half
                (halves[k, h],) = call(kernel, [shape((size, 3 * units))], [whole[k]])
        else:
            halves[k, 0] = send(halves[k ^ low, 0], low, 0)
            halves[k, 1] = send(halves[k ^ high, 1], high, 0)
    spans, pieces = [], []
    for k in range(rep):
        if k in whole:
            spans.append((k, 0, width))
            pieces.append(whole[k])
        else:
            spans += [(k, 0, half), (k, half, width)]
            pieces += [halves[k, 0], halves[k, 1]]

    order = [turned(n) for n in range(count)]
    blocks = [send(pays[j // CHIPS], 0, CORES * j) if j else pays[0] for j in order]
    nearest = blocks[order.index(1)]
    ready = [after(b, nearest) if j == 0 else b for j, b in zip(order, blocks)]
    blocks = blocks + [send(block, 0, 1) for block in ready]
    results = call(
        functools.partial(hidden_kernel, rep, count, tuple(spans)),
        [shape((rows, model_dim + LANES))] * 2
        + [shape((2 * rows, 3 * units)), shape((2, 2 * rows, width))]
        + [shape((2 * rows, width + 3 * units))] * (rep - 1),
        [caps] + blocks + pieces,
        stored=(0,),
        scratch=[pltpu.SMEM(caps.shape, jnp.int32), pltpu.SemaphoreType.DMA(())],
        flops=2 * 2 * rows * model_dim * 5 * units,
    )
    own, other, grads, here, away = *results[:4], results[4:]
    summed = call(sum_kernel, [shape((SLOT, model_dim + LANES))] * count, [own, send(other, 0, 1)])
    backs = [send(part, 0, CORES * j) if j else part for j, part in zip(order, summed)]

    near = [k for k in range(1, rep) if k & (k - 1) == 0]
    far = [k for k in range(1, rep) if k & (k - 1)]
    near_moved = [send(away[k - 1], k, 0) for k in near]
    (stacked,) = call(stack_kernel, [shape((len(near), 2 * rows, width))], near_moved)
    near_other = send(stacked, 0, 1)
    far_moved = [send(after(away[k - 1], summed[-2]), k, 0) for k in far]
    ready = [after(far_moved[0], stacked)] + far_moved[1:]
    (stacked,) = call(stack_kernel, [shape((len(far), 2 * rows, width))], ready)
    far_other = send(stacked, 0, 1)
    grad_gate, grad_up, grad_down = call(
        functools.partial(weight_kernel, rep),
        [shape((width, units))] * 3,
        [here, grads, near_other, far_other] + near_moved + far_moved,
        kept=(0, 1, 2),
        scratch=[pltpu.VMEM((width, units), BF16)] * 3 + [pltpu.SemaphoreType.DMA((3,))],
        flops=2 * 2 * rep * rows * width * 3 * units,
    )
    grad_tokens, grad_weight = call(
        functools.partial(token_kernel, rep, flight),
        [shape((tok_count, model_dim)), shape(ids_rows.shape, F32)],
        [ids_rows, placed] + backs,
        stored=(0,),
        scratch=[
            pltpu.VMEM((rep, tok_count, width), BF16),
            pltpu.VMEM(ids_rows.shape, jnp.int32),
            pltpu.SemaphoreType.DMA((1,)),
        ],
        flops=1000 * 2 * tok_count * CHIPS * SLOT * model_dim,
    )
    return grad_tokens, grad_weight.T, grad_gate, grad_up, grad_down


def solution(mesh):
    return jax.shard_map(
        local,
        mesh=mesh,
        in_specs=(
            P(("rep", "ep"), None),
            P(("rep", "ep"), None),
            P(("rep", "ep"), None),
            P(("rep", "ep"), None),
            P(),
            P(),
            P("rep", "ep"),
            P("rep", "ep"),
            P("rep", "ep"),
        ),
        out_specs=(
            P(("rep", "ep"), None),
            P(("rep", "ep"), None),
            P("rep", "ep"),
            P("rep", "ep"),
            P("rep", "ep"),
        ),
        check_vma=False,
    )
```

```python
import functools

import jax
import jax.numpy as jnp
from jax import lax
from jax.experimental import pallas as pl
from jax.experimental.pallas import tpu as pltpu
from jax.sharding import PartitionSpec as P

EXPERTS = 128
SLOT = 16
BLOCK = 128
SPLIT = 8
CORES = 2
CHIPS = SPLIT // CORES
LANES = 128
F32 = jnp.float32
BF16 = jnp.bfloat16
PARTS = 2
HBM = pl.BlockSpec(memory_space=pltpu.HBM)
VMEM = pl.BlockSpec(memory_space=pltpu.VMEM)


def shape(dims, kind=BF16):
    return jax.ShapeDtypeStruct(dims, kind)


def call(kernel, outs, args, stored=(), kept=(), scratch=(), flops=0, grant=16):
    size = sum(a.size * a.dtype.itemsize for a in args) + sum(
        o.size * o.dtype.itemsize for o in outs
    )
    return pl.pallas_call(
        kernel,
        out_shape=tuple(outs),
        in_specs=[HBM if n in stored else VMEM for n in range(len(args))],
        out_specs=tuple([HBM if n in kept else VMEM for n in range(len(outs))]),
        scratch_shapes=scratch,
        compiler_params=pltpu.CompilerParams(vmem_limit_bytes=grant * 1024 * 1024),
        cost_estimate=pl.CostEstimate(flops=flops, bytes_accessed=size, transcendentals=0),
    )(*args)


def fetch(pairs, sems, first=0):
    copies = [
        pltpu.make_async_copy(source, target, sems.at[first + n])
        for n, (source, target) in enumerate(pairs)
    ]
    for copy in copies:
        copy.start()
    return copies


def dot(a, b, dims=((1,), (0,))):
    return lax.dot_general(a, b, (dims, ((), ())), preferred_element_type=F32)


def iota(dims, axis):
    return lax.broadcasted_iota(jnp.int32, dims, axis)


def turned(n):
    return n ^ (CHIPS - 1)


def pack_kernel(rep, flight, live_ref, tok_ref, grad_ref, ids_ref, rw_ref, *refs):
    stored, pays, placed_ref, all_ref = refs[:3], refs[3 : 3 + flight], refs[-9], refs[-8]
    live, ids_held, rw_held, data, rows, joined, sems = refs[-7:]
    r = lax.axis_index("rep")
    mine = lax.axis_index("ep") // SPLIT
    count, model = tok_ref.shape
    width = model // rep
    spacing = EXPERTS // flight
    small = fetch([(live_ref, live), (ids_ref, ids_held), (rw_ref, rw_held)], sems)
    units = stored[0].shape[1]
    piece = width // 2
    pairs = []
    for p in range(2):
        some = pl.ds(p * piece, piece)
        for n, ref in enumerate(stored):
            pairs.append((ref.at[some], joined.at[some, pl.ds(n * units, units)]))
    weight_copies = fetch(pairs, sems, 3)
    pairs = []
    for part, ref in enumerate((tok_ref, grad_ref)):
        for p in range(PARTS):
            some = pl.ds(p * (count // PARTS), count // PARTS)
            pairs.append((ref.at[some], data.at[part, some]))
    large = fetch(pairs, sems, 9)
    for copy in small:
        copy.wait()
    token = iota((1, count), 1)
    upper = (iota((count, count), 0) <= iota((count, count), 1)).astype(BF16)
    slot = iota((SLOT, count), 0).astype(F32)
    lane = iota((SLOT, LANES), 1)
    ids = ids_held[...]
    weights = rw_held[...].astype(F32)
    firsts = []
    for w in range(flight):
        expert = jnp.bitwise_xor(mine, w)
        match = ids == expert * spacing
        routed = jnp.any(match, axis=0, keepdims=True) & (token < live[r])
        weight = jnp.sum(jnp.where(match, weights, 0.0), axis=0, keepdims=True)
        routed = jnp.broadcast_to(jnp.where(routed, 1.0, 0.0), (SLOT, count))
        rank = dot(routed.astype(BF16), upper) - 1.0
        placed = jnp.where(rank == slot, routed, 0.0)
        column = jnp.sum(placed * weight, axis=1, keepdims=True)
        pays[w][:, 2 * model :] = jnp.where(lane == 0, column, 0.0).astype(BF16)
        placed = placed.astype(BF16)
        firsts.append(placed)
        placed_ref[w] = jnp.concatenate([placed] * CHIPS, axis=0)
    out_copies = []
    for p in range(2):
        for n in range(len(stored)):
            weight_copies[3 * p + n].wait()
        some = pl.ds(p * piece, piece)
        out_copies += fetch([(joined.at[some], all_ref.at[some])], sems, 9 + 2 * PARTS + p)
    for part in range(2):
        for p in range(PARTS):
            large[part * PARTS + p].wait()
        for w in range(flight):
            chosen = dot(firsts[w], data[part]).astype(BF16)
            for b in range(rep):
                rows[b] = chosen[:, b * width : (b + 1) * width]
            for k in range(rep):
                n = 2 * k + part
                pays[w][:, n * width : (n + 1) * width] = rows[jnp.bitwise_xor(r, k)]
    for copy in out_copies:
        copy.wait()


def half_kernel(start, all_ref, half_ref):
    half_ref[...] = all_ref[start : start + half_ref.shape[0]]


def hidden_kernel(rep, count, spans, cap_ref, *refs):
    blocks, pieces = refs[: 2 * count], refs[2 * count : 2 * count + len(spans)]
    outs, cap, sem = refs[2 * count + len(spans) : -2], refs[-2], refs[-1]
    own_ref, other_ref, grads_ref, here_ref, away_refs = *outs[:4], outs[4:]
    cap_copy = pltpu.make_async_copy(cap_ref, cap, sem)
    cap_copy.start()
    width = here_ref.shape[2]
    units = pieces[0].shape[1] // 3
    own_rows = count * SLOT
    r = lax.axis_index("rep")
    e = lax.axis_index("ep")
    mine = e // SPLIT
    inputs = [[], []]
    for k in range(rep):
        for part in range(2):
            n = 2 * k + part
            chosen = [b[:, n * width : (n + 1) * width] for b in blocks]
            chosen = jnp.concatenate(chosen, axis=0)
            inputs[part].append(chosen)
            if k == 0:
                here_ref[part] = chosen
            else:
                some = slice(part * own_rows, (part + 1) * own_rows)
                away_refs[k - 1][some, :width] = chosen[:own_rows]
    sum_x, sum_d = 0.0, 0.0
    for (k, start, stop), piece in zip(spans, pieces):
        sum_x = sum_x + dot(inputs[0][k][:, start:stop], piece[:, : 2 * units])
        sum_d = sum_d + dot(inputs[1][k][:, start:stop], piece[:, 2 * units :])

    cap_copy.wait()
    capacity = (BLOCK * cap[mine, r]).astype(F32)
    lane = iota((SLOT, LANES), 1)
    sources, rates, counts = [], [], []
    for n in range(2 * count):
        sources.append(jnp.bitwise_xor(e, CORES * turned(n % count) + n // count))
        rate = jnp.where(lane == 0, blocks[n][:, 2 * rep * width :].astype(F32), 0.0)
        rate = jnp.sum(rate, axis=1, keepdims=True)
        rates.append(rate)
        counts.append(jnp.sum(jnp.where(rate > 0.0, 1.0, 0.0), axis=0, keepdims=True))
    slot = iota((SLOT, 1), 0).astype(F32)
    rate_rows, kept_rows = [], []
    for n in range(2 * count):
        start = jnp.zeros((1, 1), F32)
        for other in range(2 * count):
            start = start + jnp.where(sources[other] < sources[n], counts[other], 0.0)
        kept = jnp.where((rates[n] > 0.0) & (start + slot < capacity), 1.0, 0.0)
        kept_rows.append(kept)
        rate_rows.append(rates[n] * kept)
    rate = jnp.concatenate(rate_rows, axis=0)
    kept = jnp.concatenate(kept_rows, axis=0)

    pre_gate, pre_up, back_hidden = sum_x[:, :units], sum_x[:, units:], sum_d
    sig = 1.0 / (1.0 + jnp.exp(-pre_gate))
    activated = pre_gate * sig
    hidden = activated * pre_up
    score = jnp.sum(hidden * back_hidden, axis=1, keepdims=True) * kept
    lane = iota((2 * own_rows, LANES), 1)
    scores = jnp.where(lane == e % CORES, score, 0.0).astype(BF16)
    scaled = back_hidden * rate
    gate_grad = (scaled * pre_up * sig * (1.0 + pre_gate * (1.0 - sig))).astype(BF16)
    up_grad = (scaled * activated).astype(BF16)
    weighted = (hidden * rate).astype(BF16)
    grads_ref[...] = jnp.concatenate([gate_grad, up_grad, weighted], axis=1)
    for ref in away_refs:
        ref[:, width:] = grads_ref[...]
    pair = jnp.concatenate([gate_grad, up_grad], axis=1)
    for (k, start, stop), piece in zip(spans, pieces):
        back = dot(pair, piece[:, : 2 * units], ((1,), (1,))).astype(BF16)
        some = slice(k * width + start, k * width + stop)
        own_ref[:, some] = back[:own_rows]
        other_ref[:, some] = back[own_rows:]
    own_ref[:, rep * width :] = scores[:own_rows]
    other_ref[:, rep * width :] = scores[own_rows:]


def sum_kernel(own_ref, got_ref, *outs):
    for j, out in enumerate(outs):
        some = slice(j * SLOT, (j + 1) * SLOT)
        out[...] = (own_ref[some].astype(F32) + got_ref[some].astype(F32)).astype(BF16)


def stack_kernel(*refs):
    for k, ref in enumerate(refs[:-1]):
        refs[-1][k] = ref[:, : refs[-1].shape[2]]


def weight_kernel(rep, here_ref, grads_ref, near_ref, far_ref, *refs):
    away, outs, held, sems = refs[: rep - 1], refs[rep - 1 : -4], refs[-4:-1], refs[-1]
    units = outs[0].shape[1]
    width = here_ref.shape[2]
    half = grads_ref.shape[0] // 2
    copies = []
    for part, columns in enumerate((slice(0, 2 * units), slice(2 * units, 3 * units))):
        some = slice(part * half, (part + 1) * half)
        rows = [here_ref[part]]
        got = [grads_ref[:, columns]]
        others = [ref[k, some] for ref in (near_ref, far_ref) for k in range(ref.shape[0])]
        for other, ref in zip(others, away):
            rows += [ref[some, :width], other]
            got.append(ref[:, width + columns.start : width + columns.stop])
        rows = jnp.concatenate(rows, axis=0)
        got = jnp.concatenate(got, axis=0)
        total = dot(got, rows, ((0,), (0,)))
        for n in range(total.shape[0] // units):
            held[2 * part + n][...] = total[n * units : (n + 1) * units].T.astype(BF16)
            copies += fetch([(held[2 * part + n], outs[2 * part + n])], sems, 2 * part + n)
    for copy in copies:
        copy.wait()


def token_kernel(rep, flight, ids_ref, placed_ref, *refs):
    backs, rest = refs[: flight * CHIPS], refs[flight * CHIPS :]
    out_ref, weight_ref, blocks, ids, sems = rest
    (ids_copy,) = fetch([(ids_ref, ids)], sems)
    r = lax.axis_index("rep")
    mine = lax.axis_index("ep") // SPLIT
    spacing = EXPERTS // flight
    width = out_ref.shape[1] // rep
    joined = [
        jnp.concatenate([b[...] for b in backs[w * CHIPS : (w + 1) * CHIPS]], axis=0)
        for w in range(flight)
    ]
    for k in range(rep):
        total = 0.0
        for w in range(flight):
            some = joined[w][:, k * width : (k + 1) * width]
            total = total + dot(placed_ref[w], some, ((0,), (0,)))
        blocks[jnp.bitwise_xor(r, k)] = total.astype(BF16)
    for b in range(rep):
        out_ref[:, b * width : (b + 1) * width] = blocks[b]
    result = jnp.zeros(weight_ref.shape, F32)
    ids_copy.wait()
    for w in range(flight):
        score = dot(joined[w][:, rep * width :], placed_ref[w], ((0,), (0,)))
        score = jnp.sum(score, axis=0, keepdims=True)
        match = ids[...] == jnp.bitwise_xor(mine, w) * spacing
        result = result + jnp.where(match, score, 0.0)
    weight_ref[...] = result


def local(
    tokens, out_grad, expert_ids, route_weight, live_count, cap_blocks, w_gate, w_up, w_down_t
):
    rep = lax.axis_size("rep")
    ep = lax.axis_size("ep")
    far = rep // 2
    flight = ep // SPLIT
    count = ep // CORES
    tok_count, model_dim = tokens.shape
    width, units = w_gate.shape
    rows = count * SLOT
    ids_rows, rw_rows, caps = expert_ids.T, route_weight.T, cap_blocks.T

    def send(array, rep_bits, ep_bits):
        mask = rep_bits * ep + ep_bits
        pairs = [(a, a ^ mask) for a in range(rep * ep)]
        return lax.ppermute(array, ("rep", "ep"), pairs)

    def after(array, *others):
        return lax.optimization_barrier((array,) + others)[0]

    packed = call(
        functools.partial(pack_kernel, rep, flight),
        [shape((SLOT, 2 * model_dim + LANES))] * flight
        + [shape((flight, CHIPS * SLOT, tok_count)), shape((width, 3 * units))],
        [live_count, tokens, out_grad, ids_rows, rw_rows, w_gate, w_up, w_down_t],
        stored=range(8),
        kept=(flight + 1,),
        scratch=[
            pltpu.SMEM(live_count.shape, jnp.int32),
            pltpu.VMEM(ids_rows.shape, jnp.int32),
            pltpu.VMEM(rw_rows.shape, BF16),
            pltpu.VMEM((2, tok_count, model_dim), BF16),
            pltpu.VMEM((rep, SLOT, width), BF16),
            pltpu.VMEM((width, 3 * units), BF16),
            pltpu.SemaphoreType.DMA((2 * PARTS + 11,)),
        ],
        grant=54,
    )
    pays, placed, weights = packed[:flight], packed[flight], packed[flight + 1]

    half = width // 2
    whole = {0: weights}
    halves = {}
    for k in range(1, rep):
        low, high = k & -k, 1 << (k.bit_length() - 1)
        if low == high:
            whole[k] = send(weights, k, 0)
            for h in range(2):
                kernel = functools.partial(half_kernel, h * half)
                (halves[k, h],) = call(kernel, [shape((half, 3 * units))], [whole[k]])
        else:
            halves[k, 0] = send(halves[k ^ low, 0], low, 0)
            halves[k, 1] = send(halves[k ^ high, 1], high, 0)
    spans, pieces = [], []
    for k in range(rep):
        if k in whole:
            spans.append((k, 0, width))
            pieces.append(whole[k])
        else:
            spans += [(k, 0, half), (k, half, width)]
            pieces += [halves[k, 0], halves[k, 1]]

    order = [turned(n) for n in range(count)]
    blocks = [send(pays[j // CHIPS], 0, CORES * j) if j else pays[0] for j in order]
    nearest = blocks[order.index(1)]
    ready = [after(b, nearest) if j == 0 else b for j, b in zip(order, blocks)]
    blocks = blocks + [send(block, 0, 1) for block in ready]
    results = call(
        functools.partial(hidden_kernel, rep, count, tuple(spans)),
        [shape((rows, model_dim + LANES))] * 2
        + [shape((2 * rows, 3 * units)), shape((2, 2 * rows, width))]
        + [shape((2 * rows, width + 3 * units))] * (rep - 1),
        [caps] + blocks + pieces,
        stored=(0,),
        scratch=[pltpu.SMEM(caps.shape, jnp.int32), pltpu.SemaphoreType.DMA(())],
        flops=2 * 2 * rows * model_dim * 5 * units,
    )
    own, other, grads, here, away = *results[:4], results[4:]
    summed = call(sum_kernel, [shape((SLOT, model_dim + LANES))] * count, [own, send(other, 0, 1)])
    backs = [send(part, 0, CORES * j) if j else part for j, part in zip(order, summed)]

    near = [k for k in range(1, rep) if k & (k - 1) == 0]
    far = [k for k in range(1, rep) if k & (k - 1)]
    near_moved = [send(away[k - 1], k, 0) for k in near]
    (stacked,) = call(stack_kernel, [shape((len(near), 2 * rows, width))], near_moved)
    near_other = send(stacked, 0, 1)
    far_moved = [send(after(away[k - 1], summed[-2]), k, 0) for k in far]
    ready = [after(far_moved[0], stacked)] + far_moved[1:]
    (stacked,) = call(stack_kernel, [shape((len(far), 2 * rows, width))], ready)
    far_other = send(stacked, 0, 1)
    grad_gate, grad_up, grad_down = call(
        functools.partial(weight_kernel, rep),
        [shape((width, units))] * 3,
        [here, grads, near_other, far_other] + near_moved + far_moved,
        kept=(0, 1, 2),
        scratch=[pltpu.VMEM((width, units), BF16)] * 3 + [pltpu.SemaphoreType.DMA((3,))],
        flops=2 * 2 * rep * rows * width * 3 * units,
    )
    grad_tokens, grad_weight = call(
        functools.partial(token_kernel, rep, flight),
        [shape((tok_count, model_dim)), shape(ids_rows.shape, F32)],
        [ids_rows, placed] + backs,
        stored=(0,),
        scratch=[
            pltpu.VMEM((rep, tok_count, width), BF16),
            pltpu.VMEM(ids_rows.shape, jnp.int32),
            pltpu.SemaphoreType.DMA((1,)),
        ],
        flops=1000 * 2 * tok_count * CHIPS * SLOT * model_dim,
    )
    return grad_tokens, grad_weight.T, grad_gate, grad_up, grad_down


def solution(mesh):
    return jax.shard_map(
        local,
        mesh=mesh,
        in_specs=(
            P(("rep", "ep"), None),
            P(("rep", "ep"), None),
            P(("rep", "ep"), None),
            P(("rep", "ep"), None),
            P(),
            P(),
            P("rep", "ep"),
            P("rep", "ep"),
            P("rep", "ep"),
        ),
        out_specs=(
            P(("rep", "ep"), None),
            P(("rep", "ep"), None),
            P("rep", "ep"),
            P("rep", "ep"),
            P("rep", "ep"),
        ),
        check_vma=False,
    )
```
